32 devices in a mesh: dp: 8 (over z, y), tensor: 4 (over x, core).
Axes of the slice: x: 2, y: 2, z: 4, core: 2. Of those that a mesh axis runs over, the one named last changes fastest.
Arguments:
- hidden_in: bfloat16 [8192, 768], P(('dp', 'tensor')), may hold values from -6 to 6
- segment_ids: int32 [32, 256], P('dp'), may hold values from 0 to 7, never falling along the last dimension, each value on 1 to 96 neighbouring positions
- out_cotangent: bfloat16 [8192, 768], P(('dp', 'tensor')), may hold values from -18 to 18
- qkv_weight: bfloat16 [2, 768, 3, 768], P(None, None, None, 'tensor'), may hold values from -0.21875 to 0.21875
- qv_bias: bfloat16 [2, 2, 768], P(None, None, 'tensor'), may hold values from -1.796875 to 1.796875
- out_weight: bfloat16 [2, 768, 768], P(None, 'tensor'), may hold values from -0.875 to 0.875
- out_bias: bfloat16 [2, 768], replicated, may hold values from -1.796875 to 1.796875
- norm_gain: bfloat16 [2, 2, 768], replicated, may hold values from 0.5 to 1.5
- norm_bias: bfloat16 [2, 2, 768], replicated, may hold values from -1.796875 to 1.796875
- up_weight: bfloat16 [2, 768, 3072], P(None, None, 'tensor'), may hold values from -0.21875 to 0.21875
- up_bias: bfloat16 [2, 3072], P(None, 'tensor'), may hold values from -1.796875 to 1.796875
- down_weight: bfloat16 [2, 3072, 768], P(None, 'tensor'), may hold values from -0.109375 to 0.109375
- down_bias: bfloat16 [2, 768], replicated, may hold values from -1.796875 to 1.796875
Outputs:
- out_hidden: bfloat16 [8192, 768], P(('dp', 'tensor'))
- grad_hidden: float32 [8192, 768], P(('dp', 'tensor'))
- grad_qkv_weight: float32 [2, 768, 3, 768], P(None, None, None, 'tensor')
- grad_qv_bias: float32 [2, 2, 768], P(None, None, 'tensor')
- grad_out_weight: float32 [2, 768, 768], P(None, 'tensor')
- grad_out_bias: float32 [2, 768], replicated
- grad_norm_gain: float32 [2, 2, 768], replicated
- grad_norm_bias: float32 [2, 2, 768], replicated
- grad_up_weight: float32 [2, 768, 3072], P(None, None, 'tensor')
- grad_up_bias: float32 [2, 3072], P(None, 'tensor')
- grad_down_weight: float32 [2, 3072, 768], P(None, 'tensor')
- grad_down_bias: float32 [2, 768], replicated
The draws below stay inside these ranges and needn't reach their ends.
All inputs are finite; a program needn't handle non-finite values.
Results may differ from the reference program's by a relative error of at most 0.033.
Values may be sent and summed in bfloat16 or wider, within the bound.
A program may use at most 128 MiB of HBM per device.

```python
import math
import jax
import jax.numpy as jnp
import numpy as np
from jax import lax

D = 768
HEADS = 12
HEAD = 64
FF = 3072
LEN = 256
LAYERS = 2
SEQS = 32
TOKENS = 8192


def draw_out_cotangent(key, part):
    key = jax.random.fold_in(key, 7)
    position = jnp.arange(TOKENS, dtype=jnp.float32)[:, None] / max(TOKENS - 1, 1)
    rising = 1.0 + 2.0 * position
    base = jnp.clip(jax.random.normal(key, (TOKENS, D), jnp.float32), -6.0, 6.0)
    return (base * rising).astype(jnp.bfloat16)


def block_scale(rng, shape, cuts, low, top_value):
    factor_of, own = 1.0, jax.random.fold_in(rng, 6)
    for axis_at, blocks in cuts:
        steps = jnp.exp(jax.random.uniform(jax.random.fold_in(own, axis_at), (blocks,), jnp.float32, low / len(cuts), top_value / len(cuts)))
        factor_of = factor_of * jnp.repeat(steps, shape[axis_at] // blocks).reshape([-1 if axis == axis_at else 1 for axis in range(len(shape))])
    return factor_of


def length_profile(count, total, reach, lean):
    loads = [(1 << 20) // math.isqrt(grade ** lean) + 1 for grade in range(2, count + 1)]
    spare, counts = total - reach - (count - 1), [1] * (count - 1)
    while spare > 0:
        movable = [i for i in range(count - 1) if counts[i] < reach]
        mass, left = sum([loads[i] for i in movable]), spare
        for i in movable:
            more = min(reach - counts[i], max(1, left * loads[i] // mass), spare)
            counts[i] = counts[i] + more
            spare = spare - more
    return np.array([reach] + counts)


def uneven_parts(stream_key, amount, total, most, slope):
    if amount == 2:
        one = jax.random.randint(stream_key, (), max(1, total - most), min(most, total - 1) + 1)
        return jnp.stack([one, total - one])
    lengths = jnp.asarray(length_profile(amount, total, most, slope), jnp.int32)
    twos = (amount - 1) // 2
    source_of, sink = lengths[1:1 + 2 * twos:2], lengths[2:2 + 2 * twos:2]
    slack = jnp.minimum(source_of - 1, most - sink)
    moved = jax.random.randint(jax.random.fold_in(stream_key, 1), (twos,), 0, 1 << 20) % (slack + 1)
    lengths = lengths.at[1:1 + 2 * twos:2].set(source_of - moved).at[2:2 + 2 * twos:2].set(sink + moved)
    return lengths[jax.random.permutation(jax.random.fold_in(stream_key, 2), amount)]


def noise(key, shape, scale, most, cuts=(), held_as=jnp.bfloat16):
    result = scale * jax.random.normal(key, shape, jnp.float32)
    if cuts:
        result = result * block_scale(key, shape, cuts, -0.22, 0.18)
    return jnp.clip(result, -most, most).astype(held_as)


def setup_inputs(seed: int = 0) -> dict:
    keys = jax.random.split(jax.random.key(seed), 14)
    hidden_in = noise(keys[0], (TOKENS, D), 1.0, 6.0, ((0, 32),))
    segment_ids = jax.vmap(lambda own: jnp.searchsorted(jnp.cumsum(uneven_parts(own, 8, LEN, LEN * 3 // 8, 1)), jnp.arange(LEN), side="right"))(jax.random.split(keys[1], SEQS)).reshape((SEQS, LEN)).astype(jnp.int32)
    out_cotangent = draw_out_cotangent(jax.random.fold_in(keys[13], 71), 0)
    qkv_weight = noise(keys[3], (LAYERS, D, 3, D), D ** -0.5, 0.21875, ((3, 4),))
    qv_bias = noise(keys[4], (LAYERS, 2, D), 0.3, 1.796875, ((2, 4),))
    out_weight = noise(keys[5], (LAYERS, D, D), (D // 16) ** -0.5, 0.875, ((1, 4),))
    out_bias = noise(keys[6], (LAYERS, D), 0.3, 1.796875)
    norm_gain = jnp.clip(1.0 + 0.1 * jax.random.normal(keys[7], (LAYERS, 2, D), jnp.float32), 0.5, 1.5).astype(jnp.bfloat16)
    norm_bias = noise(keys[8], (LAYERS, 2, D), 0.3, 1.796875)
    up_weight = noise(keys[9], (LAYERS, D, FF), D ** -0.5, 0.21875, ((2, 4),))
    up_bias = noise(keys[10], (LAYERS, FF), 0.3, 1.796875, ((1, 4),))
    down_weight = noise(keys[11], (LAYERS, FF, D), FF ** -0.5, 0.109375, ((1, 4),))
    down_bias = noise(keys[12], (LAYERS, D), 0.3, 1.796875)
    return {"hidden_in": hidden_in, "segment_ids": segment_ids, "out_cotangent": out_cotangent, "qkv_weight": qkv_weight, "qv_bias": qv_bias, "out_weight": out_weight, "out_bias": out_bias, "norm_gain": norm_gain, "norm_bias": norm_bias, "up_weight": up_weight, "up_bias": up_bias, "down_weight": down_weight, "down_bias": down_bias}


@jax.custom_vjp
def low(v):
    return lax.optimization_barrier(v.astype(jnp.bfloat16)).astype(jnp.float32)

@jax.custom_vjp
def low_back(v):
    return v

def low_keep(v):
    return (low(v), None)

def low_pass(kept, grad):
    return (grad,)

def back_keep(v):
    return (v, None)

def back_low(kept, grad):
    return (low(grad),)
low.defvjp(low_keep, low_pass)
low_back.defvjp(back_keep, back_low)
norm_eps = 1e-05

def layer_norm(values_in, norm_gain, norm_bias):
    average = lax.optimization_barrier(jnp.mean(values_in, axis=-1, keepdims=True))
    centered = values_in - average
    variance = lax.optimization_barrier(jnp.mean(centered * centered, axis=-1, keepdims=True))
    return centered * lax.rsqrt(variance + norm_eps) * norm_gain + norm_bias

def encoder_layer(tokens_now, segment, weights):
    qkv_weight, qv_bias, out_weight, out_bias, norm_gain, norm_bias, up_weight, up_bias, down_weight, down_bias = weights
    groups, length = segment.shape
    highest = lax.Precision.HIGHEST
    inputs = low(tokens_now)
    projected = jnp.einsum('nd,dcf->ncf', inputs, qkv_weight, precision=highest)
    query_rows = low(low_back(projected[:, 0] + qv_bias[0]))
    key_rows = low(low_back(projected[:, 1]))
    value_rows = low(low_back(projected[:, 2] + qv_bias[1]))

    def head_split(flat):
        return flat.reshape(groups, length, HEADS, HEAD)
    allowed = (segment[:, :, None] == segment[:, None, :])[:, None]
    scores = jnp.einsum('sqhe,skhe->shqk', head_split(query_rows), head_split(key_rows), precision=highest) * HEAD ** (-0.5)
    scores = low_back(jnp.where(allowed, scores, -1000000000.0))
    weights_low = low(jax.nn.softmax(scores, axis=-1))
    context = jnp.einsum('shqk,skhe->sqhe', weights_low, head_split(value_rows), precision=highest)
    context = low(low_back(context.reshape(groups * length, D)))
    attended = low_back(jnp.dot(context, out_weight, precision=highest) + out_bias)
    normed = layer_norm(tokens_now + attended, norm_gain[0], norm_bias[0])
    normed_low = low(normed)
    pre_active = low_back(jnp.dot(normed_low, up_weight, precision=highest) + up_bias)
    active = low(jax.nn.gelu(pre_active, approximate=True))
    lowered = low_back(jnp.dot(active, down_weight, precision=highest) + down_bias)
    return layer_norm(normed + lowered, norm_gain[1], norm_bias[1])

def reference(hidden_in, segment_ids, out_cotangent, qkv_weight, qv_bias, out_weight, out_bias, norm_gain, norm_bias, up_weight, up_bias, down_weight, down_bias):
    params = tuple((member.astype(jnp.float32) for member in (qkv_weight, qv_bias, out_weight, out_bias, norm_gain, norm_bias, up_weight, up_bias, down_weight, down_bias)))
    group = math.gcd(SEQS, 16)
    turns = SEQS // group
    inputs_all = hidden_in.astype(jnp.float32).reshape(turns, group * LEN, D)
    cotangent_all = out_cotangent.astype(jnp.float32).reshape(turns, group * LEN, D)
    segments_all = segment_ids.reshape(turns, group, LEN)

    def one_turn(totals, pieces):
        inputs, cotangent, segment = pieces

        def forward(state, weights):
            for layer_index in range(LAYERS):
                state = encoder_layer(state, segment, tuple((member[layer_index] for member in weights)))
            return state
        output, pullback = jax.vjp(forward, inputs, params)
        grad_inputs, grad_params = pullback(cotangent)
        totals = jax.tree.map(jnp.add, totals, grad_params)
        return (totals, (output, grad_inputs))
    zeros = jax.tree.map(jnp.zeros_like, params)
    totals, (outputs, grad_inputs) = lax.scan(one_turn, zeros, (inputs_all, cotangent_all, segments_all))
    return (outputs.reshape(TOKENS, D).astype(jnp.bfloat16), grad_inputs.reshape(TOKENS, D), totals[0], totals[1], totals[2], totals[3], totals[4], totals[5], totals[6], totals[7], totals[8], totals[9])
```

```python
import jax
import jax.numpy as jnp
from jax import lax
from jax.experimental import pallas as pl
from jax.experimental.pallas import tpu as pltpu
from jax.sharding import PartitionSpec as P

HEAD = 64
MESH = pl.DeviceIdType.MESH
Y_SIZE = 2
Z_SIZE = 4
GROUP = Y_SIZE * Z_SIZE
F32 = jnp.float32
BF16 = jnp.bfloat16


class Place:
    def __init__(self):
        self.dp = lax.axis_index("dp")
        self.t = lax.axis_index("tensor")
        inner = lax.rem(self.dp, GROUP)
        base = self.dp - inner
        self.y = lax.rem(inner, Y_SIZE)
        self.z = inner // Y_SIZE
        z_pair = self.z + 1 - 2 * lax.rem(self.z, 2)
        z_mid = Z_SIZE - 1 - self.z
        self.is_end = jnp.logical_or(self.z == 0, self.z == Z_SIZE - 1)
        self.is_inner = jnp.logical_not(self.is_end)
        self.core = (self.dp, self.t + 1 - 2 * lax.rem(self.t, 2))
        self.over = (self.dp, lax.rem(self.t + 2, 4))
        self.y_pair = (base + self.z * Y_SIZE + 1 - self.y, self.t)
        self.z_pair = (base + z_pair * Y_SIZE + self.y, self.t)
        self.z_mid = (base + z_mid * Y_SIZE + self.y, self.t)


class Links:
    def __init__(self, sems):
        self.sems = sems
        self.used = 0

    def copy(self, src, dst, device):
        at = self.used
        self.used += 1
        return pltpu.make_async_remote_copy(
            src_ref=src,
            dst_ref=dst,
            send_sem=self.sems.at[0, at],
            recv_sem=self.sems.at[1, at],
            device_id=device,
            device_id_type=MESH,
        )


def greet(devices):
    barrier = pltpu.get_barrier_semaphore()
    for device in devices:
        pl.semaphore_signal(barrier, inc=1, device_id=device, device_id_type=MESH)
    pl.semaphore_wait(barrier, len(devices))


def added(one, two, dtype):
    return (one.astype(F32) + two.astype(F32)).astype(dtype)


def sum_item(place, links, mine, landing, result, start, size):
    from_y, from_z, from_mid = landing.at[0], landing.at[1], landing.at[2]
    half = mine.shape[0] // 2
    here = pl.ds(pl.multiple_of(place.y * half + start, 16), size)
    there = pl.ds(pl.multiple_of((1 - place.y) * half + start, 16), size)
    part = pl.ds(start, size)
    dtype = mine.dtype
    y_out = links.copy(mine.at[there], from_y.at[part], place.y_pair)
    pair_in = links.copy(mine.at[here], from_z.at[part], place.z_pair)
    mid = links.copy(mine.at[here], from_mid.at[part], place.z_mid)
    pair_out = links.copy(result.at[here], from_z.at[part], place.z_pair)
    y_back = links.copy(result.at[here], result.at[here], place.y_pair)
    y_out.start()
    yield
    y_out.wait_recv()
    mine[here] = added(mine[here], from_y[part], dtype)

    @pl.when(place.is_end)
    def _():
        pair_in.start()

    yield

    @pl.when(place.is_inner)
    def _():
        pair_in.wait_recv()
        mine[here] = added(mine[here], from_z[part], dtype)
        mid.start()

    yield

    @pl.when(place.is_inner)
    def _():
        mid.wait_recv()
        result[here] = added(mine[here], from_mid[part], dtype)
        pair_out.start()
        y_back.start()

    yield

    @pl.when(place.is_end)
    def _():
        pair_out.wait_recv()
        result[here] = from_z[part]
        y_back.start()

    yield
    yield
    y_back.wait_recv()
    y_out.wait_send()
    y_back.wait_send()

    @pl.when(place.is_end)
    def _():
        pair_in.wait_send()

    @pl.when(place.is_inner)
    def _():
        mid.wait_send()
        pair_out.wait_send()


def small_item(place, links, mine, steps, landing, result):
    top = pl.ds(0, 8)
    steps[0] = mine[...]
    near = links.copy(steps.at[0, top], landing.at[0, top], place.core)
    near.start()
    yield
    near.wait_recv()
    steps[1] = steps[0]
    steps[1, top] = steps[0, top] + landing[0, top]
    over = links.copy(steps.at[1, top], landing.at[1, top], place.over)
    over.start()
    yield
    over.wait_recv()
    steps[2] = steps[1]
    steps[2, top] = steps[1, top] + landing[1, top]
    across = links.copy(steps.at[2], landing.at[2], place.y_pair)
    across.start()
    yield
    across.wait_recv()
    steps[3] = steps[2] + landing[2]
    pair_in = links.copy(steps.at[3], landing.at[3], place.z_pair)
    mid = links.copy(steps.at[4], landing.at[4], place.z_mid)
    pair_out = links.copy(result, landing.at[3], place.z_pair)

    @pl.when(place.is_end)
    def _():
        pair_in.start()

    yield

    @pl.when(place.is_inner)
    def _():
        pair_in.wait_recv()
        steps[4] = steps[3] + landing[3]
        mid.start()

    yield

    @pl.when(place.is_inner)
    def _():
        mid.wait_recv()
        result[...] = steps[4] + landing[4]
        pair_out.start()

    yield

    @pl.when(place.is_end)
    def _():
        pair_out.wait_recv()
        result[...] = landing[3]

    yield
    near.wait_send()
    over.wait_send()
    across.wait_send()

    @pl.when(place.is_end)
    def _():
        pair_in.wait_send()

    @pl.when(place.is_inner)
    def _():
        mid.wait_send()
        pair_out.wait_send()


class Ticker:
    def __init__(self):
        self.waiting = []
        self.running = []

    def add(self, items):
        self.waiting.extend(items)

    def tick(self, enter=1):
        for _ in range(enter):
            if self.waiting:
                self.running.append(self.waiting.pop(0))
        left = []
        for item in self.running:
            try:
                next(item)
                left.append(item)
            except StopIteration:
                pass
        self.running = left

    def finish(self):
        while self.waiting or self.running:
            self.tick()


def chunked(place, links, mine, landing, result, size):
    half = mine.shape[0] // 2
    return [
        sum_item(place, links, mine, landing, result, start, size)
        for start in range(0, half, size)
    ]


def sum_kernel(small, down, up, qkv, out, small_sum, down_sum, up_sum, qkv_sum, out_sum,
               own_small, land_small, own_down, land_down, own_up, land_up, own_qkv, land_qkv, own_out, land_out, sems):
    place = Place()
    links = Links(sems)
    greet((place.core, place.over, place.y_pair, place.z_pair, place.z_mid))
    ticker = Ticker()
    ticker.add([small_item(place, links, small, own_small, land_small, small_sum)])
    for source, own, landing, result, size in (
        (down, own_down, land_down, down_sum, 96),
        (up, own_up, land_up, up_sum, 96),
        (qkv, own_qkv, land_qkv, qkv_sum, 96),
        (out, own_out, land_out, out_sum, 96),
    ):
        own[...] = source[...]
        ticker.add(chunked(place, links, own, landing, result, size))
    ticker.tick(6)
    ticker.finish()


def sum_over_group(small, down, up, qkv, out, which):
    arrays = (small, down, up, qkv, out)
    scratch = [pltpu.VMEM((5,) + small.shape, F32), pltpu.VMEM((5,) + small.shape, F32)]
    for array in arrays[1:]:
        half = (array.shape[0] // 2, array.shape[1])
        scratch += [pltpu.VMEM(array.shape, BF16), pltpu.VMEM((3,) + half, BF16)]
    scratch.append(pltpu.SemaphoreType.DMA((2, 128)))
    vmem = pl.BlockSpec(memory_space=pltpu.VMEM)
    return pl.pallas_call(
        sum_kernel,
        out_shape=[jax.ShapeDtypeStruct(array.shape, array.dtype) for array in arrays],
        in_specs=[vmem] * 5,
        out_specs=[vmem] * 5,
        scratch_shapes=scratch,
        compiler_params=pltpu.CompilerParams(
            collective_id=which, has_side_effects=True, vmem_limit_bytes=56 << 20
        ),
    )(*arrays)


def over_outer_groups(values):
    size = lax.axis_size("dp")
    if size == GROUP:
        return values
    groups = [[first + GROUP * turn for turn in range(size // GROUP)] for first in range(GROUP)]
    return [lax.psum(value, "dp", axis_index_groups=groups) for value in values]


norm_eps = 1e-05


def gelu_tanh(pre_active):
    return jax.nn.gelu(pre_active, approximate=True)


def norm_forward(total, norm_gain, norm_shift):
    average = jnp.mean(total, axis=-1, keepdims=True)
    centered = total - average
    variance = jnp.mean(centered * centered, axis=-1, keepdims=True)
    inverse = lax.rsqrt(variance + norm_eps)
    scaled = centered * inverse
    return (scaled * norm_gain + norm_shift, scaled, inverse)


def norm_backward(incoming, scaled, inverse, norm_gain):
    gain_grad = jnp.sum(incoming * scaled, axis=0)
    shift_grad = jnp.sum(incoming, axis=0)
    inner = incoming * norm_gain
    result = inverse * (
        inner
        - jnp.mean(inner, axis=-1, keepdims=True)
        - scaled * jnp.mean(inner * scaled, axis=-1, keepdims=True)
    )
    return (result, gain_grad, shift_grad)


def sum_forward(full, weight):
    my_rows = full.shape[0] // lax.axis_size("tensor")

    def partial_value(offset, extent):
        return jnp.dot(full, weight, preferred_element_type=jnp.float32)

    return lax.psum_scatter(
        partial_value(jnp.int32(0), my_rows * lax.axis_size("tensor")).astype(jnp.bfloat16),
        "tensor",
        scatter_dimension=0,
        tiled=True,
    ).astype(jnp.float32)


def sum_backward(full, weight):
    my_rows = full.shape[0] // lax.axis_size("tensor")

    def partial_value(offset, extent):
        return jnp.einsum("nf,df->nd", full, weight, preferred_element_type=jnp.float32)

    return lax.psum_scatter(
        partial_value(jnp.int32(0), my_rows * lax.axis_size("tensor")).astype(jnp.bfloat16),
        "tensor",
        scatter_dimension=0,
        tiled=True,
    ).astype(jnp.float32)


def project_rows(context, out_weight):
    row_context = lax.all_to_all(context, "tensor", split_axis=0, concat_axis=1, tiled=True)
    return jnp.dot(
        row_context,
        lax.all_gather(out_weight, "tensor", axis=0, tiled=True),
        preferred_element_type=jnp.float32,
    )


def spread_rows(shard):
    return lax.all_gather(shard, "tensor", axis=0, tiled=True)


def spread_grads(shard):
    return lax.all_gather(shard, "tensor", axis=0, tiled=True)


def head_split(flat, sequences):
    return flat.reshape(sequences, -1, flat.shape[-1] // HEAD, HEAD)


def scores_of(query_heads, key_heads, allowed):
    raw_scores = jnp.einsum(
        "sqhe,skhe->shqk", query_heads, key_heads, preferred_element_type=jnp.float32
    ) * HEAD ** (-0.5)
    return jnp.where(allowed, raw_scores, -1000000000.0)


def layer_forward(tokens_now, sequences, allowed, weights):
    (
        qkv_weight,
        qv_bias,
        out_weight,
        out_bias,
        norm_gain,
        norm_shift,
        up_weight,
        up_bias,
        down_weight,
        down_bias,
    ) = weights
    local_width = qkv_weight.shape[-1]
    shard_in = tokens_now.astype(jnp.bfloat16)
    full_in = spread_rows(shard_in)
    projected = jnp.dot(
        full_in,
        qkv_weight.reshape(qkv_weight.shape[0], 3 * local_width),
        preferred_element_type=jnp.float32,
    )
    projected = projected.reshape(-1, 3, local_width)
    query_rows = (projected[:, 0] + qv_bias[0]).astype(jnp.bfloat16)
    key_rows = projected[:, 1].astype(jnp.bfloat16)
    value_rows = (projected[:, 2] + qv_bias[1]).astype(jnp.bfloat16)
    scores = scores_of(head_split(query_rows, sequences), head_split(key_rows, sequences), allowed)
    highest = jnp.max(scores, axis=-1, keepdims=True)
    log_total = highest + jnp.log(jnp.sum(jnp.exp(scores - highest), axis=-1, keepdims=True))
    probs_low = jnp.exp(scores - log_total).astype(jnp.bfloat16)
    context = jnp.einsum(
        "shqk,skhe->sqhe",
        probs_low,
        head_split(value_rows, sequences),
        preferred_element_type=jnp.float32,
    )
    context = context.reshape(-1, local_width).astype(jnp.bfloat16)
    attended = project_rows(context, out_weight) + out_bias
    normed, scaled_one, inverse_one = norm_forward(
        tokens_now + attended, norm_gain[0], norm_shift[0]
    )
    shard_mid = normed.astype(jnp.bfloat16)
    full_mid = spread_rows(shard_mid)
    pre_active = jnp.dot(full_mid, up_weight, preferred_element_type=jnp.float32) + up_bias
    active = gelu_tanh(pre_active).astype(jnp.bfloat16)
    lowered = sum_forward(active, down_weight) + down_bias
    result, scaled_two, inverse_two = norm_forward(normed + lowered, norm_gain[1], norm_shift[1])
    stored = (
        full_in,
        query_rows,
        key_rows,
        value_rows,
        log_total,
        context,
        scaled_one,
        inverse_one,
        full_mid,
        pre_active,
        active,
        scaled_two,
        inverse_two,
    )
    return (result, stored)


def layer_backward(incoming, sequences, allowed, weights, stored):
    (
        qkv_weight,
        qv_bias,
        out_weight,
        out_bias,
        norm_gain,
        norm_shift,
        up_weight,
        up_bias,
        down_weight,
        down_bias,
    ) = weights
    (
        stored_in,
        query_rows,
        key_rows,
        value_rows,
        log_total,
        context,
        scaled_one,
        inverse_one,
        stored_mid,
        pre_active,
        active,
        scaled_two,
        inverse_two,
    ) = stored
    local_width = qkv_weight.shape[-1]
    dsum_two, gain_two, shift_two = norm_backward(incoming, scaled_two, inverse_two, norm_gain[1])
    full_lowered = spread_grads(dsum_two.astype(jnp.bfloat16))
    grad_down_weight = jnp.einsum(
        "nf,nd->fd", active, full_lowered, preferred_element_type=jnp.float32
    )
    grad_down_bias = jnp.sum(full_lowered, axis=0, dtype=jnp.float32)
    grad_active = jnp.einsum(
        "nd,fd->nf", full_lowered, down_weight, preferred_element_type=jnp.float32
    )
    gelu_pull = jax.vjp(gelu_tanh, pre_active)[1]
    grad_pre = gelu_pull(grad_active)[0].astype(jnp.bfloat16)
    grad_up_weight = jnp.einsum(
        "nd,nf->df", stored_mid, grad_pre, preferred_element_type=jnp.float32
    )
    grad_up_bias = jnp.sum(grad_pre, axis=0, dtype=jnp.float32)
    grad_normed = dsum_two + sum_backward(grad_pre, up_weight)
    dsum_one, gain_one, shift_one = norm_backward(
        grad_normed, scaled_one, inverse_one, norm_gain[0]
    )
    full_attended = spread_grads(dsum_one.astype(jnp.bfloat16))
    grad_out_weight = jnp.einsum(
        "nf,nd->fd", context, full_attended, preferred_element_type=jnp.float32
    )
    grad_out_bias = jnp.sum(full_attended, axis=0, dtype=jnp.float32)
    grad_context = jnp.einsum(
        "nd,fd->nf", full_attended, out_weight, preferred_element_type=jnp.float32
    ).astype(jnp.bfloat16)
    grad_heads = head_split(grad_context, sequences)
    query_heads = head_split(query_rows, sequences)
    key_heads = head_split(key_rows, sequences)
    value_heads = head_split(value_rows, sequences)
    probs = jnp.exp(scores_of(query_heads, key_heads, allowed) - log_total)
    probs_low = probs.astype(jnp.bfloat16)
    grad_probs = jnp.einsum(
        "sqhe,skhe->shqk", grad_heads, value_heads, preferred_element_type=jnp.float32
    )
    grad_values = jnp.einsum(
        "shqk,sqhe->skhe", probs_low, grad_heads, preferred_element_type=jnp.float32
    )
    grad_scores = probs * (grad_probs - jnp.sum(grad_probs * probs, axis=-1, keepdims=True))
    grad_scores = grad_scores.astype(jnp.bfloat16)
    scale = HEAD ** (-0.5)
    grad_query = (
        jnp.einsum("shqk,skhe->sqhe", grad_scores, key_heads, preferred_element_type=jnp.float32)
        * scale
    )
    grad_keys = (
        jnp.einsum("shqk,sqhe->skhe", grad_scores, query_heads, preferred_element_type=jnp.float32)
        * scale
    )
    stacked = jnp.stack(
        [
            grad_query.reshape(-1, local_width),
            grad_keys.reshape(-1, local_width),
            grad_values.reshape(-1, local_width),
        ],
        axis=1,
    ).astype(jnp.bfloat16)
    grad_qkv_weight = jnp.einsum(
        "nd,ncf->dcf", stored_in, stacked, preferred_element_type=jnp.float32
    )
    grad_qv_bias = jnp.stack(
        [
            jnp.sum(stacked[:, 0], axis=0, dtype=jnp.float32),
            jnp.sum(stacked[:, 2], axis=0, dtype=jnp.float32),
        ]
    )
    grad_tokens = dsum_one + sum_backward(
        stacked.reshape(-1, 3 * local_width),
        qkv_weight.reshape(qkv_weight.shape[0], 3 * local_width),
    )
    grads = (
        grad_qkv_weight,
        grad_qv_bias,
        grad_out_weight,
        grad_out_bias,
        jnp.stack([gain_one, gain_two]),
        jnp.stack([shift_one, shift_two]),
        grad_up_weight,
        grad_up_bias,
        grad_down_weight,
        grad_down_bias,
    )
    return (grad_tokens, grads)


def final_sums(per_layer):
    summed = []
    for layer_index, grads in enumerate(per_layer):
        width = grads[8].shape[-1]
        local = grads[1].shape[-1]
        quarter = 1.0 / lax.axis_size("tensor")
        small = jnp.concatenate(
            [
                grads[4],
                grads[5],
                grads[3][None] * quarter,
                grads[9][None] * quarter,
                jnp.zeros((2, width), F32),
                grads[7][None],
                jnp.pad(grads[1], ((0, 0), (0, width - local))),
                jnp.zeros((5, width), F32),
            ]
        )
        big = [
            member.reshape(member.shape[0], -1).astype(BF16)
            for member in (grads[8], grads[6], grads[0], grads[2])
        ]
        done = sum_over_group(small, *big, which=layer_index)
        done = over_outer_groups(list(done))
        small, down, up, qkv, out = done
        summed.append(
            (
                qkv.reshape(qkv.shape[0], 3, -1).astype(F32),
                small[9:11, :local],
                out.astype(F32),
                small[4],
                small[0:2],
                small[2:4],
                up.astype(F32),
                small[8],
                down.astype(F32),
                small[5],
            )
        )
    return tuple(
        jnp.stack([summed[layer_index][member] for layer_index in range(len(summed))])
        for member in range(10)
    )


def on_device(
    hidden_in,
    segment_ids,
    out_cotangent,
    qkv_weight,
    qv_bias,
    out_weight,
    out_bias,
    norm_gain,
    norm_bias,
    up_weight,
    up_bias,
    down_weight,
    down_bias,
):
    params = (
        qkv_weight,
        qv_bias,
        out_weight,
        out_bias,
        norm_gain,
        norm_bias,
        up_weight,
        up_bias,
        down_weight,
        down_bias,
    )
    layer_count = qkv_weight.shape[0]
    sequences = segment_ids.shape[0]
    allowed = (segment_ids[:, :, None] == segment_ids[:, None, :])[:, None]
    tokens_now = hidden_in.astype(jnp.float32)
    stored_all = []
    for layer_index in range(layer_count):
        weights = tuple((member[layer_index] for member in params))
        tokens_now, stored = layer_forward(tokens_now, sequences, allowed, weights)
        stored_all.append(stored)
    out_hidden = tokens_now.astype(jnp.bfloat16)
    gradient = out_cotangent.astype(jnp.float32)
    per_layer = [None] * layer_count
    for layer_index in reversed(range(layer_count)):
        weights = tuple((member[layer_index] for member in params))
        gradient, grads = layer_backward(
            gradient, sequences, allowed, weights, stored_all[layer_index]
        )
        per_layer[layer_index] = grads
    gathered = final_sums(per_layer)
    return (out_hidden, gradient) + tuple(gathered)


def solution(mesh):
    placed = (
        P(("dp", "tensor"), None),
        P("dp", None),
        P(("dp", "tensor"), None),
        P(None, None, None, "tensor"),
        P(None, None, "tensor"),
        P(None, "tensor", None),
        P(),
        P(),
        P(),
        P(None, None, "tensor"),
        P(None, "tensor"),
        P(None, "tensor", None),
        P(),
    )
    return jax.shard_map(
        on_device,
        mesh=mesh,
        in_specs=placed,
        out_specs=(
            P(("dp", "tensor"), None),
            P(("dp", "tensor"), None),
            P(None, None, None, "tensor"),
            P(None, None, "tensor"),
            P(None, "tensor", None),
            P(),
            P(),
            P(),
            P(None, None, "tensor"),
            P(None, "tensor"),
            P(None, "tensor", None),
            P(),
        ),
        check_vma=False,
    )
```

```python
import jax
import jax.numpy as jnp
from jax import lax
from jax.experimental import pallas as pl
from jax.experimental.pallas import tpu as pltpu
from jax.sharding import PartitionSpec as P

HEAD = 64
norm_eps = 1e-05


def gelu_tanh(pre_active):
    return jax.nn.gelu(pre_active, approximate=True)


MESH = pl.DeviceIdType.MESH
Y_SIZE = 2
Z_SIZE = 4
GROUP = Y_SIZE * Z_SIZE
F32 = jnp.float32
BF16 = jnp.bfloat16


class Place:
    def __init__(self):
        self.dp = lax.axis_index("dp")
        self.t = lax.axis_index("tensor")
        inner = lax.rem(self.dp, GROUP)
        base = self.dp - inner
        self.y = lax.rem(inner, Y_SIZE)
        self.z = inner // Y_SIZE
        z_pair = self.z + 1 - 2 * lax.rem(self.z, 2)
        z_mid = Z_SIZE - 1 - self.z
        self.is_end = jnp.logical_or(self.z == 0, self.z == Z_SIZE - 1)
        self.is_inner = jnp.logical_not(self.is_end)
        self.core = (self.dp, self.t + 1 - 2 * lax.rem(self.t, 2))
        self.over = (self.dp, lax.rem(self.t + 2, 4))
        self.diagonal = (self.dp, 3 - self.t)
        self.y_pair = (base + self.z * Y_SIZE + 1 - self.y, self.t)
        self.z_pair = (base + z_pair * Y_SIZE + self.y, self.t)
        self.z_mid = (base + z_mid * Y_SIZE + self.y, self.t)


class Links:
    def __init__(self, sems):
        self.sems = sems
        self.used = 0

    def copy(self, src, dst, device):
        at = self.used
        self.used += 1
        return pltpu.make_async_remote_copy(
            src_ref=src,
            dst_ref=dst,
            send_sem=self.sems.at[0, at],
            recv_sem=self.sems.at[1, at],
            device_id=device,
            device_id_type=MESH,
        )


def greet(devices):
    barrier = pltpu.get_barrier_semaphore()
    for device in devices:
        pl.semaphore_signal(barrier, inc=1, device_id=device, device_id_type=MESH)
    pl.semaphore_wait(barrier, len(devices))


def added(one, two, dtype):
    return (one.astype(F32) + two.astype(F32)).astype(dtype)


def sum_item(place, links, mine, landing, result, start, size):
    from_y, from_z, from_mid = landing.at[0], landing.at[1], landing.at[2]
    half = mine.shape[0] // 2
    here = pl.ds(pl.multiple_of(place.y * half + start, 16), size)
    there = pl.ds(pl.multiple_of((1 - place.y) * half + start, 16), size)
    part = pl.ds(start, size)
    dtype = mine.dtype
    y_out = links.copy(mine.at[there], from_y.at[part], place.y_pair)
    pair_in = links.copy(mine.at[here], from_z.at[part], place.z_pair)
    mid = links.copy(mine.at[here], from_mid.at[part], place.z_mid)
    pair_out = links.copy(result.at[here], from_z.at[part], place.z_pair)
    y_back = links.copy(result.at[here], result.at[here], place.y_pair)
    y_out.start()
    yield
    y_out.wait_recv()
    mine[here] = added(mine[here], from_y[part], dtype)

    @pl.when(place.is_end)
    def _():
        pair_in.start()

    yield

    @pl.when(place.is_inner)
    def _():
        pair_in.wait_recv()
        mine[here] = added(mine[here], from_z[part], dtype)
        mid.start()

    yield

    @pl.when(place.is_inner)
    def _():
        mid.wait_recv()
        result[here] = added(mine[here], from_mid[part], dtype)
        pair_out.start()
        y_back.start()

    yield

    @pl.when(place.is_end)
    def _():
        pair_out.wait_recv()
        result[here] = from_z[part]
        y_back.start()

    yield
    yield
    y_back.wait_recv()
    y_out.wait_send()
    y_back.wait_send()

    @pl.when(place.is_end)
    def _():
        pair_in.wait_send()

    @pl.when(place.is_inner)
    def _():
        mid.wait_send()
        pair_out.wait_send()


def small_item(place, links, mine, steps, landing, result):
    top = pl.ds(0, 8)
    steps[0] = mine[...]
    near = links.copy(steps.at[0, top], landing.at[0, top], place.core)
    near.start()
    yield
    near.wait_recv()
    steps[1] = steps[0]
    steps[1, top] = steps[0, top] + landing[0, top]
    over = links.copy(steps.at[1, top], landing.at[1, top], place.over)
    over.start()
    yield
    over.wait_recv()
    steps[2] = steps[1]
    steps[2, top] = steps[1, top] + landing[1, top]
    across = links.copy(steps.at[2], landing.at[2], place.y_pair)
    across.start()
    yield
    across.wait_recv()
    steps[3] = steps[2] + landing[2]
    pair_in = links.copy(steps.at[3], landing.at[3], place.z_pair)
    mid = links.copy(steps.at[4], landing.at[4], place.z_mid)
    pair_out = links.copy(result, landing.at[3], place.z_pair)

    @pl.when(place.is_end)
    def _():
        pair_in.start()

    yield

    @pl.when(place.is_inner)
    def _():
        pair_in.wait_recv()
        steps[4] = steps[3] + landing[3]
        mid.start()

    yield

    @pl.when(place.is_inner)
    def _():
        mid.wait_recv()
        result[...] = steps[4] + landing[4]
        pair_out.start()

    yield

    @pl.when(place.is_end)
    def _():
        pair_out.wait_recv()
        result[...] = landing[3]

    yield
    near.wait_send()
    over.wait_send()
    across.wait_send()

    @pl.when(place.is_end)
    def _():
        pair_in.wait_send()

    @pl.when(place.is_inner)
    def _():
        mid.wait_send()
        pair_out.wait_send()


class Ticker:
    def __init__(self):
        self.waiting = []
        self.running = []

    def add(self, items):
        self.waiting.extend(items)

    def tick(self, enter=1):
        for _ in range(enter):
            if self.waiting:
                self.running.append(self.waiting.pop(0))
        left = []
        for item in self.running:
            try:
                next(item)
                left.append(item)
            except StopIteration:
                pass
        self.running = left

    def finish(self):
        while self.waiting or self.running:
            self.tick()


def chunked(place, links, mine, landing, result, size):
    half = mine.shape[0] // 2
    return [
        sum_item(place, links, mine, landing, result, start, size)
        for start in range(0, half, size)
    ]


def sum_kernel(small, down, up, qkv, out, small_sum, down_sum, up_sum, qkv_sum, out_sum,
               own_small, land_small, own_down, land_down, own_up, land_up, own_qkv, land_qkv, own_out, land_out, sems):
    place = Place()
    links = Links(sems)
    greet((place.core, place.over, place.y_pair, place.z_pair, place.z_mid))
    ticker = Ticker()
    ticker.add([small_item(place, links, small, own_small, land_small, small_sum)])
    for source, own, landing, result, size in (
        (down, own_down, land_down, down_sum, 96),
        (up, own_up, land_up, up_sum, 96),
        (qkv, own_qkv, land_qkv, qkv_sum, 96),
        (out, own_out, land_out, out_sum, 96),
    ):
        own[...] = source[...]
        ticker.add(chunked(place, links, own, landing, result, size))
    ticker.tick(6)
    ticker.finish()


def sum_over_group(small, down, up, qkv, out, which):
    arrays = (small, down, up, qkv, out)
    scratch = [pltpu.VMEM((5,) + small.shape, F32), pltpu.VMEM((5,) + small.shape, F32)]
    for array in arrays[1:]:
        half = (array.shape[0] // 2, array.shape[1])
        scratch += [pltpu.VMEM(array.shape, BF16), pltpu.VMEM((3,) + half, BF16)]
    scratch.append(pltpu.SemaphoreType.DMA((2, 128)))
    vmem = pl.BlockSpec(memory_space=pltpu.VMEM)
    return pl.pallas_call(
        sum_kernel,
        out_shape=[jax.ShapeDtypeStruct(array.shape, array.dtype) for array in arrays],
        in_specs=[vmem] * 5,
        out_specs=[vmem] * 5,
        scratch_shapes=scratch,
        compiler_params=pltpu.CompilerParams(
            collective_id=which, has_side_effects=True, vmem_limit_bytes=56 << 20
        ),
    )(*arrays)


def over_outer_groups(values):
    size = lax.axis_size("dp")
    if size == GROUP:
        return values
    groups = [[first + GROUP * turn for turn in range(size // GROUP)] for first in range(GROUP)]
    return [lax.psum(value, "dp", axis_index_groups=groups) for value in values]


CORNER = 128
LANES = 128
SLOT = 256


def product(left, right, contract):
    return lax.dot_general(left, right, ((contract[:1], contract[1:]), ((), ())), preferred_element_type=F32)


def nn(left, right):
    return product(left, right, (1, 0))


def nt(left, right):
    return product(left, right, (1, 1))


def tn(left, right):
    return product(left, right, (0, 0))


class Gather:
    def __init__(self, place, links, rows):
        half = SLOT // 2
        self.near_copies, self.far_copies, self.pass_copies = [], [], []
        for part in range(2):
            own = pl.ds(part * half, half)
            beside = pl.ds(SLOT + part * half, half)
            over = pl.ds(2 * SLOT + part * half, half)
            diagonal = pl.ds(3 * SLOT + part * half, half)
            self.near_copies.append(links.copy(rows.at[own], rows.at[beside], place.core))
            self.far_copies.append(links.copy(rows.at[own], rows.at[over], place.over))
            self.pass_copies.append(links.copy(rows.at[over], rows.at[diagonal], place.core))

    def send(self, part):
        self.far_copies[part].start()
        self.near_copies[part].start()

    def near(self):
        for copy in self.near_copies:
            copy.wait_recv()

    def far(self, part):
        self.far_copies[part].wait_recv()
        self.pass_copies[part].start()

    def diagonal(self, part):
        self.pass_copies[part].wait_recv()

    def drain(self):
        for copy in self.near_copies + self.far_copies + self.pass_copies:
            copy.wait_send()


class Scatter:
    def __init__(self, place, links, rooms):
        self.core_out, self.core_in, self.far_out, self.far_in, self.near_out, self.near_in = rooms
        self.core_copies = [
            links.copy(self.core_out.at[part], self.core_in.at[part], place.core) for part in range(2)
        ]
        self.far_copies = [
            links.copy(self.far_out.at[part], self.far_in.at[part], place.over) for part in range(2)
        ]
        self.near_copies = [
            links.copy(self.near_out.at[part], self.near_in.at[part], place.core) for part in range(2)
        ]

    def beside(self, term):
        half = SLOT // 2
        for part in range(2):
            self.near_out[part] = term[part * half : (part + 1) * half].astype(BF16)
            self.near_copies[part].start()

    def diagonal(self, part, term):
        self.core_out[part] = term.astype(BF16)
        self.core_copies[part].start()

    def over(self, part, term):
        self.core_copies[part].wait_recv()
        self.far_out[part] = (term + self.core_in[part].astype(F32)).astype(BF16)
        self.far_copies[part].start()

    def arrived(self, part):
        self.near_copies[part].wait_recv()
        self.far_copies[part].wait_recv()
        return self.near_in[part].astype(F32) + self.far_in[part].astype(F32)

    def drain(self):
        for copy in self.core_copies + self.far_copies + self.near_copies:
            copy.wait_send()


def lane_masks():
    lane = lax.broadcasted_iota(jnp.int32, (1, LANES), 1)
    first = jnp.where(lane < HEAD, 1.0, 0.0).astype(BF16)
    return first, (1.0 - first.astype(F32)).astype(BF16)


def head_parts(tile, masks):
    parts = []
    width = tile.shape[-1]
    for first in range(0, width, LANES):
        piece = tile[:, first : min(first + LANES, width)]
        if piece.shape[-1] == HEAD:
            parts.append([piece])
        else:
            parts.append([piece * masks[0], piece * masks[1]])
    return parts


def whole_parts(tile):
    width = tile.shape[-1]
    return [tile[:, first : min(first + LANES, width)] for first in range(0, width, LANES)]


def allowed_rows(seg_cols, seg_rows, slot):
    return seg_cols[:, slot : slot + 1] == seg_rows[slot : slot + 1, :]


def attention_forward(query, keys, values, allowed):
    masks = lane_masks()
    outs = []
    for query_part, key_heads, value_heads in zip(
        whole_parts(query), head_parts(keys, masks), head_parts(values, masks)
    ):
        total = None
        for key_head, value_head in zip(key_heads, value_heads):
            scores = jnp.where(allowed, nt(query_part, key_head), -1000000000.0)
            grown = jnp.exp(scores - jnp.max(scores, axis=-1, keepdims=True))
            probs = grown * (1.0 / jnp.sum(grown, axis=-1, keepdims=True))
            term = nn(probs.astype(BF16), value_head)
            total = term if total is None else total + term
        outs.append(total.astype(BF16))
    return outs


def norm_rows(total, gain, shift):
    average = jnp.mean(total, axis=-1, keepdims=True)
    centered = total - average
    inverse = lax.rsqrt(jnp.mean(centered * centered, axis=-1, keepdims=True) + norm_eps)
    scaled = centered * inverse
    return scaled * gain + shift, scaled, inverse


OUT_BIAS, DOWN_BIAS, UP_BIAS, Q_BIAS, V_BIAS, GAIN, SHIFT = 0, 1, 2, 3, 4, 5, 7


def forward_kernel(
    hidden, seg_rows, seg_cols, small, qkv_all, out_all, up_all, down_all,
    result, full_in, query, keys, values, context, full_mid, pre, active, scaled, inverse,
    qkv_weight, out_weight, up_weight, down_weight, context_in, own_part, far_part, state,
    core_out, core_in, far_out, far_in, near_out, near_in, load_sems, sems,
):
    place = Place()
    links = Links(sems)
    layers = qkv_weight.shape[0]
    local = query.shape[-1]
    half = SLOT // 2
    halves = [pl.ds(part * half, half) for part in range(2)]
    slots = [pl.ds(slot * SLOT, SLOT) for slot in range(4)]
    loads = []
    for layer in range(layers):
        row = []
        for at, (source, target) in enumerate(
            (
                (qkv_all.at[layer], qkv_weight.at[layer]),
                (out_all.at[layer], out_weight.at[layer, 0]),
                (up_all.at[layer], up_weight.at[layer]),
                (down_all.at[layer], down_weight.at[layer]),
            )
        ):
            copy = pltpu.make_async_copy(source, target, load_sems.at[layer, at])
            copy.start()
            row.append(copy)
        loads.append(row)
    greet((place.core, place.over, place.diagonal))
    rooms = (core_out, core_in, far_out, far_in, near_out, near_in)

    state[...] = hidden[...].astype(F32)
    gather = Gather(place, links, full_in.at[0])
    for part in range(2):
        full_in[0, halves[part]] = hidden[halves[part]]
        gather.send(part)
    drains = []
    for layer in range(layers):
        vector = lambda row, width=small.shape[-1]: small[layer, row : row + 1, :width]

        def attend(slot):
            rows = slots[slot]
            mixed = nn(full_in[layer, rows], qkv_weight[layer])
            query[layer, rows] = (
                (mixed[:, :local] + vector(Q_BIAS, local)) * HEAD ** (-0.5)
            ).astype(BF16)
            keys[layer, rows] = mixed[:, SLOT : SLOT + local].astype(BF16)
            values[layer, rows] = (mixed[:, 2 * SLOT : 2 * SLOT + local] + vector(V_BIAS, local)).astype(BF16)
            outs = attention_forward(
                query[layer, rows], keys[layer, rows], values[layer, rows],
                allowed_rows(seg_cols, seg_rows, slot),
            )
            first = 0
            for out in outs:
                context[layer, rows, first : first + out.shape[-1]] = out
                first += out.shape[-1]

        sends = [
            links.copy(context.at[layer, slots[slot]], context_in.at[slot], device)
            for slot, device in ((1, place.core), (2, place.over), (3, place.diagonal))
        ]
        out_near = links.copy(out_weight.at[layer, 0], out_weight.at[layer, 1], place.core)
        out_far = links.copy(out_weight.at[layer, 0], out_weight.at[layer, 2], place.over)
        out_pass = links.copy(out_weight.at[layer, 2], out_weight.at[layer, 3], place.core)
        loads[layer][1].wait()
        out_near.start()
        loads[layer][0].wait()
        attend(0)
        gather.near()
        attend(1)
        sends[0].start()
        gather.far(0)
        gather.far(1)
        out_far.start()
        gather.diagonal(0)
        gather.diagonal(1)
        attend(2)
        sends[1].start()
        out_far.wait_recv()
        out_pass.start()
        attend(3)
        sends[2].start()
        own_part[...] = nn(context[layer, slots[0]], out_weight[layer, 0])
        out_near.wait_recv()
        sends[0].wait_recv()
        own_part[...] += nn(context_in[1], out_weight[layer, 1])
        out_pass.wait_recv()
        sends[1].wait_recv()
        sends[2].wait_recv()
        gather.drain()
        gather = Gather(place, links, full_mid.at[layer])
        for part in range(2):
            rows = halves[part]
            total = (
                own_part[rows]
                + nn(context_in[2, rows], out_weight[layer, 2])
                + nn(context_in[3, rows], out_weight[layer, 3])
                + state[rows]
                + vector(OUT_BIAS)
            )
            normed, scaled_part, inverse_part = norm_rows(total, vector(GAIN), vector(SHIFT))
            full_mid[layer, rows] = normed.astype(BF16)
            gather.send(part)
            state[rows] = normed
            scaled[layer, 0, rows] = scaled_part
            inverse[layer, 0, rows] = jnp.broadcast_to(inverse_part, (half, LANES))
        for copy in sends + [out_near, out_far, out_pass]:
            drains.append(copy)
        loads[layer][2].wait()
        loads[layer][3].wait()
        scatter = Scatter(place, links, rooms)

        def feed(pieces):
            for first in range(0, up_weight.shape[-1], SLOT):
                columns = slice(first, first + SLOT)
                rows_in = jnp.concatenate([full_mid[layer, piece] for piece in pieces])
                raised = nn(rows_in, up_weight[layer, :, columns]) + small[layer, UP_BIAS : UP_BIAS + 1, columns]
                shaped = gelu_tanh(raised).astype(BF16)
                size = rows_in.shape[0] // len(pieces)
                for at, piece in enumerate(pieces):
                    pre[layer, piece, columns] = raised[at * size : (at + 1) * size]
                    active[layer, piece, columns] = shaped[at * size : (at + 1) * size]
            return nn(jnp.concatenate([active[layer, piece] for piece in pieces]), down_weight[layer])

        own_part[...] = feed([slots[0]])
        gather.near()
        scatter.beside(feed([slots[1]]))
        for part in range(2):
            gather.far(part)
            gather.diagonal(part)
            far_part[...] = feed(
                [pl.ds(2 * SLOT + part * half, half), pl.ds(3 * SLOT + part * half, half)]
            )
            scatter.diagonal(part, far_part[half:])
            scatter.over(part, far_part[:half])
        gather.drain()
        if layer < layers - 1:
            gather = Gather(place, links, full_in.at[layer + 1])
        for part in range(2):
            rows = halves[part]
            total = state[rows] + own_part[rows] + scatter.arrived(part) + vector(DOWN_BIAS)
            normed, scaled_part, inverse_part = norm_rows(total, vector(GAIN + 1), vector(SHIFT + 1))
            state[rows] = normed
            if layer < layers - 1:
                full_in[layer + 1, rows] = normed.astype(BF16)
                gather.send(part)
            else:
                result[rows] = normed.astype(BF16)
            scaled[layer, 1, rows] = scaled_part
            inverse[layer, 1, rows] = jnp.broadcast_to(inverse_part, (half, LANES))
        scatter.drain()
    for copy in drains:
        copy.wait_send()


def run_forward(hidden, seg_rows, seg_cols, small, qkv_all, out_all, up_all, down_all):
    layers, width, wide = qkv_all.shape
    local, hidden_units = out_all.shape[1], up_all.shape[-1]
    rows = hidden.shape[0]
    group = 4 * rows
    half = rows // 2
    vmem = pl.BlockSpec(memory_space=pltpu.VMEM)
    anywhere = pl.BlockSpec(memory_space=pl.ANY)
    shape = jax.ShapeDtypeStruct
    return pl.pallas_call(
        forward_kernel,
        out_shape=[
            shape((rows, width), BF16),
            shape((layers, group, width), BF16),
            shape((layers, group, local), BF16),
            shape((layers, group, local), BF16),
            shape((layers, group, local), BF16),
            shape((layers, group, local), BF16),
            shape((layers, group, width), BF16),
            shape((layers, group, hidden_units), F32),
            shape((layers, group, hidden_units), BF16),
            shape((layers, 2, rows, width), F32),
            shape((layers, 2, rows, LANES), F32),
        ],
        in_specs=[vmem] * 4 + [anywhere] * 4,
        out_specs=[vmem] * 11,
        scratch_shapes=[
            pltpu.VMEM(qkv_all.shape, BF16),
            pltpu.VMEM((layers, 4) + out_all.shape[1:], BF16),
            pltpu.VMEM(up_all.shape, BF16),
            pltpu.VMEM(down_all.shape, BF16),
            pltpu.VMEM((4, rows, local), BF16),
            pltpu.VMEM((rows, width), F32),
            pltpu.VMEM((rows, width), F32),
            pltpu.VMEM((rows, width), F32),
        ]
        + [pltpu.VMEM((2, half, width), BF16)] * 6
        + [pltpu.SemaphoreType.DMA((layers, 4)), pltpu.SemaphoreType.DMA((2, 64))],
        compiler_params=pltpu.CompilerParams(
            collective_id=2, has_side_effects=True, vmem_limit_bytes=60 << 20
        ),
    )(hidden, seg_rows, seg_cols, small, qkv_all, out_all, up_all, down_all)


def packed_inputs(segment_ids, qkv_weight, qv_bias, out_bias, norm_gain, norm_bias, up_bias, down_bias):
    own = lax.axis_index("tensor")
    order = jnp.stack([own, own ^ 1, own ^ 2, own ^ 3])
    seg_rows = segment_ids[order]
    layers, width, _, local = qkv_weight.shape
    padded = jnp.pad(qkv_weight, ((0, 0), (0, 0), (0, 0), (0, SLOT - local)))
    wide = lambda rows: jnp.pad(rows, ((0, 0), (0, 0), (0, width - rows.shape[-1])))
    small = jnp.concatenate(
        [
            out_bias[:, None],
            down_bias[:, None],
            wide(up_bias[:, None]),
            wide(qv_bias),
            norm_gain,
            norm_bias,
            jnp.zeros((layers, 7, width), BF16),
        ],
        axis=1,
    ).astype(F32)
    return seg_rows, seg_rows.T, small, padded.reshape(layers, width, 3 * SLOT)


def norm_forward(total, norm_gain, norm_shift):
    average = jnp.mean(total, axis=-1, keepdims=True)
    centered = total - average
    variance = jnp.mean(centered * centered, axis=-1, keepdims=True)
    inverse = lax.rsqrt(variance + norm_eps)
    scaled = centered * inverse
    return (scaled * norm_gain + norm_shift, scaled, inverse)


def norm_backward(incoming, scaled, inverse, norm_gain):
    gain_grad = jnp.sum(incoming * scaled, axis=0)
    shift_grad = jnp.sum(incoming, axis=0)
    inner = incoming * norm_gain
    result = inverse * (
        inner
        - jnp.mean(inner, axis=-1, keepdims=True)
        - scaled * jnp.mean(inner * scaled, axis=-1, keepdims=True)
    )
    return (result, gain_grad, shift_grad)


def sum_forward(full, weight):
    my_rows = full.shape[0] // lax.axis_size("tensor")

    def partial_value(offset, extent):
        return jnp.dot(full, weight, preferred_element_type=jnp.float32)

    return lax.psum_scatter(
        partial_value(jnp.int32(0), my_rows * lax.axis_size("tensor")).astype(jnp.bfloat16),
        "tensor",
        scatter_dimension=0,
        tiled=True,
    ).astype(jnp.float32)


def sum_backward(full, weight):
    my_rows = full.shape[0] // lax.axis_size("tensor")

    def partial_value(offset, extent):
        return jnp.einsum("nf,df->nd", full, weight, preferred_element_type=jnp.float32)

    return lax.psum_scatter(
        partial_value(jnp.int32(0), my_rows * lax.axis_size("tensor")).astype(jnp.bfloat16),
        "tensor",
        scatter_dimension=0,
        tiled=True,
    ).astype(jnp.float32)


def project_rows(context, out_weight):
    row_context = lax.all_to_all(context, "tensor", split_axis=0, concat_axis=1, tiled=True)
    return jnp.dot(
        row_context,
        lax.all_gather(out_weight, "tensor", axis=0, tiled=True),
        preferred_element_type=jnp.float32,
    )


def spread_rows(shard):
    return lax.all_gather(shard, "tensor", axis=0, tiled=True)


def spread_grads(shard):
    return lax.all_gather(shard, "tensor", axis=0, tiled=True)


def head_split(flat, sequences):
    return flat.reshape(sequences, -1, flat.shape[-1] // HEAD, HEAD)


def scores_of(query_heads, key_heads, allowed):
    raw_scores = jnp.einsum(
        "sqhe,skhe->shqk", query_heads, key_heads, preferred_element_type=jnp.float32
    ) * HEAD ** (-0.5)
    return jnp.where(allowed, raw_scores, -1000000000.0)


def layer_forward(tokens_now, sequences, allowed, weights):
    (
        qkv_weight,
        qv_bias,
        out_weight,
        out_bias,
        norm_gain,
        norm_shift,
        up_weight,
        up_bias,
        down_weight,
        down_bias,
    ) = weights
    local_width = qkv_weight.shape[-1]
    shard_in = tokens_now.astype(jnp.bfloat16)
    full_in = spread_rows(shard_in)
    projected = jnp.dot(
        full_in,
        qkv_weight.reshape(qkv_weight.shape[0], 3 * local_width),
        preferred_element_type=jnp.float32,
    )
    projected = projected.reshape(-1, 3, local_width)
    query_rows = (projected[:, 0] + qv_bias[0]).astype(jnp.bfloat16)
    key_rows = projected[:, 1].astype(jnp.bfloat16)
    value_rows = (projected[:, 2] + qv_bias[1]).astype(jnp.bfloat16)
    scores = scores_of(head_split(query_rows, sequences), head_split(key_rows, sequences), allowed)
    highest = jnp.max(scores, axis=-1, keepdims=True)
    log_total = highest + jnp.log(jnp.sum(jnp.exp(scores - highest), axis=-1, keepdims=True))
    probs_low = jnp.exp(scores - log_total).astype(jnp.bfloat16)
    context = jnp.einsum(
        "shqk,skhe->sqhe",
        probs_low,
        head_split(value_rows, sequences),
        preferred_element_type=jnp.float32,
    )
    context = context.reshape(-1, local_width).astype(jnp.bfloat16)
    attended = project_rows(context, out_weight) + out_bias
    normed, scaled_one, inverse_one = norm_forward(
        tokens_now + attended, norm_gain[0], norm_shift[0]
    )
    shard_mid = normed.astype(jnp.bfloat16)
    full_mid = spread_rows(shard_mid)
    pre_active = jnp.dot(full_mid, up_weight, preferred_element_type=jnp.float32) + up_bias
    active = gelu_tanh(pre_active).astype(jnp.bfloat16)
    lowered = sum_forward(active, down_weight) + down_bias
    result, scaled_two, inverse_two = norm_forward(normed + lowered, norm_gain[1], norm_shift[1])
    stored = (
        full_in,
        query_rows,
        key_rows,
        value_rows,
        log_total,
        context,
        scaled_one,
        inverse_one,
        full_mid,
        pre_active,
        active,
        scaled_two,
        inverse_two,
    )
    return (result, stored)


def layer_backward(incoming, sequences, allowed, weights, stored):
    (
        qkv_weight,
        qv_bias,
        out_weight,
        out_bias,
        norm_gain,
        norm_shift,
        up_weight,
        up_bias,
        down_weight,
        down_bias,
    ) = weights
    (
        stored_in,
        query_rows,
        key_rows,
        value_rows,
        log_total,
        context,
        scaled_one,
        inverse_one,
        stored_mid,
        pre_active,
        active,
        scaled_two,
        inverse_two,
    ) = stored
    local_width = qkv_weight.shape[-1]
    dsum_two, gain_two, shift_two = norm_backward(incoming, scaled_two, inverse_two, norm_gain[1])
    full_lowered = spread_grads(dsum_two.astype(jnp.bfloat16))
    grad_down_weight = jnp.einsum(
        "nf,nd->fd", active, full_lowered, preferred_element_type=jnp.float32
    )
    grad_down_bias = jnp.sum(full_lowered, axis=0, dtype=jnp.float32)
    grad_active = jnp.einsum(
        "nd,fd->nf", full_lowered, down_weight, preferred_element_type=jnp.float32
    )
    gelu_pull = jax.vjp(gelu_tanh, pre_active)[1]
    grad_pre = gelu_pull(grad_active)[0].astype(jnp.bfloat16)
    grad_up_weight = jnp.einsum(
        "nd,nf->df", stored_mid, grad_pre, preferred_element_type=jnp.float32
    )
    grad_up_bias = jnp.sum(grad_pre, axis=0, dtype=jnp.float32)
    grad_normed = dsum_two + sum_backward(grad_pre, up_weight)
    dsum_one, gain_one, shift_one = norm_backward(
        grad_normed, scaled_one, inverse_one, norm_gain[0]
    )
    full_attended = spread_grads(dsum_one.astype(jnp.bfloat16))
    grad_out_weight = jnp.einsum(
        "nf,nd->fd", context, full_attended, preferred_element_type=jnp.float32
    )
    grad_out_bias = jnp.sum(full_attended, axis=0, dtype=jnp.float32)
    grad_context = jnp.einsum(
        "nd,fd->nf", full_attended, out_weight, preferred_element_type=jnp.float32
    ).astype(jnp.bfloat16)
    grad_heads = head_split(grad_context, sequences)
    query_heads = head_split(query_rows, sequences)
    key_heads = head_split(key_rows, sequences)
    value_heads = head_split(value_rows, sequences)
    probs = jnp.exp(scores_of(query_heads, key_heads, allowed) - log_total)
    probs_low = probs.astype(jnp.bfloat16)
    grad_probs = jnp.einsum(
        "sqhe,skhe->shqk", grad_heads, value_heads, preferred_element_type=jnp.float32
    )
    grad_values = jnp.einsum(
        "shqk,sqhe->skhe", probs_low, grad_heads, preferred_element_type=jnp.float32
    )
    grad_scores = probs * (grad_probs - jnp.sum(grad_probs * probs, axis=-1, keepdims=True))
    grad_scores = grad_scores.astype(jnp.bfloat16)
    scale = HEAD ** (-0.5)
    grad_query = (
        jnp.einsum("shqk,skhe->sqhe", grad_scores, key_heads, preferred_element_type=jnp.float32)
        * scale
    )
    grad_keys = (
        jnp.einsum("shqk,sqhe->skhe", grad_scores, query_heads, preferred_element_type=jnp.float32)
        * scale
    )
    stacked = jnp.stack(
        [
            grad_query.reshape(-1, local_width),
            grad_keys.reshape(-1, local_width),
            grad_values.reshape(-1, local_width),
        ],
        axis=1,
    ).astype(jnp.bfloat16)
    grad_qkv_weight = jnp.einsum(
        "nd,ncf->dcf", stored_in, stacked, preferred_element_type=jnp.float32
    )
    grad_qv_bias = jnp.stack(
        [
            jnp.sum(stacked[:, 0], axis=0, dtype=jnp.float32),
            jnp.sum(stacked[:, 2], axis=0, dtype=jnp.float32),
        ]
    )
    grad_tokens = dsum_one + sum_backward(
        stacked.reshape(-1, 3 * local_width),
        qkv_weight.reshape(qkv_weight.shape[0], 3 * local_width),
    )
    grads = (
        grad_qkv_weight,
        grad_qv_bias,
        grad_out_weight,
        grad_out_bias,
        jnp.stack([gain_one, gain_two]),
        jnp.stack([shift_one, shift_two]),
        grad_up_weight,
        grad_up_bias,
        grad_down_weight,
        grad_down_bias,
    )
    return (grad_tokens, grads)


def final_sums(per_layer):
    summed = []
    for layer_index, grads in enumerate(per_layer):
        width = grads[8].shape[-1]
        local = grads[1].shape[-1]
        quarter = 1.0 / lax.axis_size("tensor")
        small = jnp.concatenate(
            [
                grads[4],
                grads[5],
                grads[3][None] * quarter,
                grads[9][None] * quarter,
                jnp.zeros((2, width), F32),
                grads[7][None],
                jnp.pad(grads[1], ((0, 0), (0, width - local))),
                jnp.zeros((5, width), F32),
            ]
        )
        big = [
            member.reshape(member.shape[0], -1).astype(BF16)
            for member in (grads[8], grads[6], grads[0], grads[2])
        ]
        done = sum_over_group(small, *big, which=layer_index)
        done = over_outer_groups(list(done))
        small, down, up, qkv, out = done
        summed.append(
            (
                qkv.reshape(qkv.shape[0], 3, -1).astype(F32),
                small[9:11, :local],
                out.astype(F32),
                small[4],
                small[0:2],
                small[2:4],
                up.astype(F32),
                small[8],
                down.astype(F32),
                small[5],
            )
        )
    return tuple(
        jnp.stack([summed[layer_index][member] for layer_index in range(len(summed))])
        for member in range(10)
    )


def on_device(
    hidden_in,
    segment_ids,
    out_cotangent,
    qkv_weight,
    qv_bias,
    out_weight,
    out_bias,
    norm_gain,
    norm_bias,
    up_weight,
    up_bias,
    down_weight,
    down_bias,
):
    params = (
        qkv_weight,
        qv_bias,
        out_weight,
        out_bias,
        norm_gain,
        norm_bias,
        up_weight,
        up_bias,
        down_weight,
        down_bias,
    )
    layer_count = qkv_weight.shape[0]
    sequences = segment_ids.shape[0]
    allowed = (segment_ids[:, :, None] == segment_ids[:, None, :])[:, None]
    seg_rows, seg_cols, small, qkv_wide = packed_inputs(
        segment_ids, qkv_weight, qv_bias, out_bias, norm_gain, norm_bias, up_bias, down_bias
    )
    out_hidden, *kept = run_forward(
        hidden_in, seg_rows, seg_cols, small, qkv_wide, out_weight, up_weight, down_weight
    )
    own = lax.axis_index("tensor")
    order = jnp.stack([own, own ^ 1, own ^ 2, own ^ 3])

    def sort(kind, layer_index):
        array = kept[kind][layer_index]
        return array.reshape((4, -1) + array.shape[1:])[order].reshape(array.shape)

    stored_all = []
    for layer_index in range(layer_count):
        query = sort(1, layer_index) * jnp.bfloat16(8)
        keys = sort(2, layer_index)
        raw = jnp.where(allowed, jnp.einsum("sqhe,skhe->shqk", head_split(query, sequences), head_split(keys, sequences), preferred_element_type=F32) * 0.125, -1e9)
        log_total = jax.scipy.special.logsumexp(raw, axis=-1, keepdims=True)
        stored_all.append((sort(0, layer_index), query, keys, sort(3, layer_index), log_total, sort(4, layer_index),
          kept[8][layer_index, 0], kept[9][layer_index, 0][:, :1], sort(5, layer_index), sort(6, layer_index), sort(7, layer_index),
          kept[8][layer_index, 1], kept[9][layer_index, 1][:, :1]))
    gradient = out_cotangent.astype(jnp.float32)
    per_layer = [None] * layer_count
    for layer_index in reversed(range(layer_count)):
        weights = tuple((member[layer_index] for member in params))
        gradient, grads = layer_backward(
            gradient, sequences, allowed, weights, stored_all[layer_index]
        )
        per_layer[layer_index] = grads
    gathered = final_sums(per_layer)
    return (out_hidden, gradient) + tuple(gathered)


def solution(mesh):
    placed = (
        P(("dp", "tensor"), None),
        P("dp", None),
        P(("dp", "tensor"), None),
        P(None, None, None, "tensor"),
        P(None, None, "tensor"),
        P(None, "tensor", None),
        P(),
        P(),
        P(),
        P(None, None, "tensor"),
        P(None, "tensor"),
        P(None, "tensor", None),
        P(),
    )
    return jax.shard_map(
        on_device,
        mesh=mesh,
        in_specs=placed,
        out_specs=(
            P(("dp", "tensor"), None),
            P(("dp", "tensor"), None),
            P(None, None, None, "tensor"),
            P(None, None, "tensor"),
            P(None, "tensor", None),
            P(),
            P(),
            P(),
            P(None, None, "tensor"),
            P(None, "tensor"),
            P(None, "tensor", None),
            P(),
        ),
        check_vma=False,
    )
```

```python
import functools

import jax
import jax.numpy as jnp
from jax import lax
from jax.experimental import pallas as pl
from jax.experimental.pallas import tpu as pltpu
from jax.sharding import PartitionSpec as P

HEAD = 64
norm_eps = 1e-05
MESH = pl.DeviceIdType.MESH
Y_SIZE = 2
Z_SIZE = 4
GROUP = Y_SIZE * Z_SIZE
F32 = jnp.float32
BF16 = jnp.bfloat16


class Place:
    def __init__(self):
        self.dp = lax.axis_index("dp")
        self.t = lax.axis_index("tensor")
        inner = lax.rem(self.dp, GROUP)
        base = self.dp - inner
        self.y = lax.rem(inner, Y_SIZE)
        self.z = inner // Y_SIZE
        z_pair = self.z + 1 - 2 * lax.rem(self.z, 2)
        z_mid = Z_SIZE - 1 - self.z
        self.is_end = jnp.logical_or(self.z == 0, self.z == Z_SIZE - 1)
        self.is_inner = jnp.logical_not(self.is_end)
        self.core = (self.dp, self.t + 1 - 2 * lax.rem(self.t, 2))
        self.over = (self.dp, lax.rem(self.t + 2, 4))
        self.diagonal = (self.dp, 3 - self.t)
        self.y_pair = (base + self.z * Y_SIZE + 1 - self.y, self.t)
        self.z_pair = (base + z_pair * Y_SIZE + self.y, self.t)
        self.z_right = (base + jnp.minimum(self.z + 1, Z_SIZE - 1) * Y_SIZE + self.y, self.t)
        self.z_left = (base + jnp.maximum(self.z - 1, 0) * Y_SIZE + self.y, self.t)
        self.z_mid = (base + z_mid * Y_SIZE + self.y, self.t)


class Links:
    def __init__(self, sems):
        self.sems = sems
        self.used = 0

    def copy(self, src, dst, device):
        at = self.used
        self.used += 1
        return pltpu.make_async_remote_copy(
            src_ref=src,
            dst_ref=dst,
            send_sem=self.sems.at[0, at],
            recv_sem=self.sems.at[1, at],
            device_id=device,
            device_id_type=MESH,
        )

    def again(self, src, dst, device):
        self.used -= 1
        return self.copy(src, dst, device)


def greet(devices):
    barrier = pltpu.get_barrier_semaphore()
    for device in devices:
        pl.semaphore_signal(barrier, inc=1, device_id=device, device_id_type=MESH)
    pl.semaphore_wait(barrier, len(devices))


def added(one, two, dtype):
    return (one.astype(F32) + two.astype(F32)).astype(dtype)


def small_item(place, links, mine, steps, landing, result):
    top = pl.ds(0, 8)
    steps[0] = mine[...]
    near = links.copy(steps.at[0, top], landing.at[0, top], place.core)
    near.start()
    yield
    near.wait_recv()
    steps[1] = steps[0]
    steps[1, top] = steps[0, top] + landing[0, top]
    over = links.copy(steps.at[1, top], landing.at[1, top], place.over)
    over.start()
    yield
    over.wait_recv()
    steps[2] = steps[1]
    steps[2, top] = steps[1, top] + landing[1, top]
    across = links.copy(steps.at[2], landing.at[2], place.y_pair)
    across.start()
    yield
    across.wait_recv()
    steps[3] = steps[2] + landing[2]
    pair_in = links.copy(steps.at[3], landing.at[3], place.z_pair)
    mid = links.copy(steps.at[4], landing.at[4], place.z_mid)
    pair_out = links.copy(result, landing.at[3], place.z_pair)

    @pl.when(place.is_end)
    def _():
        pair_in.start()

    yield

    @pl.when(place.is_inner)
    def _():
        pair_in.wait_recv()
        steps[4] = steps[3] + landing[3]
        mid.start()

    yield

    @pl.when(place.is_inner)
    def _():
        mid.wait_recv()
        result[...] = steps[4] + landing[4]
        pair_out.start()

    yield

    @pl.when(place.is_end)
    def _():
        pair_out.wait_recv()
        result[...] = landing[3]

    yield
    near.wait_send()
    over.wait_send()
    across.wait_send()

    @pl.when(place.is_end)
    def _():
        pair_in.wait_send()

    @pl.when(place.is_inner)
    def _():
        mid.wait_send()
        pair_out.wait_send()


class Ticker:
    def __init__(self):
        self.waiting = []
        self.running = []

    def add(self, items):
        self.waiting.extend(items)

    def tick(self, enter=1):
        for _ in range(enter):
            if self.waiting:
                self.running.append(self.waiting.pop(0))
        left = []
        for item in self.running:
            try:
                next(item)
                left.append(item)
            except StopIteration:
                pass
        self.running = left

    def finish(self):
        while self.waiting or self.running:
            self.tick()


def over_outer_groups(values):
    size = lax.axis_size("dp")
    if size == GROUP:
        return values
    groups = [[first + GROUP * turn for turn in range(size // GROUP)] for first in range(GROUP)]
    return [lax.psum(value, "dp", axis_index_groups=groups) for value in values]


def gelu_tanh(pre_active):
    return jax.nn.gelu(pre_active, approximate=True)


LANES = 128
SLOT = 256


def product(left, right, contract):
    return lax.dot_general(left, right, ((contract[:1], contract[1:]), ((), ())), preferred_element_type=F32)


def nn(left, right):
    return product(left, right, (1, 0))


def nt(left, right):
    return product(left, right, (1, 1))


def tn(left, right):
    return product(left, right, (0, 0))


class Gather:
    def __init__(self, place, links, rows):
        half = SLOT // 2
        self.near_copies, self.far_copies, self.pass_copies = [], [], []
        for part in range(2):
            own = pl.ds(part * half, half)
            beside = pl.ds(SLOT + part * half, half)
            over = pl.ds(2 * SLOT + part * half, half)
            diagonal = pl.ds(3 * SLOT + part * half, half)
            self.near_copies.append(links.copy(rows.at[own], rows.at[beside], place.core))
            self.far_copies.append(links.copy(rows.at[own], rows.at[over], place.over))
            self.pass_copies.append(links.copy(rows.at[over], rows.at[diagonal], place.core))

    def send(self, part):
        self.far_copies[part].start()
        self.near_copies[part].start()

    def near(self):
        for copy in self.near_copies:
            copy.wait_recv()

    def far(self, part):
        self.far_copies[part].wait_recv()
        self.pass_copies[part].start()

    def diagonal(self, part):
        self.pass_copies[part].wait_recv()

    def drain(self):
        for copy in self.near_copies + self.far_copies + self.pass_copies:
            copy.wait_send()


class Scatter:
    def __init__(self, place, links, rooms):
        self.core_out, self.core_in, self.far_out, self.far_in, self.near_out, self.near_in = rooms
        self.core_copies = [
            links.copy(self.core_out.at[part], self.core_in.at[part], place.core) for part in range(2)
        ]
        self.far_copies = [
            links.copy(self.far_out.at[part], self.far_in.at[part], place.over) for part in range(2)
        ]
        self.near_copies = [
            links.copy(self.near_out.at[part], self.near_in.at[part], place.core) for part in range(2)
        ]

    def beside(self, term):
        half = SLOT // 2
        for part in range(2):
            self.near_out[part] = term[part * half : (part + 1) * half].astype(BF16)
            self.near_copies[part].start()

    def diagonal(self, part, term):
        self.core_out[part] = term.astype(BF16)
        self.core_copies[part].start()

    def over(self, part, term):
        self.core_copies[part].wait_recv()
        self.far_out[part] = (term + self.core_in[part].astype(F32)).astype(BF16)
        self.far_copies[part].start()

    def arrived(self, part):
        self.near_copies[part].wait_recv()
        self.far_copies[part].wait_recv()
        return self.near_in[part].astype(F32) + self.far_in[part].astype(F32)

    def drain(self):
        for copy in self.core_copies + self.far_copies + self.near_copies:
            copy.wait_send()


def lane_masks():
    lane = lax.broadcasted_iota(jnp.int32, (1, LANES), 1)
    first = jnp.where(lane < HEAD, 1.0, 0.0).astype(BF16)
    return first, (1.0 - first.astype(F32)).astype(BF16)


def head_parts(tile, masks):
    parts = []
    width = tile.shape[-1]
    for first in range(0, width, LANES):
        piece = tile[:, first : min(first + LANES, width)]
        if piece.shape[-1] == HEAD:
            parts.append([piece])
        else:
            parts.append([piece * masks[0], piece * masks[1]])
    return parts


def whole_parts(tile):
    width = tile.shape[-1]
    return [tile[:, first : min(first + LANES, width)] for first in range(0, width, LANES)]


def allowed_rows(seg_cols, seg_rows, slot):
    return seg_cols[:, slot : slot + 1] == seg_rows[slot : slot + 1, :]


def attention_forward(query, keys, values, allowed):
    masks = lane_masks()
    outs = []
    for query_part, key_heads, value_heads in zip(
        whole_parts(query), head_parts(keys, masks), head_parts(values, masks)
    ):
        total = None
        for key_head, value_head in zip(key_heads, value_heads):
            scores = jnp.where(allowed, nt(query_part, key_head), -1000000000.0)
            grown = jnp.exp(scores - jnp.max(scores, axis=-1, keepdims=True))
            probs = grown * (1.0 / jnp.sum(grown, axis=-1, keepdims=True))
            term = nn(probs.astype(BF16), value_head)
            total = term if total is None else total + term
        outs.append(total.astype(BF16))
    return outs


def norm_rows(total, gain, shift):
    average = jnp.mean(total, axis=-1, keepdims=True)
    centered = total - average
    inverse = lax.rsqrt(jnp.mean(centered * centered, axis=-1, keepdims=True) + norm_eps)
    scaled = centered * inverse
    return scaled * gain + shift, scaled, inverse


OUT_BIAS, DOWN_BIAS, UP_BIAS, Q_BIAS, V_BIAS, GAIN, SHIFT = 0, 1, 2, 3, 4, 5, 7


def packed_inputs(segment_ids, qkv_weight, qv_bias, out_bias, norm_gain, norm_bias, up_bias, down_bias):
    own = lax.axis_index("tensor")
    order = jnp.stack([own, own ^ 1, own ^ 2, own ^ 3])
    seg_rows = segment_ids[order]
    layers, width, _, local = qkv_weight.shape
    padded = jnp.pad(qkv_weight, ((0, 0), (0, 0), (0, 0), (0, SLOT - local)))
    wide = lambda rows: jnp.pad(rows, ((0, 0), (0, 0), (0, width - rows.shape[-1])))
    small = jnp.concatenate(
        [
            out_bias[:, None],
            down_bias[:, None],
            wide(up_bias[:, None]),
            wide(qv_bias),
            norm_gain,
            norm_bias,
            jnp.zeros((layers, 7, width), BF16),
        ],
        axis=1,
    ).astype(F32)
    return seg_rows, seg_rows.T, small, padded.reshape(layers, width, 3 * SLOT)


def gelu_slope(raised):
    curve = (2.0 / jnp.pi) ** 0.5
    square = raised * raised
    bent = jnp.tanh(curve * raised * (1.0 + 0.044715 * square))
    return 0.5 * (1.0 + bent) + (0.5 * curve) * raised * (1.0 - bent * bent) * (1.0 + 0.134145 * square)


def attention_backward(query, keys, values, context_grad, allowed):
    masks = lane_masks()
    query_out, key_out, value_out = [], [], []
    for query_part, query_heads, key_heads, value_heads, grad_part, grad_heads in zip(
        whole_parts(query),
        head_parts(query, masks),
        head_parts(keys, masks),
        head_parts(values, masks),
        whole_parts(context_grad),
        head_parts(context_grad, masks),
    ):
        totals = None
        for query_head, key_head, value_head, grad_head in zip(
            query_heads, key_heads, value_heads, grad_heads
        ):
            scores = jnp.where(allowed, nt(key_head, query_part), -1000000000.0)
            grown = jnp.exp(scores - jnp.max(scores, axis=0, keepdims=True))
            probs = grown * (1.0 / jnp.sum(grown, axis=0, keepdims=True))
            probs_grad = nt(value_head, grad_part)
            shared = jnp.sum(probs_grad * probs, axis=0, keepdims=True)
            scores_grad = (probs * (probs_grad - shared)).astype(BF16)
            terms = (
                tn(scores_grad, key_head) * HEAD ** (-0.5),
                nn(scores_grad, query_head),
                nn(probs.astype(BF16), grad_head),
            )
            totals = terms if totals is None else tuple(map(jnp.add, totals, terms))
        query_out.append(totals[0].astype(BF16))
        key_out.append(totals[1].astype(BF16))
        value_out.append(totals[2].astype(BF16))
    return query_out, key_out, value_out


def norm_rows_backward(incoming, scaled, inverse, gain):
    inner = incoming * gain
    return inverse * (
        inner
        - jnp.mean(inner, axis=-1, keepdims=True)
        - scaled * jnp.mean(inner * scaled, axis=-1, keepdims=True)
    )


def column_sum(rows):
    return jnp.sum(rows.astype(F32), axis=0, keepdims=True)


def pair_item(place, links, mine, landing, result, local_sem, start, size):
    from_y, from_z, from_mid = landing
    half = size // 2
    here = pl.ds(pl.multiple_of(start + place.y * half, 16), half)
    there = pl.ds(pl.multiple_of(start + (1 - place.y) * half, 16), half)
    y_out = links.copy(mine.at[there], from_y, place.y_pair)
    pair_in = links.copy(mine.at[here], from_z, place.z_pair)
    mid = links.copy(mine.at[here], from_mid, place.z_mid)
    pair_out = links.copy(from_mid, from_z, place.z_pair)
    back_inner = links.copy(from_mid, result.at[here], place.y_pair)
    back_end = links.again(from_z, result.at[here], place.y_pair)
    keep_inner = pltpu.make_async_copy(from_mid, result.at[here], local_sem)
    keep_end = pltpu.make_async_copy(from_z, result.at[here], local_sem)
    y_out.start()
    yield
    y_out.wait_recv()
    mine[here] = added(mine[here], from_y[...], BF16)

    @pl.when(place.is_end)
    def _():
        pair_in.start()

    yield

    @pl.when(place.is_inner)
    def _():
        pair_in.wait_recv()
        mine[here] = added(mine[here], from_z[...], BF16)
        mid.start()

    yield

    @pl.when(place.is_inner)
    def _():
        mid.wait_recv()
        from_mid[...] = added(mine[here], from_mid[...], BF16)
        pair_out.start()
        back_inner.start()
        keep_inner.start()

    yield

    @pl.when(place.is_end)
    def _():
        pair_out.wait_recv()
        back_end.start()
        keep_end.start()

    yield
    yield
    back_inner.wait_recv()
    y_out.wait_send()

    @pl.when(place.is_end)
    def _():
        pair_in.wait_send()
        back_end.wait_send()
        keep_end.wait()

    @pl.when(place.is_inner)
    def _():
        mid.wait_send()
        pair_out.wait_send()
        back_inner.wait_send()
        keep_inner.wait()


def line_item(place, links, mine, landing, result, local_sem, start, size):
    from_left, from_right, from_y = landing
    quarter = size // Z_SIZE
    last = Z_SIZE - 1
    block = lambda at: pl.ds(start + at * quarter, quarter)
    own = pl.ds(pl.multiple_of(start + place.z * quarter, 16), quarter)
    right = {q: links.copy(mine.at[block(q)], from_left.at[q - 1], place.z_right) for q in range(1, Z_SIZE)}
    left = {q: links.copy(mine.at[block(q)], from_right.at[q], place.z_left) for q in range(last)}
    across = links.copy(mine.at[own], from_y, place.y_pair)
    go_right, go_left = [], []
    for distance in range(1, Z_SIZE):
        for copies, device, sign in ((go_right, place.z_right, 1), (go_left, place.z_left, -1)):
            at = place.z - sign * (distance - 1)
            rows = pl.ds(pl.multiple_of(start + jnp.clip(at, 0, last) * quarter, 16), quarter)
            source = from_y if distance == 1 else result.at[rows]
            copies.append(links.copy(source, result.at[rows], device))
    keep = pltpu.make_async_copy(from_y, result.at[own], local_sem)

    @pl.when(place.z == 0)
    def _():
        for q in range(last, 0, -1):
            right[q].start()

    @pl.when(place.z == last)
    def _():
        for q in range(last):
            left[q].start()

    yield
    for step in range(1, Z_SIZE):

        @pl.when(place.z == step)
        def _():
            for q in range(last, step - 1, -1):
                right[q].wait_recv()
                mine[block(q)] = added(mine[block(q)], from_left[q - 1], BF16)
                if q > step:
                    right[q].start()

        @pl.when(place.z == last - step)
        def _():
            for q in range(last - step + 1):
                left[q].wait_recv()
                mine[block(q)] = added(mine[block(q)], from_right[q], BF16)
                if q < last - step:
                    left[q].start()

        yield
    across.start()
    yield
    across.wait_recv()
    from_y[...] = added(mine[own], from_y[...], BF16)
    keep.start()

    @pl.when(place.z < last)
    def _():
        go_right[0].start()

    @pl.when(place.z > 0)
    def _():
        go_left[0].start()

    yield
    for distance in range(1, Z_SIZE):

        @pl.when(place.z >= distance)
        def _():
            go_right[distance - 1].wait_recv()

        if distance < last:

            @pl.when(jnp.logical_and(place.z >= distance, place.z < last))
            def _():
                go_right[distance].start()

        @pl.when(place.z <= last - distance)
        def _():
            go_left[distance - 1].wait_recv()

        if distance < last:

            @pl.when(jnp.logical_and(place.z <= last - distance, place.z > 0))
            def _():
                go_left[distance].start()

        yield
    across.wait_send()
    keep.wait()
    for q in range(1, Z_SIZE):

        @pl.when(place.z < q)
        def _():
            right[q].wait_send()

        @pl.when(place.z > last - q)
        def _():
            left[last - q].wait_send()

    for distance in range(1, Z_SIZE):

        @pl.when(jnp.logical_and(place.z >= distance - 1, place.z < last))
        def _():
            go_right[distance - 1].wait_send()

        @pl.when(jnp.logical_and(place.z <= last - distance + 1, place.z > 0))
        def _():
            go_left[distance - 1].wait_send()


def item_plan(rows):
    if rows % 768:
        return [(0, rows, False)]
    unit = rows // 768
    return [(0, 224 * unit, False), (448 * unit, 320 * unit, True), (224 * unit, 224 * unit, False)]


def item_rooms(rows, width):
    rooms = []
    for _, size, line in item_plan(rows):
        if line:
            rooms += [pltpu.VMEM((Z_SIZE - 1, size // Z_SIZE, width), BF16)] * 2
            rooms += [pltpu.VMEM((size // Z_SIZE, width), BF16)]
        else:
            rooms += [pltpu.VMEM((size // 2, width), BF16)] * 3
    return rooms


GAIN_ROW, SHIFT_ROW, OUT_BIAS_ROW, DOWN_BIAS_ROW, UP_BIAS_ROW, QV_BIAS_ROW = 0, 2, 4, 5, 8, 9
PARKED = ("full_in", "query", "keys", "values", "context", "full_mid", "pre", "active", "scaled", "inverse")


def whole_kernel(names, *refs):
    place = Place()
    ref = dict(zip(names, refs))
    links = Links(ref["sems"])
    small, state = ref["small"], ref["state"]
    full_in, query, keys, values, context = (ref[name] for name in PARKED[:5])
    full_mid, pre, active, scaled, inverse = (ref[name] for name in PARKED[5:])
    out_own, out_got = ref["out_own"], ref["out_got"]
    own_part, far_part, context_in = ref["own_part"], ref["far_part"], ref["context_in"]
    full_down, pre_grad, full_out, mixed_grad = (
        ref[name] for name in ("full_down", "pre_grad", "full_out", "mixed_grad")
    )
    layers = small.shape[0]
    local = query.shape[-1]
    half = SLOT // 2
    halves = [pl.ds(part * half, half) for part in range(2)]
    slots = [pl.ds(slot * SLOT, SLOT) for slot in range(4)]
    far_pieces = [
        [pl.ds(2 * SLOT + part * half, half), pl.ds(3 * SLOT + part * half, half)] for part in range(2)
    ]

    def vector(layer, row, width=small.shape[-1]):
        return small[layer, row : row + 1, :width]

    loads = {}
    at = 0
    for layer in range(layers):
        for name, target in (
            ("qkv", ref["qkv"].at[layer]),
            ("out", out_own.at[layer]),
            ("up", ref["up"].at[layer]),
            ("down", ref["down"].at[layer]),
        ):
            loads[layer, name] = pltpu.make_async_copy(
                ref[name + "_in"].at[layer], target, ref["load_sems"].at[at]
            )
            loads[layer, name].start()
            at += 1
    cotangent = pltpu.make_async_copy(ref["cotangent_in"], ref["cotangent"], ref["load_sems"].at[at])
    cotangent.start()
    greet((place.core, place.over, place.diagonal, place.y_pair, place.z_pair, place.z_mid))
    rooms = tuple(ref[name] for name in ("core_out", "core_in", "far_out", "far_in", "near_out", "near_in"))
    parks = {}

    def park(layer, these):
        for name in these:
            at = PARKED.index(name)
            parks[layer, name] = pltpu.make_async_copy(
                ref[name], ref["park_" + name].at[layer], ref["park_sems"].at[layer, 0, at]
            )
            parks[layer, name].start()

    def parked(layer, these):
        for name in these:
            if (layer, name) in parks:
                parks.pop((layer, name)).wait()

    def restore(layer, these):
        if layer < 0:
            return
        for name in these:
            at = PARKED.index(name)
            parks[layer, name] = pltpu.make_async_copy(
                ref["park_" + name].at[layer], ref[name], ref["park_sems"].at[layer, 1, at]
            )
            parks[layer, name].start()

    state[...] = ref["hidden"][...].astype(F32)
    gather = Gather(place, links, full_in)
    for part in range(2):
        full_in[halves[part]] = ref["hidden"][halves[part]]
        gather.send(part)
    mixed_grad[...] = jnp.zeros_like(mixed_grad)
    ref["small_grad"][...] = jnp.zeros_like(ref["small_grad"])
    drains = []
    for layer in range(layers):
        qkv_weight, up_weight, down_weight = ref["qkv"].at[layer], ref["up"].at[layer], ref["down"].at[layer]

        def attend(slot):
            rows = slots[slot]
            mixed = nn(full_in[rows], qkv_weight[...])
            query[rows] = ((mixed[:, :local] + vector(layer, Q_BIAS, local)) * HEAD ** (-0.5)).astype(BF16)
            keys[rows] = mixed[:, SLOT : SLOT + local].astype(BF16)
            values[rows] = (
                mixed[:, 2 * SLOT : 2 * SLOT + local] + vector(layer, V_BIAS, local)
            ).astype(BF16)
            outs = attention_forward(
                query[rows], keys[rows], values[rows],
                allowed_rows(ref["seg_cols"], ref["seg_rows"], slot),
            )
            first = 0
            for out in outs:
                context[rows, first : first + out.shape[-1]] = out
                first += out.shape[-1]

        sends = [
            links.copy(context.at[slots[slot]], context_in.at[slot - 1], device)
            for slot, device in ((1, place.core), (2, place.over), (3, place.diagonal))
        ]
        out_near = links.copy(out_own.at[layer], out_got.at[0], place.core)
        out_far = links.copy(out_own.at[layer], out_got.at[1], place.over)
        out_pass = links.copy(out_got.at[1], out_got.at[2], place.core)
        loads[layer, "out"].wait()
        out_near.start()
        loads[layer, "qkv"].wait()
        parked(layer - 1, PARKED)
        attend(0)
        gather.near()
        attend(1)
        sends[0].start()
        gather.far(0)
        gather.far(1)
        out_far.start()
        gather.diagonal(0)
        gather.diagonal(1)
        attend(2)
        sends[1].start()
        out_far.wait_recv()
        out_pass.start()
        attend(3)
        sends[2].start()
        own_part[...] = nn(context[slots[0]], out_own[layer])
        out_near.wait_recv()
        sends[0].wait_recv()
        own_part[...] += nn(context_in[0], out_got[0])
        out_pass.wait_recv()
        sends[1].wait_recv()
        sends[2].wait_recv()
        gather.drain()
        for copy in sends + [out_near, out_far, out_pass]:
            copy.wait_send()
        if layer < layers - 1:
            park(layer, PARKED[:5])
        gather = Gather(place, links, full_mid)
        for part in range(2):
            rows = halves[part]
            total = (
                own_part[rows]
                + nn(context_in[1, rows], out_got[1])
                + nn(context_in[2, rows], out_got[2])
                + state[rows]
                + vector(layer, OUT_BIAS)
            )
            normed, scaled_part, inverse_part = norm_rows(total, vector(layer, GAIN), vector(layer, SHIFT))
            full_mid[rows] = normed.astype(BF16)
            gather.send(part)
            state[rows] = normed
            scaled[0, rows] = scaled_part
            inverse[0, rows] = jnp.broadcast_to(inverse_part, (half, LANES))
        loads[layer, "up"].wait()
        loads[layer, "down"].wait()
        scatter = Scatter(place, links, rooms)

        def feed(pieces):
            rows_in = jnp.concatenate([full_mid[piece] for piece in pieces])
            size = rows_in.shape[0] // len(pieces)
            for first in range(0, up_weight.shape[-1], SLOT):
                columns = slice(first, first + SLOT)
                raised = nn(rows_in, up_weight[:, columns]) + small[layer, UP_BIAS : UP_BIAS + 1, columns]
                shaped = gelu_tanh(raised).astype(BF16)
                for at, piece in enumerate(pieces):
                    pre[piece, columns] = raised[at * size : (at + 1) * size]
                    active[piece, columns] = shaped[at * size : (at + 1) * size]
            return nn(jnp.concatenate([active[piece] for piece in pieces]), down_weight[...])

        own_part[...] = feed([slots[0]])
        gather.near()
        parked(layer, PARKED[:5])
        scatter.beside(feed([slots[1]]))
        for part in range(2):
            gather.far(part)
            gather.diagonal(part)
            far_part[...] = feed(far_pieces[part])
            scatter.diagonal(part, far_part[half:])
            scatter.over(part, far_part[:half])
        gather.drain()
        if layer < layers - 1:
            gather = Gather(place, links, full_in)
        for part in range(2):
            rows = halves[part]
            total = state[rows] + own_part[rows] + scatter.arrived(part) + vector(layer, DOWN_BIAS)
            normed, scaled_part, inverse_part = norm_rows(
                total, vector(layer, GAIN + 1), vector(layer, SHIFT + 1)
            )
            state[rows] = normed
            if layer < layers - 1:
                full_in[rows] = normed.astype(BF16)
                gather.send(part)
            else:
                ref["result"][rows] = normed.astype(BF16)
            scaled[1, rows] = scaled_part
            inverse[1, rows] = jnp.broadcast_to(inverse_part, (half, LANES))
        scatter.drain()
        if layer < layers - 1:
            park(layer, PARKED[5:])

    ticker = Ticker()
    item_count = 0

    def sum_items(layer, name):
        nonlocal item_count
        mine = ref[name + "_grad"].at[layer]
        items = []
        for at, (start, size, line) in enumerate(item_plan(mine.shape[0])):
            landing = tuple(ref[f"land_{name}_{layer}_{at}_{room}"] for room in range(3))
            make = line_item if line else pair_item
            items.append(
                make(
                    place, links, mine, landing, ref[name + "_sum"].at[layer],
                    ref["item_sems"].at[item_count], start, size,
                )
            )
            item_count += 1
        return items

    cotangent.wait()
    state[...] = ref["cotangent"][...].astype(F32)
    for layer in reversed(range(layers)):
        qkv_weight, up_weight, down_weight = ref["qkv"].at[layer], ref["up"].at[layer], ref["down"].at[layer]
        small_grad = ref["small_grad"].at[layer]

        def norm_step(at, part, bias_row, target):
            rows = halves[part]
            incoming, scaled_part = state[rows], scaled[at, rows]
            small_grad[GAIN_ROW + at : GAIN_ROW + at + 1] += column_sum(incoming * scaled_part)
            small_grad[SHIFT_ROW + at : SHIFT_ROW + at + 1] += column_sum(incoming)
            total = norm_rows_backward(incoming, scaled_part, inverse[at, rows][:, :1], vector(layer, GAIN + at))
            state[rows] = total
            low = total.astype(BF16)
            target[rows] = low
            gather.send(part)
            small_grad[bias_row : bias_row + 1] += column_sum(low)

        parked(layer, ("scaled", "inverse"))
        gather = Gather(place, links, full_down)
        scatter = Scatter(place, links, rooms)
        for part in range(2):
            norm_step(1, part, DOWN_BIAS_ROW, full_down)
        parked(layer, PARKED)

        def feed_back(pieces):
            rows_in = jnp.concatenate([full_down[piece] for piece in pieces])
            size = rows_in.shape[0] // len(pieces)
            for first in range(0, up_weight.shape[-1], SLOT):
                columns = slice(first, first + SLOT)
                raised = jnp.concatenate([pre[piece, columns] for piece in pieces])
                low = (nt(rows_in, down_weight[columns]) * gelu_slope(raised)).astype(BF16)
                small_grad[UP_BIAS_ROW : UP_BIAS_ROW + 1, columns] += column_sum(low)
                for at, piece in enumerate(pieces):
                    pre_grad[piece, columns] = low[at * size : (at + 1) * size]
            return nt(jnp.concatenate([pre_grad[piece] for piece in pieces]), up_weight[...])

        own_part[...] = feed_back([slots[0]])
        gather.near()
        ticker.tick()
        scatter.beside(feed_back([slots[1]]))
        for part in range(2):
            gather.far(part)
            gather.diagonal(part)
            far_part[...] = feed_back(far_pieces[part])
            scatter.diagonal(part, far_part[half:])
            scatter.over(part, far_part[:half])
            ticker.tick()
        gather.drain()

        def weight_grad(name, left, right, columns=None):
            target = ref[name + "_grad"].at[layer]
            for first in range(0, left.shape[-1], SLOT):
                last = min(first + SLOT, left.shape[-1])
                target[first:last] = tn(left[:, first:last], right[...]).astype(BF16)

        weight_grad("down", active, full_down)
        ticker.add(sum_items(layer, "down"))
        ticker.tick(3)
        weight_grad("up", full_mid, pre_grad)
        ticker.add(sum_items(layer, "up"))
        restore(layer - 1, ("full_mid", "pre", "active"))
        ticker.tick()
        for part in range(2):
            rows = halves[part]
            state[rows] = state[rows] + own_part[rows] + scatter.arrived(part)
        scatter.drain()
        gather = Gather(place, links, full_out)
        scatter = Scatter(place, links, rooms)
        for part in range(2):
            norm_step(0, part, OUT_BIAS_ROW, full_out)
        restore(layer - 1, ("scaled", "inverse"))

        def attend_back(slot):
            rows = slots[slot]
            context_grad = nt(full_out[rows], out_own[layer]).astype(BF16)
            outs = attention_backward(
                query[rows], keys[rows], values[rows], context_grad,
                allowed_rows(ref["seg_cols"], ref["seg_rows"], slot),
            )
            for at, parts in enumerate(outs):
                first = at * SLOT
                for out in parts:
                    mixed_grad[rows, first : first + out.shape[-1]] = out
                    first += out.shape[-1]
            return nt(mixed_grad[rows], qkv_weight[...])

        own_part[...] = attend_back(0)
        ticker.tick()
        gather.near()
        scatter.beside(attend_back(1))
        gather.far(0)
        ticker.tick()
        gather.far(1)
        far_part[...] = attend_back(2)
        gather.diagonal(0)
        gather.diagonal(1)
        ticker.tick()
        term = attend_back(3)
        for part in range(2):
            scatter.diagonal(part, term[part * half : (part + 1) * half])
        for part in range(2):
            scatter.over(part, far_part[halves[part]])
        gather.drain()
        ticker.tick()
        weight_grad("out", context, full_out)
        for first in range(0, full_in.shape[-1], SLOT):
            rows = pl.ds(first, SLOT)
            mixed = tn(full_in[:, first : first + SLOT], mixed_grad[...]).astype(BF16)
            for at in range(3):
                ref["qkv_grad"][layer, rows, at * local : (at + 1) * local] = mixed[
                    :, at * SLOT : at * SLOT + local
                ]
        sums = column_sum(mixed_grad[...])
        for row, first in ((QV_BIAS_ROW, 0), (QV_BIAS_ROW + 1, 2 * SLOT)):
            small_grad[row : row + 1, :SLOT] = sums[:, first : first + SLOT]
        ticker.add(sum_items(layer, "qkv"))
        ticker.add(sum_items(layer, "out"))
        ticker.add(
            [
                small_item(
                    place, links, small_grad, ref["small_steps"].at[layer], ref["small_land"].at[layer],
                    ref["small_sum"].at[layer],
                )
            ]
        )
        restore(layer - 1, PARKED[:5])
        for part in range(2):
            rows = halves[part]
            state[rows] = state[rows] + own_part[rows] + scatter.arrived(part)
        scatter.drain()
        ticker.tick()
    ref["hidden_grad"][...] = state[...]
    ticker.tick(6)
    ticker.finish()


def run_whole(hidden, cotangent, seg_rows, seg_cols, small, qkv, out, up, down):
    layers, width, wide = qkv.shape
    local, hidden_units = out.shape[1], up.shape[-1]
    rows = hidden.shape[0]
    group, half = 4 * rows, rows // 2
    vmem = pl.BlockSpec(memory_space=pltpu.VMEM)
    anywhere = pl.BlockSpec(memory_space=pl.ANY)
    inputs = [
        ("hidden", hidden, vmem),
        ("seg_rows", seg_rows, vmem),
        ("seg_cols", seg_cols, vmem),
        ("small", small, vmem),
        ("cotangent_in", cotangent, anywhere),
        ("qkv_in", qkv, anywhere),
        ("out_in", out, anywhere),
        ("up_in", up, anywhere),
        ("down_in", down, anywhere),
    ]
    saved = [
        ((group, width), BF16),
        ((group, local), BF16),
        ((group, local), BF16),
        ((group, local), BF16),
        ((group, local), BF16),
        ((group, width), BF16),
        ((group, hidden_units), F32),
        ((group, hidden_units), BF16),
        ((2, rows, width), F32),
        ((2, rows, LANES), F32),
    ]
    grads = {
        "down": (hidden_units, width),
        "up": (width, hidden_units),
        "qkv": (width, 3 * local),
        "out": (local, width),
    }
    outputs = [
        ("result", (rows, width), BF16, vmem),
        ("hidden_grad", (rows, width), F32, vmem),
        ("small_sum", (layers, 16, width), F32, vmem),
    ]
    outputs += [(name + "_sum", (layers,) + shape, BF16, anywhere) for name, shape in grads.items()]
    outputs += [
        ("park_" + name, (layers - 1,) + shape, dtype, anywhere)
        for name, (shape, dtype) in zip(PARKED, saved)
    ]
    scratch = [(name, pltpu.VMEM(shape, dtype)) for name, (shape, dtype) in zip(PARKED, saved)]
    scratch += [
        ("cotangent", pltpu.VMEM((rows, width), BF16)),
        ("qkv", pltpu.VMEM(qkv.shape, BF16)),
        ("out_own", pltpu.VMEM(out.shape, BF16)),
        ("out_got", pltpu.VMEM((3,) + out.shape[1:], BF16)),
        ("up", pltpu.VMEM(up.shape, BF16)),
        ("down", pltpu.VMEM(down.shape, BF16)),
        ("context_in", pltpu.VMEM((3, rows, local), BF16)),
        ("own_part", pltpu.VMEM((rows, width), F32)),
        ("far_part", pltpu.VMEM((rows, width), F32)),
        ("state", pltpu.VMEM((rows, width), F32)),
        ("full_down", pltpu.VMEM((group, width), BF16)),
        ("pre_grad", pltpu.VMEM((group, hidden_units), BF16)),
        ("full_out", pltpu.VMEM((group, width), BF16)),
        ("mixed_grad", pltpu.VMEM((group, wide), BF16)),
        ("small_grad", pltpu.VMEM((layers, 16, width), F32)),
        ("small_steps", pltpu.VMEM((layers, 5, 16, width), F32)),
        ("small_land", pltpu.VMEM((layers, 5, 16, width), F32)),
    ]
    scratch += [
        (name, pltpu.VMEM((2, half, width), BF16))
        for name in ("core_out", "core_in", "far_out", "far_in", "near_out", "near_in")
    ]
    items = 0
    for name, shape in grads.items():
        scratch.append((name + "_grad", pltpu.VMEM((layers,) + shape, BF16)))
        for layer in range(layers):
            items += len(item_plan(shape[0]))
            scratch += [
                (f"land_{name}_{layer}_{at // 3}_{at % 3}", room)
                for at, room in enumerate(item_rooms(*shape))
            ]
    scratch += [
        ("load_sems", pltpu.SemaphoreType.DMA((4 * layers + 1,))),
        ("park_sems", pltpu.SemaphoreType.DMA((layers, 2, len(PARKED)))),
        ("item_sems", pltpu.SemaphoreType.DMA((items,))),
        ("sems", pltpu.SemaphoreType.DMA((2, 320))),
    ]
    names = [entry[0] for entry in inputs + outputs + scratch]
    done = pl.pallas_call(
        functools.partial(whole_kernel, names),
        out_shape=[jax.ShapeDtypeStruct(shape, dtype) for _, shape, dtype, _ in outputs],
        in_specs=[spec for _, _, spec in inputs],
        out_specs=[spec for _, _, _, spec in outputs],
        scratch_shapes=[room for _, room in scratch],
        compiler_params=pltpu.CompilerParams(
            collective_id=0, has_side_effects=True, vmem_limit_bytes=62 << 20
        ),
    )(*[array for _, array, _ in inputs])
    return done[: 3 + len(grads)]


def on_device(
    hidden_in,
    segment_ids,
    out_cotangent,
    qkv_weight,
    qv_bias,
    out_weight,
    out_bias,
    norm_gain,
    norm_bias,
    up_weight,
    up_bias,
    down_weight,
    down_bias,
):
    layers, width, _, local = qkv_weight.shape
    seg_rows, seg_cols, small, qkv_wide = packed_inputs(
        segment_ids, qkv_weight, qv_bias, out_bias, norm_gain, norm_bias, up_bias, down_bias
    )
    result, hidden_grad, *sums = run_whole(
        hidden_in, out_cotangent, seg_rows, seg_cols, small, qkv_wide, out_weight, up_weight, down_weight
    )
    sums = over_outer_groups(sums)
    small_sum, down, up, qkv, out = sums
    return (
        result,
        hidden_grad,
        qkv.reshape(layers, width, 3, local).astype(F32),
        small_sum[:, QV_BIAS_ROW : QV_BIAS_ROW + 2, :local],
        out.astype(F32),
        small_sum[:, OUT_BIAS_ROW],
        small_sum[:, GAIN_ROW : GAIN_ROW + 2],
        small_sum[:, SHIFT_ROW : SHIFT_ROW + 2],
        up.astype(F32),
        small_sum[:, UP_BIAS_ROW, : up_bias.shape[-1]],
        down.astype(F32),
        small_sum[:, DOWN_BIAS_ROW],
    )


def solution(mesh):
    placed = (
        P(("dp", "tensor"), None),
        P("dp", None),
        P(("dp", "tensor"), None),
        P(None, None, None, "tensor"),
        P(None, None, "tensor"),
        P(None, "tensor", None),
        P(),
        P(),
        P(),
        P(None, None, "tensor"),
        P(None, "tensor"),
        P(None, "tensor", None),
        P(),
    )
    return jax.shard_map(
        on_device,
        mesh=mesh,
        in_specs=placed,
        out_specs=(
            P(("dp", "tensor"), None),
            P(("dp", "tensor"), None),
            P(None, None, None, "tensor"),
            P(None, None, "tensor"),
            P(None, "tensor", None),
            P(),
            P(),
            P(),
            P(None, None, "tensor"),
            P(None, "tensor"),
            P(None, "tensor", None),
            P(),
        ),
        check_vma=False,
    )
```

```python
import functools
from types import SimpleNamespace

import jax
import jax.numpy as jnp
from jax import lax
from jax.experimental import pallas as pl
from jax.experimental.pallas import tpu as pltpu
from jax.sharding import PartitionSpec as P

HEAD = 64
norm_eps = 1e-05
MESH = pl.DeviceIdType.MESH
Y_SIZE = 2
Z_SIZE = 4
GROUP = Y_SIZE * Z_SIZE
F32 = jnp.float32
BF16 = jnp.bfloat16


class Place:
    def __init__(self):
        self.dp = lax.axis_index("dp")
        self.t = lax.axis_index("tensor")
        inner = lax.rem(self.dp, GROUP)
        base = self.dp - inner
        self.y = lax.rem(inner, Y_SIZE)
        self.z = inner // Y_SIZE
        z_pair = self.z + 1 - 2 * lax.rem(self.z, 2)
        z_mid = Z_SIZE - 1 - self.z
        self.is_end = jnp.logical_or(self.z == 0, self.z == Z_SIZE - 1)
        self.is_inner = jnp.logical_not(self.is_end)
        self.core = (self.dp, self.t + 1 - 2 * lax.rem(self.t, 2))
        self.over = (self.dp, lax.rem(self.t + 2, 4))
        self.diagonal = (self.dp, 3 - self.t)
        self.y_pair = (base + self.z * Y_SIZE + 1 - self.y, self.t)
        self.z_pair = (base + z_pair * Y_SIZE + self.y, self.t)
        self.z_right = (base + jnp.minimum(self.z + 1, Z_SIZE - 1) * Y_SIZE + self.y, self.t)
        self.z_left = (base + jnp.maximum(self.z - 1, 0) * Y_SIZE + self.y, self.t)
        self.z_mid = (base + z_mid * Y_SIZE + self.y, self.t)


class Links:
    def __init__(self, sems):
        self.sems = sems
        self.used = 0

    def copy(self, src, dst, device):
        at = self.used
        self.used += 1
        assert self.used <= self.sems.shape[1]
        return pltpu.make_async_remote_copy(
            src_ref=src,
            dst_ref=dst,
            send_sem=self.sems.at[0, at],
            recv_sem=self.sems.at[1, at],
            device_id=device,
            device_id_type=MESH,
        )

    def again(self, src, dst, device):
        self.used -= 1
        return self.copy(src, dst, device)


def greet(devices):
    barrier = pltpu.get_barrier_semaphore()
    for device in devices:
        pl.semaphore_signal(barrier, inc=1, device_id=device, device_id_type=MESH)
    pl.semaphore_wait(barrier, len(devices))


def added(one, two, dtype):
    return (one.astype(F32) + two.astype(F32)).astype(dtype)


def small_item(place, links, mine, steps, landing, result):
    top = pl.ds(0, 8)
    steps[0] = mine[...]
    near = links.copy(steps.at[0, top], landing.at[0, top], place.core)
    near.start()
    yield
    near.wait_recv()
    steps[1] = steps[0]
    steps[1, top] = steps[0, top] + landing[0, top]
    over = links.copy(steps.at[1, top], landing.at[1, top], place.over)
    over.start()
    yield
    over.wait_recv()
    steps[2] = steps[1]
    steps[2, top] = steps[1, top] + landing[1, top]
    across = links.copy(steps.at[2], landing.at[2], place.y_pair)
    across.start()
    yield
    across.wait_recv()
    steps[3] = steps[2] + landing[2]
    pair_in = links.copy(steps.at[3], landing.at[3], place.z_pair)
    mid = links.copy(steps.at[4], landing.at[4], place.z_mid)
    pair_out = links.copy(result, landing.at[3], place.z_pair)

    @pl.when(place.is_end)
    def _():
        pair_in.start()

    yield

    @pl.when(place.is_inner)
    def _():
        pair_in.wait_recv()
        steps[4] = steps[3] + landing[3]
        mid.start()

    yield

    @pl.when(place.is_inner)
    def _():
        mid.wait_recv()
        result[...] = steps[4] + landing[4]
        pair_out.start()

    yield

    @pl.when(place.is_end)
    def _():
        pair_out.wait_recv()
        result[...] = landing[3]

    yield
    near.wait_send()
    over.wait_send()
    across.wait_send()

    @pl.when(place.is_end)
    def _():
        pair_in.wait_send()

    @pl.when(place.is_inner)
    def _():
        mid.wait_send()
        pair_out.wait_send()


class Turns:
    def __init__(self, schedule):
        self.schedule = schedule
        self.place = 0
        self.items = []

    def add(self, items):
        self.items.extend(items)

    def take(self):
        for at in self.schedule[self.place] if self.place < len(self.schedule) else ():
            if at < len(self.items):
                next(self.items[at], None)
        self.place += 1

    def finish(self):
        self.take()
        running = self.items
        while running:
            running = [item for item in running if next(item, running) is not running]


def over_outer_groups(values):
    size = lax.axis_size("dp")
    if size == GROUP:
        return values
    groups = [[first + GROUP * turn for turn in range(size // GROUP)] for first in range(GROUP)]
    return [lax.psum(value, "dp", axis_index_groups=groups) for value in values]


def gelu_tanh(pre_active):
    return jax.nn.gelu(pre_active, approximate=True)


LANES = 128
SLOT = 256


def product(left, right, contract):
    return lax.dot_general(left, right, ((contract[:1], contract[1:]), ((), ())), preferred_element_type=F32)


def nn(left, right):
    return product(left, right, (1, 0))


def nt(left, right):
    return product(left, right, (1, 1))


def tn(left, right):
    return product(left, right, (0, 0))


class Gather:
    def __init__(self, place, links, rows):
        half = SLOT // 2
        self.near_copies, self.far_copies, self.pass_copies = [], [], []
        for part in range(2):
            own = pl.ds(part * half, half)
            beside = pl.ds(SLOT + part * half, half)
            over = pl.ds(2 * SLOT + part * half, half)
            diagonal = pl.ds(3 * SLOT + part * half, half)
            self.near_copies.append(links.copy(rows.at[own], rows.at[beside], place.core))
            self.far_copies.append(links.copy(rows.at[own], rows.at[over], place.over))
            self.pass_copies.append(links.copy(rows.at[over], rows.at[diagonal], place.core))

    def send(self, part):
        self.far_copies[part].start()
        self.near_copies[part].start()

    def near(self):
        for copy in self.near_copies:
            copy.wait_recv()

    def far(self, part):
        self.far_copies[part].wait_recv()
        self.pass_copies[part].start()

    def diagonal(self, part):
        self.pass_copies[part].wait_recv()

    def drain(self):
        for copy in self.near_copies + self.far_copies + self.pass_copies:
            copy.wait_send()


class Scatter:
    def __init__(self, place, links, rooms):
        self.core_out, self.core_in, self.far_out, self.far_in, self.near_out, self.near_in = rooms
        self.core_copies = [
            links.copy(self.core_out.at[part], self.core_in.at[part], place.core) for part in range(2)
        ]
        self.far_copies = [
            links.copy(self.far_out.at[part], self.far_in.at[part], place.over) for part in range(2)
        ]
        self.near_copies = [
            links.copy(self.near_out.at[part], self.near_in.at[part], place.core) for part in range(2)
        ]

    def beside(self, term):
        half = SLOT // 2
        for part in range(2):
            self.near_out[part] = term[part * half : (part + 1) * half].astype(BF16)
            self.near_copies[part].start()

    def diagonal(self, part, term):
        self.core_out[part] = term.astype(BF16)
        self.core_copies[part].start()

    def over(self, part, term):
        self.core_copies[part].wait_recv()
        self.far_out[part] = (term + self.core_in[part].astype(F32)).astype(BF16)
        self.far_copies[part].start()

    def arrived(self, part):
        self.near_copies[part].wait_recv()
        self.far_copies[part].wait_recv()
        return self.near_in[part].astype(F32) + self.far_in[part].astype(F32)

    def drain(self):
        for copy in self.core_copies + self.far_copies + self.near_copies:
            copy.wait_send()


def lane_masks():
    lane = lax.broadcasted_iota(jnp.int32, (1, LANES), 1)
    first = jnp.where(lane < HEAD, 1.0, 0.0).astype(BF16)
    return first, (1.0 - first.astype(F32)).astype(BF16)


def head_parts(tile, masks):
    parts = []
    width = tile.shape[-1]
    for first in range(0, width, LANES):
        piece = tile[:, first : min(first + LANES, width)]
        if piece.shape[-1] == HEAD:
            parts.append([piece])
        else:
            parts.append([piece * masks[0], piece * masks[1]])
    return parts


def whole_parts(tile):
    width = tile.shape[-1]
    return [tile[:, first : min(first + LANES, width)] for first in range(0, width, LANES)]


def allowed_rows(seg_cols, seg_rows, slot):
    return seg_cols[slot] == seg_rows[slot : slot + 1, :]


def attention_forward(query, keys, values, allowed):
    masks = lane_masks()
    outs = []
    for query_part, key_heads, value_heads in zip(
        whole_parts(query), head_parts(keys, masks), head_parts(values, masks)
    ):
        total = None
        for key_head, value_head in zip(key_heads, value_heads):
            scores = jnp.where(allowed, nt(query_part, key_head), -1000000000.0)
            grown = jnp.exp(scores - jnp.max(scores, axis=-1, keepdims=True))
            probs = grown * (1.0 / jnp.sum(grown, axis=-1, keepdims=True))
            term = nn(probs.astype(BF16), value_head)
            total = term if total is None else total + term
        outs.append(total.astype(BF16))
    return outs


def norm_rows(total, gain, shift):
    average = jnp.mean(total, axis=-1, keepdims=True)
    centered = total - average
    inverse = lax.rsqrt(jnp.mean(centered * centered, axis=-1, keepdims=True) + norm_eps)
    scaled = centered * inverse
    return scaled * gain + shift, scaled, inverse


OUT_BIAS, DOWN_BIAS, UP_BIAS, Q_BIAS, V_BIAS, GAIN, SHIFT = 0, 1, 2, 3, 4, 5, 7


def gelu_slope(raised):
    curve = (2.0 / jnp.pi) ** 0.5
    square = raised * raised
    bent = jnp.tanh(curve * raised * (1.0 + 0.044715 * square))
    return 0.5 * (1.0 + bent) + (0.5 * curve) * raised * (1.0 - bent * bent) * (1.0 + 0.134145 * square)


def attention_backward(query, keys, values, context_grad, allowed):
    masks = lane_masks()
    query_out, key_out, value_out = [], [], []
    for query_part, query_heads, key_heads, value_heads, grad_part, grad_heads in zip(
        whole_parts(query),
        head_parts(query, masks),
        head_parts(keys, masks),
        head_parts(values, masks),
        whole_parts(context_grad),
        head_parts(context_grad, masks),
    ):
        totals = None
        for query_head, key_head, value_head, grad_head in zip(
            query_heads, key_heads, value_heads, grad_heads
        ):
            scores = jnp.where(allowed, nt(key_head, query_part), -1000000000.0)
            grown = jnp.exp(scores - jnp.max(scores, axis=0, keepdims=True))
            probs = grown * (1.0 / jnp.sum(grown, axis=0, keepdims=True))
            probs_grad = nt(value_head, grad_part)
            shared = jnp.sum(probs_grad * probs, axis=0, keepdims=True)
            scores_grad = (probs * (probs_grad - shared)).astype(BF16)
            terms = (
                tn(scores_grad, key_head) * HEAD ** (-0.5),
                nn(scores_grad, query_head),
                nn(probs.astype(BF16), grad_head),
            )
            totals = terms if totals is None else tuple(map(jnp.add, totals, terms))
        query_out.append(totals[0].astype(BF16))
        key_out.append(totals[1].astype(BF16))
        value_out.append(totals[2].astype(BF16))
    return query_out, key_out, value_out


def norm_rows_backward(incoming, scaled, inverse, gain):
    inner = incoming * gain
    return inverse * (
        inner
        - jnp.mean(inner, axis=-1, keepdims=True)
        - scaled * jnp.mean(inner * scaled, axis=-1, keepdims=True)
    )


def column_sum(rows):
    return jnp.sum(rows.astype(F32), axis=0, keepdims=True)


def pair_item(place, links, mine, landing, result, local_sem, start, size):
    from_y, from_z, from_mid = landing
    half = size // 2
    here = pl.ds(pl.multiple_of(start + place.y * half, 16), half)
    there = pl.ds(pl.multiple_of(start + (1 - place.y) * half, 16), half)
    y_out = links.copy(mine.at[there], from_y, place.y_pair)
    pair_in = links.copy(mine.at[here], from_z, place.z_pair)
    mid = links.copy(mine.at[here], from_mid, place.z_mid)
    pair_out = links.copy(from_mid, from_z, place.z_pair)
    back_inner = links.copy(from_mid, result.at[here], place.y_pair)
    back_end = links.again(from_z, result.at[here], place.y_pair)
    keep_inner = pltpu.make_async_copy(from_mid, result.at[here], local_sem)
    keep_end = pltpu.make_async_copy(from_z, result.at[here], local_sem)
    y_out.start()
    yield
    y_out.wait_recv()
    mine[here] = added(mine[here], from_y[...], BF16)

    @pl.when(place.is_end)
    def _():
        pair_in.start()

    yield

    @pl.when(place.is_inner)
    def _():
        pair_in.wait_recv()
        mine[here] = added(mine[here], from_z[...], BF16)
        mid.start()

    yield

    @pl.when(place.is_inner)
    def _():
        mid.wait_recv()
        from_mid[...] = added(mine[here], from_mid[...], BF16)
        pair_out.start()
        back_inner.start()
        keep_inner.start()

    yield

    @pl.when(place.is_end)
    def _():
        pair_out.wait_recv()
        back_end.start()
        keep_end.start()

    yield
    back_inner.wait_recv()
    yield
    y_out.wait_send()

    @pl.when(place.is_end)
    def _():
        pair_in.wait_send()
        back_end.wait_send()
        keep_end.wait()

    @pl.when(place.is_inner)
    def _():
        mid.wait_send()
        pair_out.wait_send()
        back_inner.wait_send()
        keep_inner.wait()


def line_item(place, links, mine, landing, result, local_sem, start, size):
    from_left, from_right, from_y = landing
    quarter = size // Z_SIZE
    last = Z_SIZE - 1
    block = lambda at: pl.ds(start + at * quarter, quarter)
    own = pl.ds(pl.multiple_of(start + place.z * quarter, 16), quarter)
    right = {q: links.copy(mine.at[block(q)], from_left.at[q - 1], place.z_right) for q in range(1, Z_SIZE)}
    left = {q: links.copy(mine.at[block(q)], from_right.at[q], place.z_left) for q in range(last)}
    across = links.copy(mine.at[own], from_y, place.y_pair)
    go_right, go_left = [], []
    for distance in range(1, Z_SIZE):
        for copies, device, sign in ((go_right, place.z_right, 1), (go_left, place.z_left, -1)):
            at = place.z - sign * (distance - 1)
            rows = pl.ds(pl.multiple_of(start + jnp.clip(at, 0, last) * quarter, 16), quarter)
            source = from_y if distance == 1 else result.at[rows]
            copies.append(links.copy(source, result.at[rows], device))
    keep = pltpu.make_async_copy(from_y, result.at[own], local_sem)

    @pl.when(place.z == 0)
    def _():
        for q in range(last, 0, -1):
            right[q].start()

    @pl.when(place.z == last)
    def _():
        for q in range(last):
            left[q].start()

    yield
    for step in range(1, Z_SIZE):

        @pl.when(place.z == step)
        def _():
            for q in range(last, step - 1, -1):
                right[q].wait_recv()
                mine[block(q)] = added(mine[block(q)], from_left[q - 1], BF16)
                if q > step:
                    right[q].start()

        @pl.when(place.z == last - step)
        def _():
            for q in range(last - step + 1):
                left[q].wait_recv()
                mine[block(q)] = added(mine[block(q)], from_right[q], BF16)
                if q < last - step:
                    left[q].start()

        yield
    across.start()
    yield
    across.wait_recv()
    from_y[...] = added(mine[own], from_y[...], BF16)
    keep.start()

    @pl.when(place.z < last)
    def _():
        go_right[0].start()

    @pl.when(place.z > 0)
    def _():
        go_left[0].start()

    yield
    for distance in range(1, Z_SIZE):

        @pl.when(place.z >= distance)
        def _():
            go_right[distance - 1].wait_recv()

        if distance < last:

            @pl.when(jnp.logical_and(place.z >= distance, place.z < last))
            def _():
                go_right[distance].start()

        @pl.when(place.z <= last - distance)
        def _():
            go_left[distance - 1].wait_recv()

        if distance < last:

            @pl.when(jnp.logical_and(place.z <= last - distance, place.z > 0))
            def _():
                go_left[distance].start()

        yield
    across.wait_send()
    keep.wait()
    for q in range(1, Z_SIZE):

        @pl.when(place.z < q)
        def _():
            right[q].wait_send()

        @pl.when(place.z > last - q)
        def _():
            left[last - q].wait_send()

    for distance in range(1, Z_SIZE):

        @pl.when(jnp.logical_and(place.z >= distance - 1, place.z < last))
        def _():
            go_right[distance - 1].wait_send()

        @pl.when(jnp.logical_and(place.z <= last - distance + 1, place.z > 0))
        def _():
            go_left[distance - 1].wait_send()


ITEM_ROWS = dict(
    down=((192, False), (192, False), (192, True), (192, False)),
    up=((192, False), (192, False), (192, True), (192, False)),
    qkv=((128, False), (96, False), (256, True), (96, False)),
    out=((192, False),),
)
SCHEDULE = (
    (),
    (),
    (),
    (),
    (),
    (0, 1, 2, 3),
    (4, 5, 6),
    (0, 2, 7),
    (1,),
    (2, 3, 6),
    (2, 2, 0, 1, 6, 4, 5),
    (2, 6, 6, 3, 7, 0, 4),
    (1, 5, 8, 9, 10, 11, 12, 13, 2, 6),
    (0, 3, 7, 13),
    (1, 4, 8),
    (5, 13, 9, 10, 2, 11),
    (6, 8, 12),
    (0, 1, 3, 4, 7, 9, 11),
    (2, 5, 10, 12),
    (6, 3, 14, 13, 13, 8, 15, 16, 17),
    (4, 7, 9, 11, 18, 20),
    (6, 5, 10, 10, 12, 13, 16),
    (8, 14, 9, 20),
    (11, 14, 16, 15),
    (13, 7, 12, 16, 16, 15, 20, 17, 19),
    (14, 20, 20, 18, 8, 21),
    (9, 10, 11, 14, 15, 17, 24),
    (10, 12, 16, 17, 18, 22, 23),
    (15, 19, 10, 25, 20, 24, 26, 16, 18, 19, 21, 17, 10, 14, 20, 27, 24, 21, 16, 22, 23, 19, 22, 23, 27, 18, 15, 20, 25, 24, 24, 16, 26, 21, 25, 27, 22, 23, 26, 25, 19, 17, 20, 18, 21, 24, 22, 23, 19, 25, 26, 27, 24, 21, 22, 26, 27, 23, 24, 25, 24, 27, 27, 26),
)


def item_plan(name, rows):
    sizes = ITEM_ROWS[name]
    if sum(size for size, _ in sizes) != rows:
        sizes = ((rows, False),)
    plan, first = [], 0
    for size, line in sizes:
        plan.append((first, size, line))
        first += size
    return plan


def land_name(*place):
    return "_".join(map(str, place))


def item_rooms(name, rows, width):
    rooms = []
    for _, size, line in item_plan(name, rows):
        if line:
            rooms += [pltpu.VMEM((Z_SIZE - 1, size // Z_SIZE, width), BF16)] * 2
            rooms += [pltpu.VMEM((size // Z_SIZE, width), BF16)]
        else:
            rooms += [pltpu.VMEM((size // 2, width), BF16)] * 3
    return rooms


GAIN_ROW, SHIFT_ROW, OUT_BIAS_ROW, DOWN_BIAS_ROW, UP_BIAS_ROW, QV_BIAS_ROW = 0, 2, 4, 5, 8, 9
PARKED = tuple(
    dict(
        full_in=0, query=0, keys=0, values=0, context=0, full_mid=0, pre=0, active=0, scaled=0, inverse=0
    )
)


def whole_kernel(names, *refs):
    place = Place()
    table = dict(zip(names, refs))
    ref = SimpleNamespace(**table)
    links = Links(ref.sems)
    small, state = ref.small, ref.state
    full_in, query, keys, values, context = (table[name] for name in PARKED[:5])
    full_mid, pre, active, scaled, inverse = (table[name] for name in PARKED[5:])
    out_own, out_got = ref.out_own, ref.out_got
    own_part, far_part, context_in = ref.own_part, ref.far_part, ref.context_in
    full_down, pre_grad, full_out = ref.full_down, ref.pre_grad, ref.full_out
    mixed_grads = [ref.query_grad, ref.key_grad, ref.value_grad]
    layers = small.shape[0]
    local = query.shape[-1]
    half = SLOT // 2
    halves = [pl.ds(part * half, half) for part in range(2)]
    thirds = [pl.ds(part * local, local) for part in range(3)]
    slots = [pl.ds(slot * SLOT, SLOT) for slot in range(4)]
    far_pieces = [
        [pl.ds(2 * SLOT + part * half, half), pl.ds(3 * SLOT + part * half, half)] for part in range(2)
    ]

    def vector(layer, row, width=small.shape[-1]):
        return small[layer, row : row + 1, :width]

    loads = {}
    at = 0
    for layer in range(layers):
        for name, target in (
            ("qkv", ref.qkv.at[layer]),
            ("out", out_own.at[layer]),
            ("up", ref.up.at[layer]),
            ("down", ref.down.at[layer]),
        ):
            loads[layer, name] = pltpu.make_async_copy(
                table[name + "_in"].at[layer], target, ref.load_sems.at[at]
            )
            loads[layer, name].start()
            at += 1
    cotangent = pltpu.make_async_copy(ref.cotangent_in, ref.cotangent, ref.load_sems.at[at])
    cotangent.start()
    for layer in range(layers):
        for source, row in (
            (ref.out_bias_in, OUT_BIAS),
            (ref.down_bias_in, DOWN_BIAS),
            (ref.up_bias_in, UP_BIAS),
            (ref.qv_bias_in, Q_BIAS),
            (ref.norm_gain_in, GAIN),
            (ref.norm_bias_in, SHIFT),
        ):
            rows = source[layer].astype(F32).reshape(-1, source.shape[-1])
            small[layer, row : row + rows.shape[0], : rows.shape[1]] = rows
    for slot, index in enumerate((place.t, place.core[1], place.over[1], place.diagonal[1])):
        row = ref.segments[pl.ds(index, 1), :].astype(F32)
        ref.seg_rows[slot : slot + 1] = row
        ref.seg_cols[slot] = jnp.transpose(jnp.broadcast_to(row, ref.seg_cols.shape[1:]))
    greet((place.core, place.over, place.diagonal, place.y_pair, place.z_pair, place.z_mid))
    rooms = (ref.core_out, ref.core_in, ref.far_out, ref.far_in, ref.near_out, ref.near_in)
    parks = {}

    def park(layer, these):
        for name in these:
            at = PARKED.index(name)
            parks[layer, name] = pltpu.make_async_copy(
                table[name], table["park_" + name].at[layer], ref.park_sems.at[layer, 0, at]
            )
            parks[layer, name].start()

    def parked(layer, these):
        for name in these:
            if (layer, name) in parks:
                parks.pop((layer, name)).wait()

    def restore(layer, these):
        if layer < 0:
            return
        for name in these:
            at = PARKED.index(name)
            parks[layer, name] = pltpu.make_async_copy(
                table["park_" + name].at[layer], table[name], ref.park_sems.at[layer, 1, at]
            )
            parks[layer, name].start()

    state[...] = ref.hidden[...].astype(F32)
    gather = Gather(place, links, full_in)
    for part in range(2):
        full_in[halves[part]] = ref.hidden[halves[part]]
        gather.send(part)
    ref.small_grad[...] = jnp.zeros_like(ref.small_grad)
    drains = []
    for layer in range(layers):
        qkv_weight, up_weight, down_weight = ref.qkv.at[layer], ref.up.at[layer], ref.down.at[layer]

        def attend(slot):
            rows = slots[slot]
            rows_in = full_in[rows]
            mixed = [nt(rows_in, qkv_weight[piece]) for piece in thirds]
            query[rows] = ((mixed[0] + vector(layer, Q_BIAS, local)) * HEAD ** (-0.5)).astype(BF16)
            keys[rows] = mixed[1].astype(BF16)
            values[rows] = (mixed[2] + vector(layer, V_BIAS, local)).astype(BF16)
            outs = attention_forward(
                query[rows], keys[rows], values[rows],
                allowed_rows(ref.seg_cols, ref.seg_rows, slot),
            )
            first = 0
            for out in outs:
                context[rows, first : first + out.shape[-1]] = out
                first += out.shape[-1]

        sends = [
            links.copy(context.at[slots[slot]], context_in.at[slot - 1], device)
            for slot, device in ((1, place.core), (2, place.over), (3, place.diagonal))
        ]
        out_near = links.copy(out_own.at[layer], out_got.at[0], place.core)
        out_far = links.copy(out_own.at[layer], out_got.at[1], place.over)
        out_pass = links.copy(out_got.at[1], out_got.at[2], place.core)
        loads[layer, "out"].wait()
        out_near.start()
        loads[layer, "qkv"].wait()
        parked(layer - 1, PARKED)
        attend(0)
        gather.near()
        attend(1)
        sends[0].start()
        gather.far(0)
        gather.far(1)
        out_far.start()
        attend(2)
        sends[1].start()
        out_far.wait_recv()
        out_pass.start()
        gather.diagonal(0)
        gather.diagonal(1)
        attend(3)
        sends[2].start()
        own_part[...] = nn(context[slots[0]], out_own[layer])
        out_near.wait_recv()
        sends[0].wait_recv()
        own_part[...] += nn(context_in[0], out_got[0])
        out_pass.wait_recv()
        sends[1].wait_recv()
        sends[2].wait_recv()
        gather.drain()
        for copy in sends + [out_near, out_far, out_pass]:
            copy.wait_send()
        if layer < layers - 1:
            park(layer, PARKED[:5])
        gather = Gather(place, links, full_mid)
        for part in range(2):
            rows = halves[part]
            total = (
                own_part[rows]
                + nn(context_in[1, rows], out_got[1])
                + nn(context_in[2, rows], out_got[2])
                + state[rows]
                + vector(layer, OUT_BIAS)
            )
            normed, scaled_part, inverse_part = norm_rows(total, vector(layer, GAIN), vector(layer, SHIFT))
            full_mid[rows] = normed.astype(BF16)
            gather.send(part)
            state[rows] = normed
            scaled[0, rows] = scaled_part
            inverse[0, rows] = jnp.broadcast_to(inverse_part, (half, LANES))
        loads[layer, "up"].wait()
        loads[layer, "down"].wait()
        scatter = Scatter(place, links, rooms)

        def feed(pieces):
            rows_in = jnp.concatenate([full_mid[piece] for piece in pieces])
            size = rows_in.shape[0] // len(pieces)
            for first in range(0, up_weight.shape[-1], SLOT):
                columns = slice(first, first + SLOT)
                raised = nn(rows_in, up_weight[:, columns]) + small[layer, UP_BIAS : UP_BIAS + 1, columns]
                shaped = gelu_tanh(raised).astype(BF16)
                for at, piece in enumerate(pieces):
                    pre[piece, columns] = raised[at * size : (at + 1) * size]
                    active[piece, columns] = shaped[at * size : (at + 1) * size]
            return nn(jnp.concatenate([active[piece] for piece in pieces]), down_weight[...])

        own_part[...] = feed([slots[0]])
        gather.near()
        parked(layer, PARKED[:5])
        scatter.beside(feed([slots[1]]))
        for part in range(2):
            gather.far(part)
            gather.diagonal(part)
            far_part[...] = feed(far_pieces[part])
            scatter.diagonal(part, far_part[half:])
            scatter.over(part, far_part[:half])
        gather.drain()
        if layer < layers - 1:
            gather = Gather(place, links, full_in)
        for part in range(2):
            rows = halves[part]
            total = state[rows] + own_part[rows] + scatter.arrived(part) + vector(layer, DOWN_BIAS)
            normed, scaled_part, inverse_part = norm_rows(
                total, vector(layer, GAIN + 1), vector(layer, SHIFT + 1)
            )
            state[rows] = normed
            if layer < layers - 1:
                full_in[rows] = normed.astype(BF16)
                gather.send(part)
            else:
                ref.result[rows] = normed.astype(BF16)
            scaled[1, rows] = scaled_part
            inverse[1, rows] = jnp.broadcast_to(inverse_part, (half, LANES))
        scatter.drain()
        if layer < layers - 1:
            park(layer, PARKED[5:])

    turns = Turns(SCHEDULE)
    item_count = 0

    def sum_items(layer, name):
        nonlocal item_count
        mine = table[name + "_grad"].at[layer]
        items = []
        for at, (start, size, line) in enumerate(item_plan(name, mine.shape[0])):
            landing = tuple(table[land_name(name, layer, at, room)] for room in range(3))
            make = line_item if line else pair_item
            items.append(
                make(
                    place, links, mine, landing, table[name + "_sum"].at[layer],
                    ref.item_sems.at[item_count], start, size,
                )
            )
            item_count += 1
        return items

    cotangent.wait()
    state[...] = ref.cotangent[...].astype(F32)
    for layer in reversed(range(layers)):
        qkv_weight, up_weight, down_weight = ref.qkv.at[layer], ref.up.at[layer], ref.down.at[layer]
        small_grad = ref.small_grad.at[layer]

        def norm_step(at, part, bias_row, target):
            rows = halves[part]
            incoming, scaled_part = state[rows], scaled[at, rows]
            small_grad[GAIN_ROW + at : GAIN_ROW + at + 1] += column_sum(incoming * scaled_part)
            small_grad[SHIFT_ROW + at : SHIFT_ROW + at + 1] += column_sum(incoming)
            total = norm_rows_backward(incoming, scaled_part, inverse[at, rows][:, :1], vector(layer, GAIN + at))
            state[rows] = total
            low = total.astype(BF16)
            target[rows] = low
            gather.send(part)
            small_grad[bias_row : bias_row + 1] += column_sum(low)

        parked(layer, PARKED[8:])
        gather = Gather(place, links, full_down)
        scatter = Scatter(place, links, rooms)
        for part in range(2):
            norm_step(1, part, DOWN_BIAS_ROW, full_down)
        turns.take()
        parked(layer, PARKED)

        def feed_back(pieces):
            rows_in = jnp.concatenate([full_down[piece] for piece in pieces])
            size = rows_in.shape[0] // len(pieces)
            for first in range(0, up_weight.shape[-1], SLOT):
                columns = slice(first, first + SLOT)
                raised = jnp.concatenate([pre[piece, columns] for piece in pieces])
                low = (nt(rows_in, down_weight[columns]) * gelu_slope(raised)).astype(BF16)
                small_grad[UP_BIAS_ROW : UP_BIAS_ROW + 1, columns] += column_sum(low)
                for at, piece in enumerate(pieces):
                    pre_grad[piece, columns] = low[at * size : (at + 1) * size]
            return nt(jnp.concatenate([pre_grad[piece] for piece in pieces]), up_weight[...])

        own_part[...] = feed_back([slots[0]])
        turns.take()
        gather.near()
        scatter.beside(feed_back([slots[1]]))
        turns.take()
        for part in range(2):
            gather.far(part)
            gather.diagonal(part)
            far_part[...] = feed_back(far_pieces[part])
            scatter.diagonal(part, far_part[half:])
            scatter.over(part, far_part[:half])
            turns.take()
        gather.drain()

        def weight_grad(name, left, right, columns=None):
            target = table[name + "_grad"].at[layer]
            for first in range(0, left.shape[-1], SLOT):
                last = min(first + SLOT, left.shape[-1])
                target[first:last] = tn(left[:, first:last], right[...]).astype(BF16)

        weight_grad("down", active, full_down)
        turns.add(sum_items(layer, "down"))
        turns.take()
        weight_grad("up", full_mid, pre_grad)
        turns.add(sum_items(layer, "up"))
        restore(layer - 1, PARKED[5:8])
        turns.take()
        for part in range(2):
            rows = halves[part]
            state[rows] = state[rows] + own_part[rows] + scatter.arrived(part)
        scatter.drain()
        gather = Gather(place, links, full_out)
        scatter = Scatter(place, links, rooms)
        for part in range(2):
            norm_step(0, part, OUT_BIAS_ROW, full_out)
        restore(layer - 1, PARKED[8:])
        turns.take()

        def attend_back(slot):
            rows = slots[slot]
            context_grad = nt(full_out[rows], out_own[layer]).astype(BF16)
            outs = attention_backward(
                query[rows], keys[rows], values[rows], context_grad,
                allowed_rows(ref.seg_cols, ref.seg_rows, slot),
            )
            total = None
            for target, parts, piece in zip(mixed_grads, outs, thirds):
                first = 0
                for out in parts:
                    target[rows, first : first + out.shape[-1]] = out
                    first += out.shape[-1]
                term = nn(target[rows], qkv_weight[piece])
                total = term if total is None else total + term
            return total

        own_part[...] = attend_back(0)
        turns.take()
        gather.near()
        scatter.beside(attend_back(1))
        turns.take()
        gather.far(0)
        gather.far(1)
        far_part[...] = attend_back(2)
        turns.take()
        gather.diagonal(0)
        gather.diagonal(1)
        term = attend_back(3)
        for part in range(2):
            scatter.diagonal(part, term[part * half : (part + 1) * half])
        for part in range(2):
            scatter.over(part, far_part[halves[part]])
        turns.take()
        gather.drain()
        weight_grad("out", context, full_out)
        for target, piece in zip(mixed_grads, thirds):
            ref.qkv_grad[layer, piece] = tn(target[...], full_in[...]).astype(BF16)
        for at, target in enumerate((mixed_grads[0], mixed_grads[2])):
            small_grad[QV_BIAS_ROW + at : QV_BIAS_ROW + at + 1, :local] = column_sum(target[...])
        turns.add(sum_items(layer, "qkv"))
        turns.add(sum_items(layer, "out"))
        turns.add(
            [
                small_item(
                    place, links, small_grad, ref.small_steps.at[layer], ref.small_land.at[layer],
                    ref.small_sum.at[layer],
                )
            ]
        )
        restore(layer - 1, PARKED[:5])
        turns.take()
        for part in range(2):
            rows = halves[part]
            state[rows] = state[rows] + own_part[rows] + scatter.arrived(part)
        scatter.drain()
        turns.take()
    ref.hidden_grad[...] = state[...]
    turns.finish()


def run_whole(hidden, cotangent, segments, vectors, qkv, out, up, down):
    layers, _, width = qkv.shape
    local, hidden_units = out.shape[1], up.shape[-1]
    rows = hidden.shape[0]
    group, half = 4 * rows, rows // 2
    vmem = pl.BlockSpec(memory_space=pltpu.VMEM)
    anywhere = pl.BlockSpec(memory_space=pl.ANY)
    inputs = dict(
        hidden=(hidden, vmem),
        segments=(segments, vmem),
        cotangent_in=(cotangent, anywhere),
        qkv_in=(qkv, anywhere),
        out_in=(out, anywhere),
        up_in=(up, anywhere),
        down_in=(down, anywhere),
    )
    inputs.update({name + "_in": (array, vmem) for name, array in vectors.items()})
    saved = [
        ((group, width), BF16),
        ((group, local), BF16),
        ((group, local), BF16),
        ((group, local), BF16),
        ((group, local), BF16),
        ((group, width), BF16),
        ((group, hidden_units), F32),
        ((group, hidden_units), BF16),
        ((2, rows, width), F32),
        ((2, rows, LANES), F32),
    ]
    grads = dict(
        down=(hidden_units, width),
        up=(width, hidden_units),
        qkv=(3 * local, width),
        out=(local, width),
    )
    outputs = dict(
        result=((rows, width), BF16, vmem),
        hidden_grad=((rows, width), F32, vmem),
        small_sum=((layers, 16, width), F32, vmem),
    )
    outputs.update({name + "_sum": ((layers,) + shape, BF16, anywhere) for name, shape in grads.items()})
    outputs.update(
        {
            "park_" + name: ((layers - 1,) + shape, dtype, anywhere)
            for name, (shape, dtype) in zip(PARKED, saved)
        }
    )
    scratch = {name: pltpu.VMEM(shape, dtype) for name, (shape, dtype) in zip(PARKED, saved)}
    scratch.update(
        seg_rows=pltpu.VMEM((4, rows), F32),
        seg_cols=pltpu.VMEM((4, rows, rows), F32),
        small=pltpu.VMEM((layers, 16, width), F32),
        cotangent=pltpu.VMEM((rows, width), BF16),
        qkv=pltpu.VMEM(qkv.shape, BF16),
        out_own=pltpu.VMEM(out.shape, BF16),
        out_got=pltpu.VMEM((3,) + out.shape[1:], BF16),
        up=pltpu.VMEM(up.shape, BF16),
        down=pltpu.VMEM(down.shape, BF16),
        context_in=pltpu.VMEM((3, rows, local), BF16),
        own_part=pltpu.VMEM((rows, width), F32),
        far_part=pltpu.VMEM((rows, width), F32),
        state=pltpu.VMEM((rows, width), F32),
        full_down=pltpu.VMEM((group, width), BF16),
        pre_grad=pltpu.VMEM((group, hidden_units), BF16),
        full_out=pltpu.VMEM((group, width), BF16),
        query_grad=pltpu.VMEM((group, local), BF16),
        key_grad=pltpu.VMEM((group, local), BF16),
        value_grad=pltpu.VMEM((group, local), BF16),
        small_grad=pltpu.VMEM((layers, 16, width), F32),
        small_steps=pltpu.VMEM((layers, 5, 16, width), F32),
        small_land=pltpu.VMEM((layers, 5, 16, width), F32),
    )
    room = pltpu.VMEM((2, half, width), BF16)
    scratch.update(core_out=room, core_in=room, far_out=room, far_in=room, near_out=room, near_in=room)
    items = 0
    for name, shape in grads.items():
        scratch[name + "_grad"] = pltpu.VMEM((layers,) + shape, BF16)
        for layer in range(layers):
            items += len(item_plan(name, shape[0]))
            for at, land in enumerate(item_rooms(name, *shape)):
                scratch[land_name(name, layer, at // 3, at % 3)] = land
    scratch.update(
        load_sems=pltpu.SemaphoreType.DMA((4 * layers + 1,)),
        park_sems=pltpu.SemaphoreType.DMA((layers, 2, len(PARKED))),
        item_sems=pltpu.SemaphoreType.DMA((items,)),
        sems=pltpu.SemaphoreType.DMA((2, 400)),
    )
    names = [*inputs, *outputs, *scratch]
    done = pl.pallas_call(
        functools.partial(whole_kernel, names),
        out_shape=[jax.ShapeDtypeStruct(shape, dtype) for shape, dtype, _ in outputs.values()],
        in_specs=[spec for _, spec in inputs.values()],
        out_specs=[spec for _, _, spec in outputs.values()],
        scratch_shapes=list(scratch.values()),
        compiler_params=pltpu.CompilerParams(
            collective_id=0, has_side_effects=True, vmem_limit_bytes=62 << 20
        ),
    )(*[array for array, _ in inputs.values()])
    return done[: 3 + len(grads)]


def widen_kernel(result_in, hidden_in, small, down_in, up_in, qkv_in, out_in, *outs):
    result, hidden, qkv, qv_bias, out, out_bias, gain, shift, up, up_bias, down, down_bias = outs
    for source, target in ((down_in, down), (up_in, up), (qkv_in, qkv), (out_in, out)):
        target[...] = source[...].astype(F32)

    @pl.when(jnp.logical_and(pl.program_id(0) == 0, pl.program_id(1) == 0))
    def _():
        result[...] = result_in[...]
        hidden[...] = hidden_in[...]
        for layer in range(small.shape[0]):
            here = pl.ds(layer, 1)
            out_bias[here] = small[layer, OUT_BIAS_ROW : OUT_BIAS_ROW + 1]
            down_bias[here] = small[layer, DOWN_BIAS_ROW : DOWN_BIAS_ROW + 1]
            up_bias[here] = small[layer, UP_BIAS_ROW : UP_BIAS_ROW + 1, : up_bias.shape[-1]]
            qv_bias[layer] = small[layer, QV_BIAS_ROW : QV_BIAS_ROW + 2, : qv_bias.shape[-1]]
            gain[layer] = small[layer, GAIN_ROW : GAIN_ROW + 2]
            shift[layer] = small[layer, SHIFT_ROW : SHIFT_ROW + 2]


def on_device(
    hidden_in,
    segment_ids,
    out_cotangent,
    qkv_weight,
    qv_bias,
    out_weight,
    out_bias,
    norm_gain,
    norm_bias,
    up_weight,
    up_bias,
    down_weight,
    down_bias,
):
    layers, width, _, local = qkv_weight.shape
    vectors = dict(
        out_bias=out_bias,
        down_bias=down_bias,
        up_bias=up_bias,
        qv_bias=qv_bias,
        norm_gain=norm_gain,
        norm_bias=norm_bias,
    )
    qkv_turned = jnp.transpose(qkv_weight, (0, 2, 3, 1)).reshape(layers, 3 * local, width)
    result, hidden_grad, *sums = run_whole(
        hidden_in, out_cotangent, segment_ids, vectors, qkv_turned, out_weight, up_weight, down_weight
    )
    sums = over_outer_groups(sums)
    small, down, up, qkv, out = sums
    shape = jax.ShapeDtypeStruct
    outs = [
        shape(result.shape, BF16),
        shape(hidden_grad.shape, F32),
        shape(qkv.shape, F32),
        shape(qv_bias.shape, F32),
        shape(out.shape, F32),
        shape(out_bias.shape, F32),
        shape(norm_gain.shape, F32),
        shape(norm_bias.shape, F32),
        shape(up.shape, F32),
        shape(up_bias.shape, F32),
        shape(down.shape, F32),
        shape(down_bias.shape, F32),
    ]
    cuts = 3

    def whole(array):
        return pl.BlockSpec(array.shape, lambda layer, cut, zeros=(0,) * len(array.shape): zeros)

    def piece(array):
        return pl.BlockSpec((1, array.shape[1] // cuts, array.shape[2]), lambda layer, cut: (layer, cut, 0))

    inputs = (result, hidden_grad, small, down, up, qkv, out)
    done = pl.pallas_call(
        widen_kernel,
        grid=(layers, cuts),
        out_shape=outs,
        in_specs=[whole(array) for array in inputs[:3]] + [piece(array) for array in inputs[3:]],
        out_specs=[piece(array) if at in (2, 4, 8, 10) else whole(array) for at, array in enumerate(outs)],
        compiler_params=pltpu.CompilerParams(vmem_limit_bytes=62 << 20),
    )(*inputs)
    done = list(done)
    done[2] = jnp.transpose(done[2].reshape(layers, 3, local, width), (0, 3, 1, 2))
    return tuple(done)


def solution(mesh):
    placed = (
        P(("dp", "tensor"), None),
        P("dp", None),
        P(("dp", "tensor"), None),
        P(None, None, None, "tensor"),
        P(None, None, "tensor"),
        P(None, "tensor", None),
        P(),
        P(),
        P(),
        P(None, None, "tensor"),
        P(None, "tensor"),
        P(None, "tensor", None),
        P(),
    )
    return jax.shard_map(
        on_device,
        mesh=mesh,
        in_specs=placed,
        out_specs=(
            P(("dp", "tensor"), None),
            P(("dp", "tensor"), None),
            P(None, None, None, "tensor"),
            P(None, None, "tensor"),
            P(None, "tensor", None),
            P(),
            P(),
            P(),
            P(None, None, "tensor"),
            P(None, "tensor"),
            P(None, "tensor", None),
            P(),
        ),
        check_vma=False,
    )
```

```python
import functools
from types import SimpleNamespace

import jax
import jax.numpy as jnp
from jax import lax
from jax.experimental import pallas as pl
from jax.experimental.pallas import tpu as pltpu
from jax.sharding import PartitionSpec as P

HEAD = 64
norm_eps = 1e-05
MESH = pl.DeviceIdType.MESH
Y_SIZE = 2
Z_SIZE = 4
GROUP = Y_SIZE * Z_SIZE
F32 = jnp.float32
BF16 = jnp.bfloat16


class Place:
    def __init__(self):
        self.dp = lax.axis_index("dp")
        self.t = lax.axis_index("tensor")
        inner = lax.rem(self.dp, GROUP)
        base = self.dp - inner
        self.y = lax.rem(inner, Y_SIZE)
        self.z = inner // Y_SIZE
        z_pair = self.z + 1 - 2 * lax.rem(self.z, 2)
        z_mid = Z_SIZE - 1 - self.z
        self.is_end = jnp.logical_or(self.z == 0, self.z == Z_SIZE - 1)
        self.is_inner = jnp.logical_not(self.is_end)
        self.core = (self.dp, self.t + 1 - 2 * lax.rem(self.t, 2))
        self.over = (self.dp, lax.rem(self.t + 2, 4))
        self.diagonal = (self.dp, 3 - self.t)
        self.y_pair = (base + self.z * Y_SIZE + 1 - self.y, self.t)
        self.z_pair = (base + z_pair * Y_SIZE + self.y, self.t)
        self.z_right = (base + jnp.minimum(self.z + 1, Z_SIZE - 1) * Y_SIZE + self.y, self.t)
        self.z_left = (base + jnp.maximum(self.z - 1, 0) * Y_SIZE + self.y, self.t)
        self.z_mid = (base + z_mid * Y_SIZE + self.y, self.t)


class Links:
    def __init__(self, out_sems, in_sems, first=(0, 0), end=None):
        self.sems = (out_sems, in_sems)
        self.first = first
        self.used = list(first)
        self.end = end or (out_sems.shape[0], in_sems.shape[0])

    def take(self, side, count):
        start = self.used[side]
        self.used[side] += count
        assert self.used[side] <= self.end[side]
        return list(range(start, start + count))

    def outs(self, count):
        return self.take(0, count)

    def ins(self, count):
        return self.take(1, count)

    def keep(self, count):
        first = (self.outs(count)[0], self.ins(count)[0])
        return Links(*self.sems, first, tuple(self.used))

    def restart(self):
        self.used = list(self.first)

    def on(self, src, dst, device, out_at, in_at):
        return pltpu.make_async_remote_copy(
            src_ref=src,
            dst_ref=dst,
            send_sem=self.sems[0].at[out_at],
            recv_sem=self.sems[1].at[in_at],
            device_id=device,
            device_id_type=MESH,
        )

    def copy(self, src, dst, device):
        return self.on(src, dst, device, self.outs(1)[0], self.ins(1)[0])


def greet(devices):
    barrier = pltpu.get_barrier_semaphore()
    for device in devices:
        pl.semaphore_signal(barrier, inc=1, device_id=device, device_id_type=MESH)
    pl.semaphore_wait(barrier, len(devices))


def added(one, two, dtype):
    return (one.astype(F32) + two.astype(F32)).astype(dtype)


def small_item(place, links, mine, steps, landing, result):
    top = pl.ds(0, 8)
    steps[0] = mine[...]
    near = links.copy(steps.at[0, top], landing.at[0, top], place.core)
    near.start()
    yield
    near.wait_recv()
    steps[1] = steps[0]
    steps[1, top] = steps[0, top] + landing[0, top]
    over = links.copy(steps.at[1, top], landing.at[1, top], place.over)
    over.start()
    yield
    over.wait_recv()
    steps[2] = steps[1]
    steps[2, top] = steps[1, top] + landing[1, top]
    across = links.copy(steps.at[2], landing.at[2], place.y_pair)
    across.start()
    yield
    across.wait_recv()
    steps[3] = steps[2] + landing[2]
    pair_in = links.copy(steps.at[3], landing.at[3], place.z_pair)
    mid = links.copy(steps.at[4], landing.at[4], place.z_mid)
    pair_out = links.copy(result, landing.at[3], place.z_pair)

    @pl.when(place.is_end)
    def _():
        pair_in.start()

    yield

    @pl.when(place.is_inner)
    def _():
        pair_in.wait_recv()
        steps[4] = steps[3] + landing[3]
        mid.start()

    yield

    @pl.when(place.is_inner)
    def _():
        mid.wait_recv()
        result[...] = steps[4] + landing[4]
        pair_out.start()

    yield

    @pl.when(place.is_end)
    def _():
        pair_out.wait_recv()
        result[...] = landing[3]

    yield
    near.wait_send()
    over.wait_send()
    across.wait_send()

    @pl.when(place.is_end)
    def _():
        pair_in.wait_send()

    @pl.when(place.is_inner)
    def _():
        mid.wait_send()
        pair_out.wait_send()


class Turns:
    def __init__(self, schedule):
        self.schedule = schedule
        self.place = 0
        self.items = []

    def add(self, items):
        self.items.extend(items)

    def take(self):
        for at in self.schedule[self.place] if self.place < len(self.schedule) else ():
            if at < len(self.items):
                next(self.items[at], None)
        self.place += 1

    def finish(self):
        self.take()
        running = self.items
        while running:
            running = [item for item in running if next(item, running) is not running]


def over_outer_groups(values):
    size = lax.axis_size("dp")
    if size == GROUP:
        return values
    groups = [[first + GROUP * turn for turn in range(size // GROUP)] for first in range(GROUP)]
    return [lax.psum(value, "dp", axis_index_groups=groups) for value in values]


def gelu_tanh(pre_active):
    return jax.nn.gelu(pre_active, approximate=True)


LANES = 128
SLOT = 256


def product(left, right, contract):
    return lax.dot_general(left, right, ((contract[:1], contract[1:]), ((), ())), preferred_element_type=F32)


def nn(left, right):
    return product(left, right, (1, 0))


def nt(left, right):
    return product(left, right, (1, 1))


def tn(left, right):
    return product(left, right, (0, 0))


class Gather:
    def __init__(self, place, links, rows):
        links.restart()
        half = SLOT // 2
        self.near_copies, self.far_copies, self.pass_copies = [], [], []
        for part in range(2):
            own = pl.ds(part * half, half)
            beside = pl.ds(SLOT + part * half, half)
            over = pl.ds(2 * SLOT + part * half, half)
            diagonal = pl.ds(3 * SLOT + part * half, half)
            self.near_copies.append(links.copy(rows.at[own], rows.at[beside], place.core))
            self.far_copies.append(links.copy(rows.at[own], rows.at[over], place.over))
            self.pass_copies.append(links.copy(rows.at[over], rows.at[diagonal], place.core))

    def send(self, part):
        self.far_copies[part].start()
        self.near_copies[part].start()

    def near(self):
        for copy in self.near_copies:
            copy.wait_recv()

    def far(self, part):
        self.far_copies[part].wait_recv()
        self.pass_copies[part].start()

    def diagonal(self, part):
        self.pass_copies[part].wait_recv()

    def drain(self):
        for copy in self.near_copies + self.far_copies + self.pass_copies:
            copy.wait_send()


class Scatter:
    def __init__(self, place, links, rooms):
        links.restart()
        self.core_out, self.core_in, self.far_out, self.far_in, self.near_out, self.near_in = rooms
        self.core_copies = [
            links.copy(self.core_out.at[part], self.core_in.at[part], place.core) for part in range(2)
        ]
        self.far_copies = [
            links.copy(self.far_out.at[part], self.far_in.at[part], place.over) for part in range(2)
        ]
        self.near_copies = [
            links.copy(self.near_out.at[part], self.near_in.at[part], place.core) for part in range(2)
        ]

    def beside(self, term):
        half = SLOT // 2
        for part in range(2):
            self.near_out[part] = term[part * half : (part + 1) * half].astype(BF16)
            self.near_copies[part].start()

    def diagonal(self, part, term):
        self.core_out[part] = term.astype(BF16)
        self.core_copies[part].start()

    def over(self, part, term):
        self.core_copies[part].wait_recv()
        self.far_out[part] = (term + self.core_in[part].astype(F32)).astype(BF16)
        self.far_copies[part].start()

    def arrived(self, part):
        self.near_copies[part].wait_recv()
        self.far_copies[part].wait_recv()
        return self.near_in[part].astype(F32) + self.far_in[part].astype(F32)

    def drain(self):
        for copy in self.core_copies + self.far_copies + self.near_copies:
            copy.wait_send()


def lane_masks():
    lane = lax.broadcasted_iota(jnp.int32, (1, LANES), 1)
    first = jnp.where(lane < HEAD, 1.0, 0.0).astype(BF16)
    return first, (1.0 - first.astype(F32)).astype(BF16)


def head_parts(tile, masks):
    parts = []
    width = tile.shape[-1]
    for first in range(0, width, LANES):
        piece = tile[:, first : min(first + LANES, width)]
        if piece.shape[-1] == HEAD:
            parts.append([piece])
        else:
            parts.append([piece * masks[0], piece * masks[1]])
    return parts


def whole_parts(tile):
    width = tile.shape[-1]
    return [tile[:, first : min(first + LANES, width)] for first in range(0, width, LANES)]


def allowed_rows(seg_cols, seg_rows, slot):
    return seg_cols[slot] == seg_rows[slot : slot + 1, :]


def attention_forward(query, keys, values, allowed):
    masks = lane_masks()
    outs = []
    for query_part, key_heads, value_heads in zip(
        whole_parts(query), head_parts(keys, masks), head_parts(values, masks)
    ):
        total = None
        for key_head, value_head in zip(key_heads, value_heads):
            scores = jnp.where(allowed, nt(query_part, key_head), -1000000000.0)
            grown = jnp.exp(scores - jnp.max(scores, axis=-1, keepdims=True))
            probs = grown * (1.0 / jnp.sum(grown, axis=-1, keepdims=True))
            term = nn(probs.astype(BF16), value_head)
            total = term if total is None else total + term
        outs.append(total.astype(BF16))
    return outs


def norm_rows(total, gain, shift):
    average = jnp.mean(total, axis=-1, keepdims=True)
    centered = total - average
    inverse = lax.rsqrt(jnp.mean(centered * centered, axis=-1, keepdims=True) + norm_eps)
    scaled = centered * inverse
    return scaled * gain + shift, scaled, inverse


OUT_BIAS, DOWN_BIAS, UP_BIAS, Q_BIAS, V_BIAS, GAIN, SHIFT = 0, 1, 2, 3, 4, 5, 7


def gelu_slope(raised):
    curve = (2.0 / jnp.pi) ** 0.5
    square = raised * raised
    bent = jnp.tanh(curve * raised * (1.0 + 0.044715 * square))
    return 0.5 * (1.0 + bent) + (0.5 * curve) * raised * (1.0 - bent * bent) * (1.0 + 0.134145 * square)


def attention_backward(query, keys, values, context_grad, allowed):
    masks = lane_masks()
    query_out, key_out, value_out = [], [], []
    for query_part, query_heads, key_heads, value_heads, grad_part, grad_heads in zip(
        whole_parts(query),
        head_parts(query, masks),
        head_parts(keys, masks),
        head_parts(values, masks),
        whole_parts(context_grad),
        head_parts(context_grad, masks),
    ):
        totals = None
        for query_head, key_head, value_head, grad_head in zip(
            query_heads, key_heads, value_heads, grad_heads
        ):
            scores = jnp.where(allowed, nt(key_head, query_part), -1000000000.0)
            grown = jnp.exp(scores - jnp.max(scores, axis=0, keepdims=True))
            probs = grown * (1.0 / jnp.sum(grown, axis=0, keepdims=True))
            probs_grad = nt(value_head, grad_part)
            shared = jnp.sum(probs_grad * probs, axis=0, keepdims=True)
            scores_grad = (probs * (probs_grad - shared)).astype(BF16)
            terms = (
                tn(scores_grad, key_head) * HEAD ** (-0.5),
                nn(scores_grad, query_head),
                nn(probs.astype(BF16), grad_head),
            )
            totals = terms if totals is None else tuple(map(jnp.add, totals, terms))
        query_out.append(totals[0].astype(BF16))
        key_out.append(totals[1].astype(BF16))
        value_out.append(totals[2].astype(BF16))
    return query_out, key_out, value_out


def norm_rows_backward(incoming, scaled, inverse, gain):
    inner = incoming * gain
    return inverse * (
        inner
        - jnp.mean(inner, axis=-1, keepdims=True)
        - scaled * jnp.mean(inner * scaled, axis=-1, keepdims=True)
    )


def column_sum(rows):
    return jnp.sum(rows.astype(F32), axis=0, keepdims=True)


def pair_item(place, links, mine, landing, result, local_sem, start, size):
    from_y, from_z, from_mid = landing
    half = size // 2
    here = pl.ds(pl.multiple_of(start + place.y * half, 16), half)
    there = pl.ds(pl.multiple_of(start + (1 - place.y) * half, 16), half)
    first, second = links.outs(2)
    over_y, pair, middle, back = links.ins(4)
    y_out = links.on(mine.at[there], from_y, place.y_pair, first, over_y)
    pair_in = links.on(mine.at[here], from_z, place.z_pair, second, pair)
    mid = links.on(mine.at[here], from_mid, place.z_mid, second, middle)
    pair_out = links.on(from_mid, from_z, place.z_pair, second, pair)
    back_inner = links.on(from_mid, result.at[here], place.y_pair, first, back)
    back_end = links.on(from_z, result.at[here], place.y_pair, first, back)
    keep_inner = pltpu.make_async_copy(from_mid, result.at[here], local_sem)
    keep_end = pltpu.make_async_copy(from_z, result.at[here], local_sem)
    y_out.start()
    yield
    y_out.wait_recv()
    y_out.wait_send()
    mine[here] = added(mine[here], from_y[...], BF16)

    @pl.when(place.is_end)
    def _():
        pair_in.start()

    yield

    @pl.when(place.is_inner)
    def _():
        pair_in.wait_recv()
        mine[here] = added(mine[here], from_z[...], BF16)
        mid.start()

    yield

    @pl.when(place.is_inner)
    def _():
        mid.wait_recv()
        mid.wait_send()
        from_mid[...] = added(mine[here], from_mid[...], BF16)
        pair_out.start()
        back_inner.start()
        keep_inner.start()

    yield

    @pl.when(place.is_end)
    def _():
        pair_out.wait_recv()
        back_end.start()
        keep_end.start()

    yield
    back_inner.wait_recv()
    yield

    @pl.when(place.is_end)
    def _():
        pair_in.wait_send()
        back_end.wait_send()
        keep_end.wait()

    @pl.when(place.is_inner)
    def _():
        pair_out.wait_send()
        back_inner.wait_send()
        keep_inner.wait()


def line_item(place, links, mine, landing, result, local_sem, start, size):
    from_left, from_right, from_y = landing
    quarter = size // Z_SIZE
    last = Z_SIZE - 1
    block = lambda at: pl.ds(start + at * quarter, quarter)
    own = pl.ds(pl.multiple_of(start + place.z * quarter, 16), quarter)
    send, receive, back = links.outs(last), links.ins(2 * last - 1), links.ins(last)
    right = {
        q: links.on(mine.at[block(q)], from_left.at[q - 1], place.z_right, send[q - 1], receive[q - 1])
        for q in range(1, Z_SIZE)
    }
    left = {
        q: links.on(
            mine.at[block(q)], from_right.at[q], place.z_left, send[q],
            receive[last + q] if q < last - 1 else receive[0],
        )
        for q in range(last)
    }
    across = links.copy(mine.at[own], from_y, place.y_pair)
    go_right, go_left = [], []
    for distance in range(1, Z_SIZE):
        for copies, device, sign in ((go_right, place.z_right, 1), (go_left, place.z_left, -1)):
            at = place.z - sign * (distance - 1)
            rows = pl.ds(pl.multiple_of(start + jnp.clip(at, 0, last) * quarter, 16), quarter)
            source = from_y if distance == 1 else result.at[rows]
            arrival = back[distance - 1] if sign > 0 else back[last - distance]
            copies.append(links.on(source, result.at[rows], device, send[0 if sign > 0 else 1], arrival))
    keep = pltpu.make_async_copy(from_y, result.at[own], local_sem)

    @pl.when(place.z == 0)
    def _():
        for q in range(last, 0, -1):
            right[q].start()

    @pl.when(place.z == last)
    def _():
        for q in range(last):
            left[q].start()

    yield
    for step in range(1, Z_SIZE):

        @pl.when(place.z == step)
        def _():
            for q in range(last, step - 1, -1):
                right[q].wait_recv()
                mine[block(q)] = added(mine[block(q)], from_left[q - 1], BF16)
                if q > step:
                    right[q].start()

        @pl.when(place.z == last - step)
        def _():
            for q in range(last - step + 1):
                left[q].wait_recv()
                mine[block(q)] = added(mine[block(q)], from_right[q], BF16)
                if q < last - step:
                    left[q].start()

        yield
    across.start()
    for q in range(1, Z_SIZE):

        @pl.when(place.z < q)
        def _():
            right[q].wait_send()

        @pl.when(place.z > last - q)
        def _():
            left[last - q].wait_send()

    yield
    across.wait_recv()
    across.wait_send()
    from_y[...] = added(mine[own], from_y[...], BF16)
    keep.start()

    @pl.when(place.z < last)
    def _():
        go_right[0].start()

    @pl.when(place.z > 0)
    def _():
        go_left[0].start()

    yield
    for distance in range(1, Z_SIZE):

        @pl.when(place.z >= distance)
        def _():
            go_right[distance - 1].wait_recv()

        if distance < last:

            @pl.when(jnp.logical_and(place.z >= distance, place.z < last))
            def _():
                go_right[distance - 1].wait_send()
                go_right[distance].start()

        @pl.when(place.z <= last - distance)
        def _():
            go_left[distance - 1].wait_recv()

        if distance < last:

            @pl.when(jnp.logical_and(place.z <= last - distance, place.z > 0))
            def _():
                go_left[distance - 1].wait_send()
                go_left[distance].start()

        yield
    keep.wait()

    @pl.when(place.z < last)
    def _():
        go_right[0].wait_send()

    @pl.when(place.z > 0)
    def _():
        go_left[0].wait_send()


ITEM_ROWS = dict(
    down=((96, False), (96, False), (192, False), (192, True), (192, False)),
    up=((96, False), (96, False), (192, False), (192, True), (192, False)),
    qkv=((128, True), (256, False), (192, False)),
    out=((128, True), (64, False)),
)
SCHEDULE = (
    (),
    (),
    (),
    (),
    (),
    (0, 1, 2, 3, 4),
    (5, 6, 7, 8, 9),
    (0, 1, 3),
    (2,),
    (0, 1, 3, 4, 5, 6, 8),
    (0, 1, 3, 3, 2, 4, 7, 9),
    (0, 1, 2, 3, 5, 6, 7, 8),
    (4, 9, 10, 11, 12, 13, 14, 15),
    (3, 0, 1, 2, 5, 6, 8, 8, 10, 15),
    (4, 7, 13, 15, 11, 9),
    (3, 5, 12, 10, 14, 2, 6),
    (11, 13),
    (4, 8, 7, 12, 14),
    (3, 5, 6, 9, 10, 10, 11, 13, 13, 15),
    (8, 7, 16, 17, 18, 19, 20),
    (15, 12, 14, 21, 22, 24, 9, 10, 11),
    (8, 15, 19, 13, 23),
    (12, 14, 16, 17, 24, 10, 19, 18, 25),
    (8, 15, 13, 16, 17, 24, 20, 10),
    (19, 19, 13, 18, 16),
    (10, 13, 11, 17, 24, 24, 20, 21, 22, 18),
    (16, 21, 22, 20, 23, 26, 27, 28, 29),
    (12, 14, 17, 18, 21, 23, 22, 25, 19, 30),
    (26, 31, 24, 20, 16, 21, 23, 29, 31, 22, 25, 26, 19, 31, 24, 29, 27, 25, 27, 28, 23, 17, 26, 26, 19, 18, 24, 29, 29, 28, 30, 30, 27, 20, 25, 21, 19, 22, 24, 31, 28, 30, 31, 23, 26, 29, 31, 27, 25, 28, 30, 26, 29, 31, 27, 26, 29, 28, 26, 29, 30),
)


def item_plan(name, rows):
    sizes = ITEM_ROWS[name]
    if sum(size for size, _ in sizes) != rows:
        sizes = ((rows, False),)
    plan, first = [], 0
    for size, line in sizes:
        plan.append((first, size, line))
        first += size
    return plan


OUT_COPIES, IN_COPIES = 178, 268
SHARE_ROWS = dict(qkv=(576,), out=(192,), up=(512, 256), down=(384, 192))
SHARES = (
    (),
    (0, 1),
    (),
    (4, 5),
    (),
    (0, 1, 0, 1),
    (2, 3),
    (4, 5, 0, 1),
    (),
    (),
    (4, 5),
    (2,),
    (3, 0, 1, 4, 5),
    (),
    (),
    (2, 3),
    (4,),
    (),
    (6,),
    (0, 5, 1),
    (2, 1, 3),
    (0, 2, 4, 3),
    (),
    (5, 4),
    (5,),
    (2,),
    (6, 3),
    (2, 6),
    (3,),
)


def share_item(place, links, mine, near, over, diagonal):
    rows, columns = mine.shape
    tall, broad, end = rows // Z_SIZE, columns // Y_SIZE, Z_SIZE - 1

    def cut(array, at):
        first = pl.multiple_of(jnp.clip(at, 0, end) * tall, 16)
        return array.at[pl.ds(first, tall), pl.ds(pl.multiple_of(place.y * broad, LANES), broad)]

    beside = links.copy(mine, near, place.core)
    across = links.copy(cut(mine, place.z), cut(over, place.z), place.over)
    chains, pair_sends = links.outs(2), links.outs(Z_SIZE)
    hops, pair_hops = links.ins(end), links.ins(Z_SIZE)
    flows = []
    for sign, device in ((1, place.z_right), (-1, place.z_left)):
        along, pair = [], []
        for distance in range(Z_SIZE):
            block = cut(over, place.z - sign * distance)
            at = distance - 1 if sign > 0 else end - distance
            if distance < end:
                hop = hops[distance if sign > 0 else end - 1 - distance]
                along.append(links.on(block, block, device, chains[sign > 0], hop))
            if distance:
                pair.append(links.on(block, block, place.y_pair, pair_sends[at], pair_hops[at]))
            else:
                pair.append(links.on(block, block, place.y_pair, pair_sends[end], pair_hops[end]))
        flows.append((along, pair))
    (go_right, pair_right), (go_left, pair_left) = flows
    passing = links.copy(over, diagonal, place.core)
    beside.start()
    across.start()
    yield
    for distance in range(Z_SIZE):
        if distance == 0:
            across.wait_recv()
            pair_right[0].start()

        for z, along, pair in ((place.z, go_right, pair_right), (end - place.z, go_left, pair_left)):

            @pl.when(z >= distance)
            def _():
                if distance:
                    along[distance - 1].wait_recv()
                    pair[distance].start()

            if distance < end:

                @pl.when(jnp.logical_and(z >= distance, z < end))
                def _():
                    if distance:
                        along[distance - 1].wait_send()
                    along[distance].start()

        yield
    pair_right[0].wait_recv()
    for z, pair in ((place.z, pair_right), (end - place.z, pair_left)):
        for distance in range(1, Z_SIZE):

            @pl.when(z >= distance)
            def _():
                pair[distance].wait_recv()

    passing.start()
    yield
    passing.wait_recv()
    beside.wait_recv()
    yield
    beside.wait_send()
    across.wait_send()
    passing.wait_send()
    pair_right[0].wait_send()
    for z, along, pair in ((place.z, go_right, pair_right), (end - place.z, go_left, pair_left)):
        for distance in range(Z_SIZE):
            if distance:

                @pl.when(z >= distance)
                def _():
                    pair[distance].wait_send()


        @pl.when(z < end)
        def _():
            along[0].wait_send()


def direct_item(place, links, mine, near, over, diagonal):
    beside = links.copy(mine, near, place.core)
    across = links.copy(mine, over, place.over)
    passing = links.copy(over, diagonal, place.core)
    beside.start()
    across.start()
    yield
    across.wait_recv()
    passing.start()
    yield
    passing.wait_recv()
    beside.wait_recv()
    yield
    for copy in (beside, across, passing):
        copy.wait_send()


def land_name(*place):
    return "_".join(map(str, place))


def item_rooms(name, rows, width):
    rooms = []
    for _, size, line in item_plan(name, rows):
        if line:
            rooms += [pltpu.VMEM((Z_SIZE - 1, size // Z_SIZE, width), BF16)] * 2
            rooms += [pltpu.VMEM((size // Z_SIZE, width), BF16)]
        else:
            rooms += [pltpu.VMEM((size // 2, width), BF16)] * 3
    return rooms


GAIN_ROW, SHIFT_ROW, OUT_BIAS_ROW, DOWN_BIAS_ROW, UP_BIAS_ROW, QV_BIAS_ROW = 0, 2, 4, 5, 8, 9
PARKED = tuple(
    dict(
        full_in=0, query=0, keys=0, values=0, context=0, active=0, scaled=0, inverse=0
    )
)


def whole_kernel(names, *refs):
    place = Place()
    table = dict(zip(names, refs))
    ref = SimpleNamespace(**table)
    links = Links(ref.out_sems, ref.in_sems)
    turning, middle, entering, summing = (links.keep(6) for _ in range(4))
    small, state = ref.small, ref.state
    full_in, query, keys, values, context = (table[name] for name in PARKED[:5])
    active, scaled, inverse = (table[name] for name in PARKED[5:])
    pre = ref.pre
    out_own, out_got = ref.out_own, ref.out_got
    own_part, far_part, context_in = ref.own_part, ref.far_part, ref.context_in
    full_down, pre_grad, full_out = ref.full_down, ref.pre_grad, ref.full_out
    mixed_grads = [ref.query_grad, ref.key_grad, ref.value_grad]
    layers = small.shape[0]
    local = query.shape[-1]
    half = SLOT // 2
    halves = [pl.ds(part * half, half) for part in range(2)]
    thirds = [pl.ds(part * local, local) for part in range(3)]
    slots = [pl.ds(slot * SLOT, SLOT) for slot in range(4)]
    far_pieces = [
        [pl.ds(2 * SLOT + part * half, half), pl.ds(3 * SLOT + part * half, half)] for part in range(2)
    ]

    def vector(layer, row, width=small.shape[-1]):
        return small[layer, row : row + 1, :width]

    loads = {}
    at = 0
    for layer in range(layers):
        for name, target in (
            ("qkv", ref.qkv.at[layer]),
            ("out", out_own.at[layer]),
            ("up", ref.up.at[layer]),
            ("down", ref.down.at[layer]),
        ):
            loads[layer, name] = pltpu.make_async_copy(
                table[name + "_in"].at[layer], target, ref.load_sems.at[at]
            )
            loads[layer, name].start()
            at += 1
    cotangent = pltpu.make_async_copy(ref.cotangent_in, ref.cotangent, ref.load_sems.at[at])
    cotangent.start()
    for layer in range(layers):
        for source, row in (
            (ref.out_bias_in, OUT_BIAS),
            (ref.down_bias_in, DOWN_BIAS),
            (ref.up_bias_in, UP_BIAS),
            (ref.qv_bias_in, Q_BIAS),
            (ref.norm_gain_in, GAIN),
            (ref.norm_bias_in, SHIFT),
        ):
            rows = source[layer].astype(F32).reshape(-1, source.shape[-1])
            small[layer, row : row + rows.shape[0], : rows.shape[1]] = rows
    for slot, index in enumerate((place.t, place.core[1], place.over[1], place.diagonal[1])):
        row = ref.segments[pl.ds(index, 1), :].astype(F32)
        ref.seg_rows[slot : slot + 1] = row
        ref.seg_cols[slot] = jnp.transpose(jnp.broadcast_to(row, ref.seg_cols.shape[1:]))
    greet((place.core, place.over, place.diagonal, place.y_pair, place.z_pair, place.z_mid))
    rooms = (ref.core_out, ref.core_in, ref.far_out, ref.far_in, ref.near_out, ref.near_in)
    parks = {}

    def park(layer, these):
        for name in these:
            at = PARKED.index(name)
            parks[layer, name] = pltpu.make_async_copy(
                table[name], table["park_" + name].at[layer], ref.park_sems.at[layer, 0, at]
            )
            parks[layer, name].start()

    def parked(layer, these):
        for name in these:
            if (layer, name) in parks:
                parks.pop((layer, name)).wait()

    def restore(layer, these):
        if layer < 0:
            return
        for name in these:
            at = PARKED.index(name)
            parks[layer, name] = pltpu.make_async_copy(
                table["park_" + name].at[layer], table[name], ref.park_sems.at[layer, 1, at]
            )
            parks[layer, name].start()

    def attend(layer, slot):
        qkv_weight = ref.qkv.at[layer]
        rows = slots[slot]
        rows_in = full_in[rows]
        mixed = [nt(rows_in, qkv_weight[piece]) for piece in thirds]
        query[rows] = ((mixed[0] + vector(layer, Q_BIAS, local)) * HEAD ** (-0.5)).astype(BF16)
        keys[rows] = mixed[1].astype(BF16)
        values[rows] = (mixed[2] + vector(layer, V_BIAS, local)).astype(BF16)
        outs = attention_forward(
            query[rows], keys[rows], values[rows],
            allowed_rows(ref.seg_cols, ref.seg_rows, slot),
        )
        first = 0
        for out in outs:
            context[rows, first : first + out.shape[-1]] = out
            first += out.shape[-1]

    state[...] = ref.hidden[...].astype(F32)
    gather = Gather(place, turning, full_in)
    for part in range(2):
        full_in[halves[part]] = ref.hidden[halves[part]]
        gather.send(part)
    ref.small_grad[...] = jnp.zeros_like(ref.small_grad)
    last = layers - 1
    peers = [
        links.copy(small.at[last], ref.peer_small.at[at], device)
        for at, device in enumerate((place.core, place.over, place.diagonal))
    ]
    for copy in peers:
        copy.start()
    shares = Turns(SHARES)
    for name in ("qkv", "out", "up", "down"):
        arrays = (
            (out_own if name == "out" else table[name]).at[last],
            table[name + "_grad"].at[0],
            table[name + "_grad"].at[1],
            table[name + "_far"],
        )
        first = 0
        for size in SHARE_ROWS[name]:
            rows = pl.ds(first, size)
            shares.add([share_item(place, links, *[array.at[rows] for array in arrays])])
            first += size
        if first < arrays[0].shape[0]:
            rows = pl.ds(first, arrays[0].shape[0] - first)
            shares.add([direct_item(place, links, *[array.at[rows] for array in arrays])])

    def share_turn():
        shares.take()

    for layer in range(last):
        up_weight, down_weight, full_mid = ref.up.at[layer], ref.down.at[layer], ref.full_mid.at[layer]

        sends = [
            links.copy(context.at[slots[slot]], context_in.at[slot - 1], device)
            for slot, device in ((1, place.core), (2, place.over), (3, place.diagonal))
        ]
        out_near = links.copy(out_own.at[layer], out_got.at[0], place.core)
        out_far = links.copy(out_own.at[layer], out_got.at[1], place.over)
        out_pass = links.copy(out_got.at[1], out_got.at[2], place.core)
        loads[layer, "out"].wait()
        out_near.start()
        loads[layer, "qkv"].wait()
        parked(layer - 1, PARKED)
        attend(layer, 0)
        gather.near()
        attend(layer, 1)
        sends[0].start()
        for name in ("qkv", "out", "up", "down"):
            if (last, name) in loads:
                loads.pop((last, name)).wait()
        share_turn()
        gather.far(0)
        share_turn()
        share_turn()
        gather.far(1)
        out_far.start()
        share_turn()
        attend(layer, 2)
        sends[1].start()
        share_turn()
        share_turn()
        out_far.wait_recv()
        out_pass.start()
        gather.diagonal(0)
        gather.diagonal(1)
        attend(layer, 3)
        sends[2].start()
        share_turn()
        own_part[...] = nn(context[slots[0]], out_own[layer])
        out_near.wait_recv()
        sends[0].wait_recv()
        own_part[...] += nn(context_in[0], out_got[0])
        out_pass.wait_recv()
        share_turn()
        sends[1].wait_recv()
        share_turn()
        sends[2].wait_recv()
        gather.drain()
        for copy in sends + [out_near, out_far, out_pass]:
            copy.wait_send()
        park(layer, PARKED[:5])
        gather = Gather(place, turning, full_mid)
        for part in range(2):
            rows = halves[part]
            total = (
                own_part[rows]
                + nn(context_in[1, rows], out_got[1])
                + nn(context_in[2, rows], out_got[2])
                + state[rows]
                + vector(layer, OUT_BIAS)
            )
            normed, scaled_part, inverse_part = norm_rows(total, vector(layer, GAIN), vector(layer, SHIFT))
            full_mid[rows] = normed.astype(BF16)
            gather.send(part)
            state[rows] = normed
            scaled[0, rows] = scaled_part
            inverse[0, rows] = jnp.broadcast_to(inverse_part, (half, LANES))
        share_turn()
        loads[layer, "up"].wait()
        loads[layer, "down"].wait()
        scatter = Scatter(place, summing, rooms)

        def feed(pieces):
            rows_in = jnp.concatenate([full_mid[piece] for piece in pieces])
            size = rows_in.shape[0] // len(pieces)
            for first in range(0, up_weight.shape[-1], SLOT):
                columns = slice(first, first + SLOT)
                raised = nn(rows_in, up_weight[:, columns]) + small[layer, UP_BIAS : UP_BIAS + 1, columns]
                shaped = gelu_tanh(raised).astype(BF16)
                for at, piece in enumerate(pieces):
                    pre[piece, columns] = raised[at * size : (at + 1) * size]
                    active[piece, columns] = shaped[at * size : (at + 1) * size]
            return nn(jnp.concatenate([active[piece] for piece in pieces]), down_weight[...])

        share_turn()
        own_part[...] = feed([slots[0]])
        share_turn()
        gather.near()
        parked(layer, PARKED[:5])
        scatter.beside(feed([slots[1]]))
        for part in range(2):
            share_turn()
            gather.far(part)
            share_turn()
            gather.diagonal(part)
            far_part[...] = feed(far_pieces[part])
            scatter.diagonal(part, far_part[half:])
            scatter.over(part, far_part[:half])
            share_turn()
            share_turn()
        gather.drain()
        gather = Gather(place, entering, full_in)
        for part in range(2):
            rows = halves[part]
            share_turn()
            total = state[rows] + own_part[rows] + scatter.arrived(part) + vector(layer, DOWN_BIAS)
            normed, scaled_part, inverse_part = norm_rows(
                total, vector(layer, GAIN + 1), vector(layer, SHIFT + 1)
            )
            state[rows] = normed
            full_in[rows] = normed.astype(BF16)
            gather.send(part)
            scaled[1, rows] = scaled_part
            inverse[1, rows] = jnp.broadcast_to(inverse_part, (half, LANES))
        scatter.drain()
        park(layer, PARKED[5:])

    vectors = [small.at[last]] + [ref.peer_small.at[at] for at in range(3)]
    for copy in peers:
        copy.wait_recv()

    def quarters(name):
        own = out_own if name == "out" else table[name]
        return [own.at[last], table[name + "_grad"].at[0], table[name + "_grad"].at[1], table[name + "_far"]]

    gather_in = gather
    share_turn()
    rows_in = full_in[slots[0]]
    allowed = allowed_rows(ref.seg_cols, ref.seg_rows, 0)
    for role, (weight, out_weight, own) in enumerate(zip(quarters("qkv"), quarters("out"), vectors)):
        mixed = [nt(rows_in, weight[piece]) for piece in thirds]
        outs = attention_forward(
            ((mixed[0] + own[Q_BIAS : Q_BIAS + 1, :local]) * HEAD ** (-0.5)).astype(BF16),
            mixed[1].astype(BF16),
            (mixed[2] + own[V_BIAS : V_BIAS + 1, :local]).astype(BF16),
            allowed,
        )
        first = 0
        for out in outs:
            ref.context_own[:, first : first + out.shape[-1]] = out
            first += out.shape[-1]
        term = nn(ref.context_own[...], out_weight[...])
        own_part[...] = term if role == 0 else own_part[...] + term
        share_turn()
    parked(last - 1, PARKED)
    full_mid = ref.full_mid.at[last]
    gather_mid = Gather(place, middle, full_mid)
    for part in range(2):
        rows = halves[part]
        total = own_part[rows] + state[rows] + vector(last, OUT_BIAS)
        normed, scaled_part, inverse_part = norm_rows(total, vector(last, GAIN), vector(last, SHIFT))
        full_mid[rows] = normed.astype(BF16)
        gather_mid.send(part)
        state[rows] = normed
        scaled[0, rows] = scaled_part
        inverse[0, rows] = jnp.broadcast_to(inverse_part, (half, LANES))
    share_turn()
    share_turn()
    for role, (weight, down_weight, own) in enumerate(zip(quarters("up"), quarters("down"), vectors)):
        raised = nn(full_mid[slots[0]], weight[...]) + own[UP_BIAS : UP_BIAS + 1]
        term = nn(gelu_tanh(raised).astype(BF16), down_weight[...])
        own_part[...] = term if role == 0 else own_part[...] + term
    for part in range(2):
        rows = halves[part]
        total = state[rows] + own_part[rows] + vector(last, DOWN_BIAS)
        normed, scaled_part, inverse_part = norm_rows(
            total, vector(last, GAIN + 1), vector(last, SHIFT + 1)
        )
        ref.result[rows] = normed.astype(BF16)
        scaled[1, rows] = scaled_part
        inverse[1, rows] = jnp.broadcast_to(inverse_part, (half, LANES))
    shares.finish()

    turns = Turns(SCHEDULE)
    item_count = 0

    def sum_items(layer, name):
        nonlocal item_count
        mine = table[name + "_grad"].at[layer]
        items = []
        for at, (start, size, line) in enumerate(item_plan(name, mine.shape[0])):
            landing = tuple(table[land_name(name, layer, at, room)] for room in range(3))
            make = line_item if line else pair_item
            items.append(
                make(
                    place, links, mine, landing, table[name + "_sum"].at[layer],
                    ref.item_sems.at[item_count], start, size,
                )
            )
            item_count += 1
        return items

    cotangent.wait()
    state[...] = ref.cotangent[...].astype(F32)
    for layer in reversed(range(layers)):
        qkv_weight, up_weight, down_weight = ref.qkv.at[layer], ref.up.at[layer], ref.down.at[layer]
        full_mid = ref.full_mid.at[layer]
        small_grad = ref.small_grad.at[layer]
        again = layer == last

        def norm_step(at, part, bias_row, target):
            rows = halves[part]
            incoming, scaled_part = state[rows], scaled[at, rows]
            small_grad[GAIN_ROW + at : GAIN_ROW + at + 1] += column_sum(incoming * scaled_part)
            small_grad[SHIFT_ROW + at : SHIFT_ROW + at + 1] += column_sum(incoming)
            total = norm_rows_backward(incoming, scaled_part, inverse[at, rows][:, :1], vector(layer, GAIN + at))
            state[rows] = total
            low = total.astype(BF16)
            target[rows] = low
            gather.send(part)
            small_grad[bias_row : bias_row + 1] += column_sum(low)

        parked(layer, PARKED[6:])
        gather = Gather(place, turning, full_down)
        scatter = Scatter(place, summing, rooms)
        for part in range(2):
            norm_step(1, part, DOWN_BIAS_ROW, full_down)
        turns.take()
        parked(layer, PARKED)

        def feed_back(pieces):
            rows_in = jnp.concatenate([full_down[piece] for piece in pieces])
            mid_in = jnp.concatenate([full_mid[piece] for piece in pieces])
            size = rows_in.shape[0] // len(pieces)
            for first in range(0, up_weight.shape[-1], SLOT):
                columns = slice(first, first + SLOT)
                if again:
                    raised = nn(mid_in, up_weight[:, columns]) + small[layer, UP_BIAS : UP_BIAS + 1, columns]
                    shaped = gelu_tanh(raised).astype(BF16)
                    for at, piece in enumerate(pieces):
                        active[piece, columns] = shaped[at * size : (at + 1) * size]
                else:
                    raised = jnp.concatenate([pre[piece, columns] for piece in pieces])
                low = (nt(rows_in, down_weight[columns]) * gelu_slope(raised)).astype(BF16)
                small_grad[UP_BIAS_ROW : UP_BIAS_ROW + 1, columns] += column_sum(low)
                for at, piece in enumerate(pieces):
                    pre_grad[piece, columns] = low[at * size : (at + 1) * size]
            return nt(jnp.concatenate([pre_grad[piece] for piece in pieces]), up_weight[...])

        own_part[...] = feed_back([slots[0]])
        turns.take()
        if again:
            gather_mid.near()
        gather.near()
        scatter.beside(feed_back([slots[1]]))
        turns.take()
        for part in range(2):
            if again:
                gather_mid.far(part)
            gather.far(part)
            if again:
                gather_mid.diagonal(part)
            gather.diagonal(part)
            far_part[...] = feed_back(far_pieces[part])
            scatter.diagonal(part, far_part[half:])
            scatter.over(part, far_part[:half])
            turns.take()
        gather.drain()
        if again:
            gather_mid.drain()

        def weight_grad(name, left, right, columns=None):
            target = table[name + "_grad"].at[layer]
            for first in range(0, left.shape[-1], SLOT):
                last = min(first + SLOT, left.shape[-1])
                target[first:last] = tn(left[:, first:last], right[...]).astype(BF16)

        weight_grad("down", active, full_down)
        turns.add(sum_items(layer, "down"))
        turns.take()
        weight_grad("up", full_mid, pre_grad)
        turns.add(sum_items(layer, "up"))
        restore(layer - 1, PARKED[5:6])
        turns.take()
        for part in range(2):
            rows = halves[part]
            state[rows] = state[rows] + own_part[rows] + scatter.arrived(part)
        scatter.drain()
        gather = Gather(place, turning, full_out)
        scatter = Scatter(place, summing, rooms)
        for part in range(2):
            norm_step(0, part, OUT_BIAS_ROW, full_out)
        restore(layer - 1, PARKED[6:])
        turns.take()

        def attend_back(slot):
            rows = slots[slot]
            if again:
                attend(layer, slot)
            context_grad = nt(full_out[rows], out_own[layer]).astype(BF16)
            outs = attention_backward(
                query[rows], keys[rows], values[rows], context_grad,
                allowed_rows(ref.seg_cols, ref.seg_rows, slot),
            )
            total = None
            for target, parts, piece in zip(mixed_grads, outs, thirds):
                first = 0
                for out in parts:
                    target[rows, first : first + out.shape[-1]] = out
                    first += out.shape[-1]
                term = nn(target[rows], qkv_weight[piece])
                total = term if total is None else total + term
            return total

        own_part[...] = attend_back(0)
        turns.take()
        if again:
            gather_in.near()
        gather.near()
        scatter.beside(attend_back(1))
        turns.take()
        if again:
            gather_in.far(0)
            gather_in.far(1)
        gather.far(0)
        gather.far(1)
        far_part[...] = attend_back(2)
        turns.take()
        if again:
            gather_in.diagonal(0)
            gather_in.diagonal(1)
            gather_in.drain()
        gather.diagonal(0)
        gather.diagonal(1)
        term = attend_back(3)
        for part in range(2):
            scatter.diagonal(part, term[part * half : (part + 1) * half])
        for part in range(2):
            scatter.over(part, far_part[halves[part]])
        turns.take()
        gather.drain()
        weight_grad("out", context, full_out)
        for target, piece in zip(mixed_grads, thirds):
            ref.qkv_grad[layer, piece] = tn(target[...], full_in[...]).astype(BF16)
        for at, target in enumerate((mixed_grads[0], mixed_grads[2])):
            small_grad[QV_BIAS_ROW + at : QV_BIAS_ROW + at + 1, :local] = column_sum(target[...])
        turns.add(sum_items(layer, "qkv"))
        turns.add(sum_items(layer, "out"))
        turns.add(
            [
                small_item(
                    place, links, small_grad, ref.small_steps.at[layer], ref.small_land.at[layer],
                    ref.small_sum.at[layer],
                )
            ]
        )
        restore(layer - 1, PARKED[:5])
        turns.take()
        for part in range(2):
            rows = halves[part]
            state[rows] = state[rows] + own_part[rows] + scatter.arrived(part)
        scatter.drain()
        turns.take()
    ref.hidden_grad[...] = state[...]
    turns.finish()
    for copy in peers:
        copy.wait_send()


def run_whole(hidden, cotangent, segments, vectors, qkv, out, up, down):
    layers, _, width = qkv.shape
    local, hidden_units = out.shape[1], up.shape[-1]
    rows = hidden.shape[0]
    group, half = 4 * rows, rows // 2
    vmem = pl.BlockSpec(memory_space=pltpu.VMEM)
    anywhere = pl.BlockSpec(memory_space=pl.ANY)
    inputs = dict(
        hidden=(hidden, vmem),
        segments=(segments, vmem),
        cotangent_in=(cotangent, anywhere),
        qkv_in=(qkv, anywhere),
        out_in=(out, anywhere),
        up_in=(up, anywhere),
        down_in=(down, anywhere),
    )
    inputs.update({name + "_in": (array, vmem) for name, array in vectors.items()})
    saved = [
        ((group, width), BF16),
        ((group, local), BF16),
        ((group, local), BF16),
        ((group, local), BF16),
        ((group, local), BF16),
        ((group, hidden_units), BF16),
        ((2, rows, width), F32),
        ((2, rows, LANES), F32),
    ]
    grads = dict(
        down=(hidden_units, width),
        up=(width, hidden_units),
        qkv=(3 * local, width),
        out=(local, width),
    )
    outputs = dict(
        result=((rows, width), BF16, vmem),
        hidden_grad=((rows, width), F32, vmem),
        small_sum=((layers, 16, width), F32, vmem),
    )
    outputs.update({name + "_sum": ((layers,) + shape, BF16, anywhere) for name, shape in grads.items()})
    outputs.update(
        {
            "park_" + name: ((layers - 1,) + shape, dtype, anywhere)
            for name, (shape, dtype) in zip(PARKED, saved)
        }
    )
    scratch = {name: pltpu.VMEM(shape, dtype) for name, (shape, dtype) in zip(PARKED, saved)}
    scratch.update(
        seg_rows=pltpu.VMEM((4, rows), F32),
        seg_cols=pltpu.VMEM((4, rows, rows), F32),
        small=pltpu.VMEM((layers, 16, width), F32),
        cotangent=pltpu.VMEM((rows, width), BF16),
        qkv=pltpu.VMEM(qkv.shape, BF16),
        out_own=pltpu.VMEM(out.shape, BF16),
        out_got=pltpu.VMEM((3,) + out.shape[1:], BF16),
        up=pltpu.VMEM(up.shape, BF16),
        down=pltpu.VMEM(down.shape, BF16),
        full_mid=pltpu.VMEM((layers, group, width), BF16),
        pre=pltpu.VMEM((group, hidden_units), F32),
        context_own=pltpu.VMEM((rows, local), BF16),
        peer_small=pltpu.VMEM((3, 16, width), F32),
        qkv_far=pltpu.VMEM(qkv.shape[1:], BF16),
        out_far=pltpu.VMEM(out.shape[1:], BF16),
        up_far=pltpu.VMEM(up.shape[1:], BF16),
        down_far=pltpu.VMEM(down.shape[1:], BF16),
        context_in=pltpu.VMEM((3, rows, local), BF16),
        own_part=pltpu.VMEM((rows, width), F32),
        far_part=pltpu.VMEM((rows, width), F32),
        state=pltpu.VMEM((rows, width), F32),
        full_down=pltpu.VMEM((group, width), BF16),
        pre_grad=pltpu.VMEM((group, hidden_units), BF16),
        full_out=pltpu.VMEM((group, width), BF16),
        query_grad=pltpu.VMEM((group, local), BF16),
        key_grad=pltpu.VMEM((group, local), BF16),
        value_grad=pltpu.VMEM((group, local), BF16),
        small_grad=pltpu.VMEM((layers, 16, width), F32),
        small_steps=pltpu.VMEM((layers, 5, 16, width), F32),
        small_land=pltpu.VMEM((layers, 5, 16, width), F32),
    )
    room = pltpu.VMEM((2, half, width), BF16)
    scratch.update(core_out=room, core_in=room, far_out=room, far_in=room, near_out=room, near_in=room)
    items = 0
    for name, shape in grads.items():
        scratch[name + "_grad"] = pltpu.VMEM((layers,) + shape, BF16)
        for layer in range(layers):
            items += len(item_plan(name, shape[0]))
            for at, land in enumerate(item_rooms(name, *shape)):
                scratch[land_name(name, layer, at // 3, at % 3)] = land
    scratch.update(
        load_sems=pltpu.SemaphoreType.DMA((4 * layers + 1,)),
        park_sems=pltpu.SemaphoreType.DMA((layers, 2, len(PARKED))),
        item_sems=pltpu.SemaphoreType.DMA((items,)),
        out_sems=pltpu.SemaphoreType.DMA((OUT_COPIES,)),
        in_sems=pltpu.SemaphoreType.DMA((IN_COPIES,)),
    )
    names = [*inputs, *outputs, *scratch]
    done = pl.pallas_call(
        functools.partial(whole_kernel, names),
        out_shape=[jax.ShapeDtypeStruct(shape, dtype) for shape, dtype, _ in outputs.values()],
        in_specs=[spec for _, spec in inputs.values()],
        out_specs=[spec for _, _, spec in outputs.values()],
        scratch_shapes=list(scratch.values()),
        compiler_params=pltpu.CompilerParams(
            collective_id=0, has_side_effects=True, vmem_limit_bytes=62 << 20
        ),
    )(*[array for array, _ in inputs.values()])
    return done[: 3 + len(grads)]


def widen_kernel(result_in, hidden_in, small, down_in, up_in, qkv_in, out_in, *outs):
    result, hidden, qkv, qv_bias, out, out_bias, gain, shift, up, up_bias, down, down_bias = outs
    for source, target in ((down_in, down), (up_in, up), (qkv_in, qkv), (out_in, out)):
        target[...] = source[...].astype(F32)

    @pl.when(jnp.logical_and(pl.program_id(0) == 0, pl.program_id(1) == 0))
    def _():
        result[...] = result_in[...]
        hidden[...] = hidden_in[...]
        for layer in range(small.shape[0]):
            here = pl.ds(layer, 1)
            out_bias[here] = small[layer, OUT_BIAS_ROW : OUT_BIAS_ROW + 1]
            down_bias[here] = small[layer, DOWN_BIAS_ROW : DOWN_BIAS_ROW + 1]
            up_bias[here] = small[layer, UP_BIAS_ROW : UP_BIAS_ROW + 1, : up_bias.shape[-1]]
            qv_bias[layer] = small[layer, QV_BIAS_ROW : QV_BIAS_ROW + 2, : qv_bias.shape[-1]]
            gain[layer] = small[layer, GAIN_ROW : GAIN_ROW + 2]
            shift[layer] = small[layer, SHIFT_ROW : SHIFT_ROW + 2]


def on_device(
    hidden_in,
    segment_ids,
    out_cotangent,
    qkv_weight,
    qv_bias,
    out_weight,
    out_bias,
    norm_gain,
    norm_bias,
    up_weight,
    up_bias,
    down_weight,
    down_bias,
):
    layers, width, _, local = qkv_weight.shape
    vectors = dict(
        out_bias=out_bias,
        down_bias=down_bias,
        up_bias=up_bias,
        qv_bias=qv_bias,
        norm_gain=norm_gain,
        norm_bias=norm_bias,
    )
    qkv_turned = jnp.transpose(qkv_weight, (0, 2, 3, 1)).reshape(layers, 3 * local, width)
    result, hidden_grad, *sums = run_whole(
        hidden_in, out_cotangent, segment_ids, vectors, qkv_turned, out_weight, up_weight, down_weight
    )
    sums = over_outer_groups(sums)
    small, down, up, qkv, out = sums
    shape = jax.ShapeDtypeStruct
    outs = [
        shape(result.shape, BF16),
        shape(hidden_grad.shape, F32),
        shape(qkv.shape, F32),
        shape(qv_bias.shape, F32),
        shape(out.shape, F32),
        shape(out_bias.shape, F32),
        shape(norm_gain.shape, F32),
        shape(norm_bias.shape, F32),
        shape(up.shape, F32),
        shape(up_bias.shape, F32),
        shape(down.shape, F32),
        shape(down_bias.shape, F32),
    ]
    cuts = 3

    def whole(array):
        return pl.BlockSpec(array.shape, lambda layer, cut, zeros=(0,) * len(array.shape): zeros)

    def piece(array):
        return pl.BlockSpec((1, array.shape[1] // cuts, array.shape[2]), lambda layer, cut: (layer, cut, 0))

    inputs = (result, hidden_grad, small, down, up, qkv, out)
    done = pl.pallas_call(
        widen_kernel,
        grid=(layers, cuts),
        out_shape=outs,
        in_specs=[whole(array) for array in inputs[:3]] + [piece(array) for array in inputs[3:]],
        out_specs=[piece(array) if at in (2, 4, 8, 10) else whole(array) for at, array in enumerate(outs)],
        compiler_params=pltpu.CompilerParams(vmem_limit_bytes=62 << 20),
    )(*inputs)
    done = list(done)
    done[2] = jnp.transpose(done[2].reshape(layers, 3, local, width), (0, 3, 1, 2))
    return tuple(done)


def solution(mesh):
    placed = (
        P(("dp", "tensor"), None),
        P("dp", None),
        P(("dp", "tensor"), None),
        P(None, None, None, "tensor"),
        P(None, None, "tensor"),
        P(None, "tensor", None),
        P(),
        P(),
        P(),
        P(None, None, "tensor"),
        P(None, "tensor"),
        P(None, "tensor", None),
        P(),
    )
    return jax.shard_map(
        on_device,
        mesh=mesh,
        in_specs=placed,
        out_specs=(
            P(("dp", "tensor"), None),
            P(("dp", "tensor"), None),
            P(None, None, None, "tensor"),
            P(None, None, "tensor"),
            P(None, "tensor", None),
            P(),
            P(),
            P(),
            P(None, None, "tensor"),
            P(None, "tensor"),
            P(None, "tensor", None),
            P(),
        ),
        check_vma=False,
    )
```

```python
import functools
from types import SimpleNamespace

import jax
import jax.numpy as jnp
from jax import lax
from jax.experimental import pallas as pl
from jax.experimental.pallas import tpu as pltpu
from jax.sharding import PartitionSpec as P

HEAD = 64
norm_eps = 1e-05
MESH = pl.DeviceIdType.MESH
Y_SIZE = 2
Z_SIZE = 4
GROUP = Y_SIZE * Z_SIZE
F32 = jnp.float32
BF16 = jnp.bfloat16


class Place:
    def __init__(self):
        self.dp = lax.axis_index("dp")
        self.t = lax.axis_index("tensor")
        inner = lax.rem(self.dp, GROUP)
        base = self.dp - inner
        self.y = lax.rem(inner, Y_SIZE)
        self.z = inner // Y_SIZE
        z_pair = self.z + 1 - 2 * lax.rem(self.z, 2)
        z_mid = Z_SIZE - 1 - self.z
        self.is_end = jnp.logical_or(self.z == 0, self.z == Z_SIZE - 1)
        self.is_inner = jnp.logical_not(self.is_end)
        self.core = (self.dp, self.t + 1 - 2 * lax.rem(self.t, 2))
        self.over = (self.dp, lax.rem(self.t + 2, 4))
        self.diagonal = (self.dp, 3 - self.t)
        self.y_pair = (base + self.z * Y_SIZE + 1 - self.y, self.t)
        self.z_pair = (base + z_pair * Y_SIZE + self.y, self.t)
        self.z_right = (base + jnp.minimum(self.z + 1, Z_SIZE - 1) * Y_SIZE + self.y, self.t)
        self.z_left = (base + jnp.maximum(self.z - 1, 0) * Y_SIZE + self.y, self.t)
        self.z_mid = (base + z_mid * Y_SIZE + self.y, self.t)


class Links:
    def __init__(self, out_sems, in_sems, first=(0, 0), end=None):
        self.sems = (out_sems, in_sems)
        self.first = first
        self.used = list(first)
        self.end = end or (out_sems.shape[0], in_sems.shape[0])

    def take(self, side, count):
        start = self.used[side]
        self.used[side] += count
        assert self.used[side] <= self.end[side]
        return list(range(start, start + count))

    def outs(self, count):
        return self.take(0, count)

    def ins(self, count):
        return self.take(1, count)

    def keep(self, count):
        first = (self.outs(count)[0], self.ins(count)[0])
        return Links(*self.sems, first, tuple(self.used))

    def restart(self):
        self.used = list(self.first)

    def on(self, src, dst, device, out_at, in_at):
        return pltpu.make_async_remote_copy(
            src_ref=src,
            dst_ref=dst,
            send_sem=self.sems[0].at[out_at],
            recv_sem=self.sems[1].at[in_at],
            device_id=device,
            device_id_type=MESH,
        )

    def copy(self, src, dst, device):
        return self.on(src, dst, device, self.outs(1)[0], self.ins(1)[0])


def greet(devices):
    for device in devices:
        pl.semaphore_signal(pltpu.get_barrier_semaphore(), inc=1, device_id=device, device_id_type=MESH)


def met(devices):
    pl.semaphore_wait(pltpu.get_barrier_semaphore(), len(devices))


def added(one, two, dtype):
    return (one.astype(F32) + two.astype(F32)).astype(dtype)


def small_item(place, links, mine, steps, landing, result):
    top = pl.ds(0, 8)
    steps[0] = mine[...]
    near = links.copy(steps.at[0, top], landing.at[0, top], place.core)
    near.start()
    yield
    near.wait_recv()
    steps[1] = steps[0]
    steps[1, top] = steps[0, top] + landing[0, top]
    over = links.copy(steps.at[1, top], landing.at[1, top], place.over)
    over.start()
    yield
    over.wait_recv()
    steps[2] = steps[1]
    steps[2, top] = steps[1, top] + landing[1, top]
    across = links.copy(steps.at[2], landing.at[2], place.y_pair)
    across.start()
    yield
    across.wait_recv()
    steps[3] = steps[2] + landing[2]
    pair_in = links.copy(steps.at[3], landing.at[3], place.z_pair)
    mid = links.copy(steps.at[4], landing.at[4], place.z_mid)
    pair_out = links.copy(result, landing.at[3], place.z_pair)

    @pl.when(place.is_end)
    def _():
        pair_in.start()

    yield

    @pl.when(place.is_inner)
    def _():
        pair_in.wait_recv()
        steps[4] = steps[3] + landing[3]
        mid.start()

    yield

    @pl.when(place.is_inner)
    def _():
        mid.wait_recv()
        result[...] = steps[4] + landing[4]
        pair_out.start()

    yield

    @pl.when(place.is_end)
    def _():
        pair_out.wait_recv()
        result[...] = landing[3]

    yield
    near.wait_send()
    over.wait_send()
    across.wait_send()

    @pl.when(place.is_end)
    def _():
        pair_in.wait_send()

    @pl.when(place.is_inner)
    def _():
        mid.wait_send()
        pair_out.wait_send()


class Turns:
    def __init__(self, schedule):
        self.schedule = schedule
        self.place = 0
        self.items = []

    def add(self, items):
        self.items.extend(items)

    def take(self):
        for at in self.schedule[self.place] if self.place < len(self.schedule) else ():
            if at < len(self.items):
                next(self.items[at], None)
        self.place += 1

    def finish(self):
        self.take()
        running = self.items
        while running:
            running = [item for item in running if next(item, running) is not running]


def over_outer_groups(values):
    size = lax.axis_size("dp")
    if size == GROUP:
        return values
    groups = [[first + GROUP * turn for turn in range(size // GROUP)] for first in range(GROUP)]
    return [lax.psum(value, "dp", axis_index_groups=groups) for value in values]


def gelu_tanh(pre_active):
    return jax.nn.gelu(pre_active, approximate=True)


LANES = 128
SLOT = 256


def product(left, right, contract):
    return lax.dot_general(left, right, ((contract[:1], contract[1:]), ((), ())), preferred_element_type=F32)


def nn(left, right):
    return product(left, right, (1, 0))


def nt(left, right):
    return product(left, right, (1, 1))


def tn(left, right):
    return product(left, right, (0, 0))


class Gather:
    def __init__(self, place, links, rows):
        links.restart()
        half = SLOT // 2
        self.near_copies, self.far_copies, self.pass_copies = [], [], []
        for part in range(2):
            own = pl.ds(part * half, half)
            beside = pl.ds(SLOT + part * half, half)
            over = pl.ds(2 * SLOT + part * half, half)
            diagonal = pl.ds(3 * SLOT + part * half, half)
            self.near_copies.append(links.copy(rows.at[own], rows.at[beside], place.core))
            self.far_copies.append(links.copy(rows.at[own], rows.at[over], place.over))
            self.pass_copies.append(links.copy(rows.at[over], rows.at[diagonal], place.core))

    def send(self, part):
        self.far_copies[part].start()
        self.near_copies[part].start()

    def near(self):
        for copy in self.near_copies:
            copy.wait_recv()

    def far(self, part):
        self.far_copies[part].wait_recv()
        self.pass_copies[part].start()

    def diagonal(self, part):
        self.pass_copies[part].wait_recv()

    def drain(self):
        for copy in self.near_copies + self.far_copies + self.pass_copies:
            copy.wait_send()


class Scatter:
    def __init__(self, place, links, rooms):
        links.restart()
        self.core_out, self.core_in, self.far_out, self.far_in, self.near_out, self.near_in = rooms
        self.core_copies = [
            links.copy(self.core_out.at[part], self.core_in.at[part], place.core) for part in range(2)
        ]
        self.far_copies = [
            links.copy(self.far_out.at[part], self.far_in.at[part], place.over) for part in range(2)
        ]
        self.near_copies = [
            links.copy(self.near_out.at[part], self.near_in.at[part], place.core) for part in range(2)
        ]

    def beside(self, term):
        half = SLOT // 2
        for part in range(2):
            self.near_out[part] = term[part * half : (part + 1) * half].astype(BF16)
            self.near_copies[part].start()

    def diagonal(self, part, term):
        self.core_out[part] = term.astype(BF16)
        self.core_copies[part].start()

    def over(self, part, term):
        self.core_copies[part].wait_recv()
        self.far_out[part] = (term + self.core_in[part].astype(F32)).astype(BF16)
        self.far_copies[part].start()

    def arrived(self, part):
        self.near_copies[part].wait_recv()
        self.far_copies[part].wait_recv()
        return self.near_in[part].astype(F32) + self.far_in[part].astype(F32)

    def drain(self):
        for copy in self.core_copies + self.far_copies + self.near_copies:
            copy.wait_send()


def lane_masks():
    lane = lax.broadcasted_iota(jnp.int32, (1, LANES), 1)
    first = jnp.where(lane < HEAD, 1.0, 0.0).astype(BF16)
    return first, (1.0 - first.astype(F32)).astype(BF16)


def head_parts(tile, masks):
    parts = []
    width = tile.shape[-1]
    for first in range(0, width, LANES):
        piece = tile[:, first : min(first + LANES, width)]
        if piece.shape[-1] == HEAD:
            parts.append([piece])
        else:
            parts.append([piece * masks[0], piece * masks[1]])
    return parts


def whole_parts(tile):
    width = tile.shape[-1]
    return [tile[:, first : min(first + LANES, width)] for first in range(0, width, LANES)]


def allowed_rows(seg_cols, seg_rows, slot):
    return seg_cols[slot] == seg_rows[slot : slot + 1, :]


def attention_forward(query, keys, values, allowed):
    masks = lane_masks()
    outs = []
    for query_part, key_heads, value_heads in zip(
        whole_parts(query), head_parts(keys, masks), head_parts(values, masks)
    ):
        total = None
        for key_head, value_head in zip(key_heads, value_heads):
            scores = jnp.where(allowed, nt(query_part, key_head), -1000000000.0)
            grown = jnp.exp(scores - jnp.max(scores, axis=-1, keepdims=True))
            probs = grown * (1.0 / jnp.sum(grown, axis=-1, keepdims=True))
            term = nn(probs.astype(BF16), value_head)
            total = term if total is None else total + term
        outs.append(total.astype(BF16))
    return outs


def norm_rows(total, gain, shift):
    average = jnp.mean(total, axis=-1, keepdims=True)
    centered = total - average
    inverse = lax.rsqrt(jnp.mean(centered * centered, axis=-1, keepdims=True) + norm_eps)
    scaled = centered * inverse
    return scaled * gain + shift, scaled, inverse


OUT_BIAS, DOWN_BIAS, UP_BIAS, Q_BIAS, V_BIAS, GAIN, SHIFT = 0, 1, 2, 3, 4, 5, 7


def gelu_slope(raised):
    curve = (2.0 / jnp.pi) ** 0.5
    square = raised * raised
    bent = jnp.tanh(curve * raised * (1.0 + 0.044715 * square))
    return 0.5 * (1.0 + bent) + (0.5 * curve) * raised * (1.0 - bent * bent) * (1.0 + 0.134145 * square)


def attention_backward(query, keys, values, context_grad, allowed):
    masks = lane_masks()
    query_out, key_out, value_out = [], [], []
    for query_part, query_heads, key_heads, value_heads, grad_part, grad_heads in zip(
        whole_parts(query),
        head_parts(query, masks),
        head_parts(keys, masks),
        head_parts(values, masks),
        whole_parts(context_grad),
        head_parts(context_grad, masks),
    ):
        totals = None
        for query_head, key_head, value_head, grad_head in zip(
            query_heads, key_heads, value_heads, grad_heads
        ):
            scores = jnp.where(allowed, nt(key_head, query_part), -1000000000.0)
            grown = jnp.exp(scores - jnp.max(scores, axis=0, keepdims=True))
            probs = grown * (1.0 / jnp.sum(grown, axis=0, keepdims=True))
            probs_grad = nt(value_head, grad_part)
            shared = jnp.sum(probs_grad * probs, axis=0, keepdims=True)
            scores_grad = (probs * (probs_grad - shared)).astype(BF16)
            terms = (
                tn(scores_grad, key_head) * HEAD ** (-0.5),
                nn(scores_grad, query_head),
                nn(probs.astype(BF16), grad_head),
            )
            totals = terms if totals is None else tuple(map(jnp.add, totals, terms))
        query_out.append(totals[0].astype(BF16))
        key_out.append(totals[1].astype(BF16))
        value_out.append(totals[2].astype(BF16))
    return query_out, key_out, value_out


def norm_rows_backward(incoming, scaled, inverse, gain):
    inner = incoming * gain
    return inverse * (
        inner
        - jnp.mean(inner, axis=-1, keepdims=True)
        - scaled * jnp.mean(inner * scaled, axis=-1, keepdims=True)
    )


def column_sum(rows):
    return jnp.sum(rows.astype(F32), axis=0, keepdims=True)


def pair_item(place, links, mine, landing, result, local_sem, start, size):
    from_y, from_z, from_mid = landing
    half = size // 2
    here = pl.ds(pl.multiple_of(start + place.y * half, 16), half)
    there = pl.ds(pl.multiple_of(start + (1 - place.y) * half, 16), half)
    first, second = links.outs(2)
    over_y, pair, middle, back = links.ins(4)
    y_out = links.on(mine.at[there], from_y, place.y_pair, first, over_y)
    pair_in = links.on(mine.at[here], from_z, place.z_pair, second, pair)
    mid = links.on(mine.at[here], from_mid, place.z_mid, second, middle)
    pair_out = links.on(from_mid, from_z, place.z_pair, second, pair)
    back_inner = links.on(from_mid, result.at[here], place.y_pair, first, back)
    back_end = links.on(from_z, result.at[here], place.y_pair, first, back)
    keep_inner = pltpu.make_async_copy(from_mid, result.at[here], local_sem)
    keep_end = pltpu.make_async_copy(from_z, result.at[here], local_sem)
    y_out.start()
    yield
    y_out.wait_recv()
    y_out.wait_send()
    mine[here] = added(mine[here], from_y[...], BF16)

    @pl.when(place.is_end)
    def _():
        pair_in.start()

    yield

    @pl.when(place.is_inner)
    def _():
        pair_in.wait_recv()
        mine[here] = added(mine[here], from_z[...], BF16)
        mid.start()

    yield

    @pl.when(place.is_inner)
    def _():
        mid.wait_recv()
        mid.wait_send()
        from_mid[...] = added(mine[here], from_mid[...], BF16)
        pair_out.start()
        back_inner.start()
        keep_inner.start()

    yield

    @pl.when(place.is_end)
    def _():
        pair_out.wait_recv()
        back_end.start()
        keep_end.start()

    yield
    back_inner.wait_recv()
    yield

    @pl.when(place.is_end)
    def _():
        pair_in.wait_send()
        back_end.wait_send()
        keep_end.wait()

    @pl.when(place.is_inner)
    def _():
        pair_out.wait_send()
        back_inner.wait_send()
        keep_inner.wait()


def line_item(place, links, mine, landing, result, local_sem, start, size):
    from_left, from_right, from_y = landing
    quarter = size // Z_SIZE
    last = Z_SIZE - 1
    block = lambda at: pl.ds(start + at * quarter, quarter)
    own = pl.ds(pl.multiple_of(start + place.z * quarter, 16), quarter)
    send, receive, back = links.outs(last), links.ins(2 * last - 1), links.ins(last)
    right = {
        q: links.on(mine.at[block(q)], from_left.at[q - 1], place.z_right, send[q - 1], receive[q - 1])
        for q in range(1, Z_SIZE)
    }
    left = {
        q: links.on(
            mine.at[block(q)], from_right.at[q], place.z_left, send[q],
            receive[last + q] if q < last - 1 else receive[0],
        )
        for q in range(last)
    }
    across = links.copy(mine.at[own], from_y, place.y_pair)
    go_right, go_left = [], []
    for distance in range(1, Z_SIZE):
        for copies, device, sign in ((go_right, place.z_right, 1), (go_left, place.z_left, -1)):
            at = place.z - sign * (distance - 1)
            rows = pl.ds(pl.multiple_of(start + jnp.clip(at, 0, last) * quarter, 16), quarter)
            source = from_y if distance == 1 else result.at[rows]
            arrival = back[distance - 1] if sign > 0 else back[last - distance]
            copies.append(links.on(source, result.at[rows], device, send[0 if sign > 0 else 1], arrival))
    keep = pltpu.make_async_copy(from_y, result.at[own], local_sem)

    @pl.when(place.z == 0)
    def _():
        for q in range(last, 0, -1):
            right[q].start()

    @pl.when(place.z == last)
    def _():
        for q in range(last):
            left[q].start()

    yield
    for step in range(1, Z_SIZE):

        @pl.when(place.z == step)
        def _():
            for q in range(last, step - 1, -1):
                right[q].wait_recv()
                mine[block(q)] = added(mine[block(q)], from_left[q - 1], BF16)
                if q > step:
                    right[q].start()

        @pl.when(place.z == last - step)
        def _():
            for q in range(last - step + 1):
                left[q].wait_recv()
                mine[block(q)] = added(mine[block(q)], from_right[q], BF16)
                if q < last - step:
                    left[q].start()

        yield
    across.start()
    for q in range(1, Z_SIZE):

        @pl.when(place.z < q)
        def _():
            right[q].wait_send()

        @pl.when(place.z > last - q)
        def _():
            left[last - q].wait_send()

    yield
    across.wait_recv()
    across.wait_send()
    from_y[...] = added(mine[own], from_y[...], BF16)
    keep.start()

    @pl.when(place.z < last)
    def _():
        go_right[0].start()

    @pl.when(place.z > 0)
    def _():
        go_left[0].start()

    yield
    for distance in range(1, Z_SIZE):

        @pl.when(place.z >= distance)
        def _():
            go_right[distance - 1].wait_recv()

        if distance < last:

            @pl.when(jnp.logical_and(place.z >= distance, place.z < last))
            def _():
                go_right[distance - 1].wait_send()
                go_right[distance].start()

        @pl.when(place.z <= last - distance)
        def _():
            go_left[distance - 1].wait_recv()

        if distance < last:

            @pl.when(jnp.logical_and(place.z <= last - distance, place.z > 0))
            def _():
                go_left[distance - 1].wait_send()
                go_left[distance].start()

        yield
    keep.wait()

    @pl.when(place.z < last)
    def _():
        go_right[0].wait_send()

    @pl.when(place.z > 0)
    def _():
        go_left[0].wait_send()


ITEM_ROWS = dict(
    down=((96, False), (96, False), (192, False), (192, True), (192, False)),
    up=((96, False), (96, False), (192, False), (192, True), (192, False)),
    qkv=((128, True), (256, False), (192, False)),
    out=((128, True), (64, False)),
)
SCHEDULE = (
    (),
    (),
    (),
    (),
    (),
    (0, 1, 2, 3, 4),
    (5, 6, 7, 8, 9),
    (0, 1, 3),
    (2,),
    (0, 1, 3, 4, 5, 6, 8),
    (0, 1, 3, 3, 2, 4, 7, 9),
    (0, 1, 2, 3, 5, 6, 7, 8),
    (4, 9, 10, 11, 12, 13, 14, 15),
    (3, 0, 1, 2, 5, 6, 8, 8, 10, 15),
    (4, 7, 13, 15, 11, 9),
    (3, 5, 12, 10, 14, 2, 6),
    (11, 13),
    (4, 8, 7, 12, 14),
    (3, 5, 6, 9, 10, 10, 11, 13, 13, 15),
    (8, 7, 16, 17, 18, 19, 20),
    (15, 12, 14, 21, 22, 24, 9, 10, 11),
    (8, 15, 19, 13, 23),
    (12, 14, 16, 17, 24, 10, 19, 18, 25),
    (8, 15, 13, 16, 17, 24, 20, 10),
    (19, 19, 13, 18, 16),
    (10, 13, 11, 17, 24, 24, 20, 21, 22, 18),
    (16, 21, 22, 20, 23, 26, 27, 28, 29),
    (12, 14, 17, 18, 21, 23, 22, 25, 19, 30),
    (26, 31, 24, 20, 16, 21, 23, 29, 31, 22, 25, 26, 19, 31, 24, 29, 27, 25, 27, 28, 23, 17, 26, 26, 19, 18, 24, 29, 29, 28, 30, 30, 27, 20, 25, 21, 19, 22, 24, 31, 28, 30, 31, 23, 26, 29, 31, 27, 25, 28, 30, 26, 29, 31, 27, 26, 29, 28, 26, 29, 30),
)


def item_plan(name, rows):
    sizes = ITEM_ROWS[name]
    if sum(size for size, _ in sizes) != rows:
        sizes = ((rows, False),)
    plan, first = [], 0
    for size, line in sizes:
        plan.append((first, size, line))
        first += size
    return plan


OUT_COPIES, IN_COPIES = 190, 282
SHARE_ROWS = dict(qkv=(576,), out=(192,), up=(384, 192, 192), down=(384, 384))
SHARES = (
    (0,),
    (0, 0),
    (1, 2, 3, 4),
    (0,),
    (),
    (),
    (6,),
    (5, 7, 1, 0, 2, 3, 4, 1, 0, 2, 0),
    (),
    (),
    (),
    (6, 3, 5, 4),
    (7,),
    (1, 2, 6, 3),
    (7,),
    (5,),
    (4, 1),
    (),
    (),
    (),
    (2, 6),
    (3, 7, 5),
    (4, 6, 1, 7, 2, 5),
    (2, 1),
    (),
    (3,),
    (),
    (4, 3),
    (6,),
    (4, 7, 5, 6, 7, 5),
)


def share_item(place, links, mine, near, over, diagonal):
    rows, columns = mine.shape
    tall, broad, end = rows // Z_SIZE, columns // Y_SIZE, Z_SIZE - 1

    def cut(array, at):
        first = pl.multiple_of(jnp.clip(at, 0, end) * tall, 16)
        return array.at[pl.ds(first, tall), pl.ds(pl.multiple_of(place.y * broad, LANES), broad)]

    beside = links.copy(mine, near, place.core)
    across = links.copy(cut(mine, place.z), cut(over, place.z), place.over)
    chains, pair_sends = links.outs(2), links.outs(Z_SIZE)
    hops, pair_hops = links.ins(end), links.ins(Z_SIZE)
    flows = []
    for sign, device in ((1, place.z_right), (-1, place.z_left)):
        along, pair = [], []
        for distance in range(Z_SIZE):
            block = cut(over, place.z - sign * distance)
            at = distance - 1 if sign > 0 else end - distance
            if distance < end:
                hop = hops[distance if sign > 0 else end - 1 - distance]
                along.append(links.on(block, block, device, chains[sign > 0], hop))
            if distance:
                pair.append(links.on(block, block, place.y_pair, pair_sends[at], pair_hops[at]))
            else:
                pair.append(links.on(block, block, place.y_pair, pair_sends[end], pair_hops[end]))
        flows.append((along, pair))
    (go_right, pair_right), (go_left, pair_left) = flows
    passing = links.copy(over, diagonal, place.core)
    beside.start()
    across.start()
    yield
    for distance in range(Z_SIZE):
        if distance == 0:
            across.wait_recv()
            pair_right[0].start()

        for z, along, pair in ((place.z, go_right, pair_right), (end - place.z, go_left, pair_left)):

            @pl.when(z >= distance)
            def _():
                if distance:
                    along[distance - 1].wait_recv()
                    pair[distance].start()

            if distance < end:

                @pl.when(jnp.logical_and(z >= distance, z < end))
                def _():
                    if distance:
                        along[distance - 1].wait_send()
                    along[distance].start()

        yield
    pair_right[0].wait_recv()
    for z, pair in ((place.z, pair_right), (end - place.z, pair_left)):
        for distance in range(1, Z_SIZE):

            @pl.when(z >= distance)
            def _():
                pair[distance].wait_recv()

    passing.start()
    yield
    passing.wait_recv()
    beside.wait_recv()
    yield
    beside.wait_send()
    across.wait_send()
    passing.wait_send()
    pair_right[0].wait_send()
    for z, along, pair in ((place.z, go_right, pair_right), (end - place.z, go_left, pair_left)):
        for distance in range(Z_SIZE):
            if distance:

                @pl.when(z >= distance)
                def _():
                    pair[distance].wait_send()


        @pl.when(z < end)
        def _():
            along[0].wait_send()


def direct_item(place, links, mine, near, over, diagonal):
    beside = links.copy(mine, near, place.core)
    across = links.copy(mine, over, place.over)
    passing = links.copy(over, diagonal, place.core)
    beside.start()
    across.start()
    yield
    across.wait_recv()
    passing.start()
    yield
    passing.wait_recv()
    beside.wait_recv()
    yield
    for copy in (beside, across, passing):
        copy.wait_send()


def land_name(*place):
    return "_".join(map(str, place))


def item_rooms(name, rows, width):
    rooms = []
    for _, size, line in item_plan(name, rows):
        if line:
            rooms += [pltpu.VMEM((Z_SIZE - 1, size // Z_SIZE, width), BF16)] * 2
            rooms += [pltpu.VMEM((size // Z_SIZE, width), BF16)]
        else:
            rooms += [pltpu.VMEM((size // 2, width), BF16)] * 3
    return rooms


GAIN_ROW, SHIFT_ROW, OUT_BIAS_ROW, DOWN_BIAS_ROW, UP_BIAS_ROW, QV_BIAS_ROW = 0, 2, 4, 5, 8, 9
PARKED = tuple(
    dict(
        full_in=0, query=0, keys=0, values=0, context=0, active=0, scaled=0, inverse=0
    )
)


def whole_kernel(names, *refs):
    place = Place()
    table = dict(zip(names, refs))
    ref = SimpleNamespace(**table)
    links = Links(ref.out_sems, ref.in_sems)
    turning, middle, entering, summing = (links.keep(6) for _ in range(4))
    small, state = ref.small, ref.state
    full_in, query, keys, values, context = (table[name] for name in PARKED[:5])
    active, scaled, inverse = (table[name] for name in PARKED[5:])
    pre = ref.pre
    out_own, out_got = ref.out_own, ref.out_got
    own_part, far_part, context_in = ref.own_part, ref.far_part, ref.context_in
    full_down, pre_grad, full_out = ref.full_down, ref.pre_grad, ref.full_out
    mixed_grads = [ref.query_grad, ref.key_grad, ref.value_grad]
    layers = small.shape[0]
    local = query.shape[-1]
    half = SLOT // 2
    halves = [pl.ds(part * half, half) for part in range(2)]
    thirds = [pl.ds(part * local, local) for part in range(3)]
    slots = [pl.ds(slot * SLOT, SLOT) for slot in range(4)]
    far_pieces = [
        [pl.ds(2 * SLOT + part * half, half), pl.ds(3 * SLOT + part * half, half)] for part in range(2)
    ]

    def vector(layer, row, width=small.shape[-1]):
        return small[layer, row : row + 1, :width]

    partners = (place.core, place.over, place.diagonal, place.y_pair, place.z_pair, place.z_mid)
    greet(partners)
    loads = {}
    at = 0
    for layer in range(layers):
        for name, target in (
            ("qkv", ref.qkv.at[layer]),
            ("out", out_own.at[layer]),
            ("up", ref.up.at[layer]),
            ("down", ref.down.at[layer]),
        ):
            loads[layer, name] = pltpu.make_async_copy(
                table[name + "_in"].at[layer], target, ref.load_sems.at[at]
            )
            loads[layer, name].start()
            at += 1
    cotangent = pltpu.make_async_copy(ref.cotangent_in, ref.cotangent, ref.load_sems.at[at])
    cotangent.start()
    for layer in range(layers):
        for source, row in (
            (ref.out_bias_in, OUT_BIAS),
            (ref.down_bias_in, DOWN_BIAS),
            (ref.up_bias_in, UP_BIAS),
            (ref.qv_bias_in, Q_BIAS),
            (ref.norm_gain_in, GAIN),
            (ref.norm_bias_in, SHIFT),
        ):
            rows = source[layer].astype(F32).reshape(-1, source.shape[-1])
            small[layer, row : row + rows.shape[0], : rows.shape[1]] = rows
    for slot, index in enumerate((place.t, place.core[1], place.over[1], place.diagonal[1])):
        row = ref.segments[pl.ds(index, 1), :].astype(F32)
        ref.seg_rows[slot : slot + 1] = row
        ref.seg_cols[slot] = jnp.transpose(jnp.broadcast_to(row, ref.seg_cols.shape[1:]))
    rooms = (ref.core_out, ref.core_in, ref.far_out, ref.far_in, ref.near_out, ref.near_in)
    parks = {}

    def park(layer, these):
        for name in these:
            at = PARKED.index(name)
            parks[layer, name] = pltpu.make_async_copy(
                table[name], table["park_" + name].at[layer], ref.park_sems.at[layer, 0, at]
            )
            parks[layer, name].start()

    def parked(layer, these):
        for name in these:
            if (layer, name) in parks:
                parks.pop((layer, name)).wait()

    def restore(layer, these):
        if layer < 0:
            return
        for name in these:
            at = PARKED.index(name)
            parks[layer, name] = pltpu.make_async_copy(
                table["park_" + name].at[layer], table[name], ref.park_sems.at[layer, 1, at]
            )
            parks[layer, name].start()

    def attend(layer, slot):
        qkv_weight = ref.qkv.at[layer]
        rows = slots[slot]
        rows_in = full_in[rows]
        mixed = [nt(rows_in, qkv_weight[piece]) for piece in thirds]
        query[rows] = ((mixed[0] + vector(layer, Q_BIAS, local)) * HEAD ** (-0.5)).astype(BF16)
        keys[rows] = mixed[1].astype(BF16)
        values[rows] = (mixed[2] + vector(layer, V_BIAS, local)).astype(BF16)
        outs = attention_forward(
            query[rows], keys[rows], values[rows],
            allowed_rows(ref.seg_cols, ref.seg_rows, slot),
        )
        first = 0
        for out in outs:
            context[rows, first : first + out.shape[-1]] = out
            first += out.shape[-1]

    state[...] = ref.hidden[...].astype(F32)
    full_in[slots[0]] = ref.hidden[...]
    loads.pop((0, "out")).wait()
    met(partners)
    shares = Turns(SHARES)
    shares.add([share_item(place, links, out_own.at[0], *[out_got.at[at] for at in range(3)])])
    share_turn = shares.take
    share_turn()
    gather = Gather(place, turning, full_in)
    for part in range(2):
        gather.send(part)
    ref.small_grad[...] = jnp.zeros_like(ref.small_grad)
    last = layers - 1
    peers = [
        links.copy(small.at[last], ref.peer_small.at[at], device)
        for at, device in enumerate((place.core, place.over, place.diagonal))
    ]
    for copy in peers:
        copy.start()
    for name in ("qkv", "out", "up", "down"):
        arrays = (
            (out_own if name == "out" else table[name]).at[last],
            table[name + "_grad"].at[0],
            table[name + "_grad"].at[1],
            table[name + "_far"],
        )
        first = 0
        for size in SHARE_ROWS[name]:
            rows = pl.ds(first, size)
            shares.add([share_item(place, links, *[array.at[rows] for array in arrays])])
            first += size
        if first < arrays[0].shape[0]:
            rows = pl.ds(first, arrays[0].shape[0] - first)
            shares.add([direct_item(place, links, *[array.at[rows] for array in arrays])])

    for layer in range(last):
        up_weight, down_weight, full_mid = ref.up.at[layer], ref.down.at[layer], ref.full_mid.at[layer]

        sends = [
            links.copy(context.at[slots[slot]], context_in.at[slot - 1], device)
            for slot, device in ((1, place.core), (2, place.over), (3, place.diagonal))
        ]
        loads[layer, "qkv"].wait()
        parked(layer - 1, PARKED)
        attend(layer, 0)
        gather.near()
        attend(layer, 1)
        sends[0].start()
        for name in ("qkv", "out", "up", "down"):
            if (last, name) in loads:
                loads.pop((last, name)).wait()
        share_turn()
        gather.far(0)
        share_turn()
        share_turn()
        gather.far(1)
        share_turn()
        attend(layer, 2)
        sends[1].start()
        share_turn()
        gather.diagonal(0)
        gather.diagonal(1)
        attend(layer, 3)
        sends[2].start()
        share_turn()
        own_part[...] = nn(context[slots[0]], out_own[layer])
        share_turn()
        sends[0].wait_recv()
        own_part[...] += nn(context_in[0], out_got[0])
        share_turn()
        sends[1].wait_recv()
        share_turn()
        sends[2].wait_recv()
        gather.drain()
        for copy in sends:
            copy.wait_send()
        park(layer, PARKED[:5])
        gather = Gather(place, turning, full_mid)
        for part in range(2):
            rows = halves[part]
            total = (
                own_part[rows]
                + nn(context_in[1, rows], out_got[1])
                + nn(context_in[2, rows], out_got[2])
                + state[rows]
                + vector(layer, OUT_BIAS)
            )
            normed, scaled_part, inverse_part = norm_rows(total, vector(layer, GAIN), vector(layer, SHIFT))
            full_mid[rows] = normed.astype(BF16)
            gather.send(part)
            state[rows] = normed
            scaled[0, rows] = scaled_part
            inverse[0, rows] = jnp.broadcast_to(inverse_part, (half, LANES))
        share_turn()
        loads[layer, "up"].wait()
        loads[layer, "down"].wait()
        scatter = Scatter(place, summing, rooms)

        def feed(pieces):
            rows_in = jnp.concatenate([full_mid[piece] for piece in pieces])
            size = rows_in.shape[0] // len(pieces)
            for first in range(0, up_weight.shape[-1], SLOT):
                columns = slice(first, first + SLOT)
                raised = nn(rows_in, up_weight[:, columns]) + small[layer, UP_BIAS : UP_BIAS + 1, columns]
                shaped = gelu_tanh(raised).astype(BF16)
                for at, piece in enumerate(pieces):
                    pre[piece, columns] = raised[at * size : (at + 1) * size]
                    active[piece, columns] = shaped[at * size : (at + 1) * size]
            return nn(jnp.concatenate([active[piece] for piece in pieces]), down_weight[...])

        share_turn()
        own_part[...] = feed([slots[0]])
        share_turn()
        gather.near()
        parked(layer, PARKED[:5])
        scatter.beside(feed([slots[1]]))
        for part in range(2):
            share_turn()
            gather.far(part)
            share_turn()
            gather.diagonal(part)
            far_part[...] = feed(far_pieces[part])
            scatter.diagonal(part, far_part[half:])
            scatter.over(part, far_part[:half])
            share_turn()
            share_turn()
        gather.drain()
        gather = Gather(place, entering, full_in)
        for part in range(2):
            rows = halves[part]
            share_turn()
            total = state[rows] + own_part[rows] + scatter.arrived(part) + vector(layer, DOWN_BIAS)
            normed, scaled_part, inverse_part = norm_rows(
                total, vector(layer, GAIN + 1), vector(layer, SHIFT + 1)
            )
            state[rows] = normed
            full_in[rows] = normed.astype(BF16)
            gather.send(part)
            scaled[1, rows] = scaled_part
            inverse[1, rows] = jnp.broadcast_to(inverse_part, (half, LANES))
        scatter.drain()
        park(layer, PARKED[5:])

    vectors = [small.at[last]] + [ref.peer_small.at[at] for at in range(3)]
    for copy in peers:
        copy.wait_recv()

    def quarters(name):
        own = out_own if name == "out" else table[name]
        return [own.at[last], table[name + "_grad"].at[0], table[name + "_grad"].at[1], table[name + "_far"]]

    gather_in = gather
    share_turn()
    rows_in = full_in[slots[0]]
    allowed = allowed_rows(ref.seg_cols, ref.seg_rows, 0)
    for role, (weight, out_weight, own) in enumerate(zip(quarters("qkv"), quarters("out"), vectors)):
        mixed = [nt(rows_in, weight[piece]) for piece in thirds]
        outs = attention_forward(
            ((mixed[0] + own[Q_BIAS : Q_BIAS + 1, :local]) * HEAD ** (-0.5)).astype(BF16),
            mixed[1].astype(BF16),
            (mixed[2] + own[V_BIAS : V_BIAS + 1, :local]).astype(BF16),
            allowed,
        )
        first = 0
        for out in outs:
            ref.context_own[:, first : first + out.shape[-1]] = out
            first += out.shape[-1]
        term = nn(ref.context_own[...], out_weight[...])
        own_part[...] = term if role == 0 else own_part[...] + term
        share_turn()
    parked(last - 1, PARKED)
    full_mid = ref.full_mid.at[last]
    gather_mid = Gather(place, middle, full_mid)
    for part in range(2):
        rows = halves[part]
        total = own_part[rows] + state[rows] + vector(last, OUT_BIAS)
        normed, scaled_part, inverse_part = norm_rows(total, vector(last, GAIN), vector(last, SHIFT))
        full_mid[rows] = normed.astype(BF16)
        gather_mid.send(part)
        state[rows] = normed
        scaled[0, rows] = scaled_part
        inverse[0, rows] = jnp.broadcast_to(inverse_part, (half, LANES))
    share_turn()
    share_turn()
    for role, (weight, down_weight, own) in enumerate(zip(quarters("up"), quarters("down"), vectors)):
        raised = nn(full_mid[slots[0]], weight[...]) + own[UP_BIAS : UP_BIAS + 1]
        term = nn(gelu_tanh(raised).astype(BF16), down_weight[...])
        own_part[...] = term if role == 0 else own_part[...] + term
    for part in range(2):
        rows = halves[part]
        total = state[rows] + own_part[rows] + vector(last, DOWN_BIAS)
        normed, scaled_part, inverse_part = norm_rows(
            total, vector(last, GAIN + 1), vector(last, SHIFT + 1)
        )
        ref.result[rows] = normed.astype(BF16)
        scaled[1, rows] = scaled_part
        inverse[1, rows] = jnp.broadcast_to(inverse_part, (half, LANES))
    shares.finish()

    turns = Turns(SCHEDULE)
    item_count = 0

    def sum_items(layer, name):
        nonlocal item_count
        mine = table[name + "_grad"].at[layer]
        items = []
        for at, (start, size, line) in enumerate(item_plan(name, mine.shape[0])):
            landing = tuple(table[land_name(name, layer, at, room)] for room in range(3))
            make = line_item if line else pair_item
            items.append(
                make(
                    place, links, mine, landing, table[name + "_sum"].at[layer],
                    ref.item_sems.at[item_count], start, size,
                )
            )
            item_count += 1
        return items

    cotangent.wait()
    state[...] = ref.cotangent[...].astype(F32)
    for layer in reversed(range(layers)):
        qkv_weight, up_weight, down_weight = ref.qkv.at[layer], ref.up.at[layer], ref.down.at[layer]
        full_mid = ref.full_mid.at[layer]
        small_grad = ref.small_grad.at[layer]
        again = layer == last

        def norm_step(at, part, bias_row, target):
            rows = halves[part]
            incoming, scaled_part = state[rows], scaled[at, rows]
            small_grad[GAIN_ROW + at : GAIN_ROW + at + 1] += column_sum(incoming * scaled_part)
            small_grad[SHIFT_ROW + at : SHIFT_ROW + at + 1] += column_sum(incoming)
            total = norm_rows_backward(incoming, scaled_part, inverse[at, rows][:, :1], vector(layer, GAIN + at))
            state[rows] = total
            low = total.astype(BF16)
            target[rows] = low
            gather.send(part)
            small_grad[bias_row : bias_row + 1] += column_sum(low)

        parked(layer, PARKED[6:])
        gather = Gather(place, turning, full_down)
        scatter = Scatter(place, summing, rooms)
        for part in range(2):
            norm_step(1, part, DOWN_BIAS_ROW, full_down)
        turns.take()
        parked(layer, PARKED)

        def feed_back(pieces):
            rows_in = jnp.concatenate([full_down[piece] for piece in pieces])
            mid_in = jnp.concatenate([full_mid[piece] for piece in pieces])
            size = rows_in.shape[0] // len(pieces)
            for first in range(0, up_weight.shape[-1], SLOT):
                columns = slice(first, first + SLOT)
                if again:
                    raised = nn(mid_in, up_weight[:, columns]) + small[layer, UP_BIAS : UP_BIAS + 1, columns]
                    shaped = gelu_tanh(raised).astype(BF16)
                    for at, piece in enumerate(pieces):
                        active[piece, columns] = shaped[at * size : (at + 1) * size]
                else:
                    raised = jnp.concatenate([pre[piece, columns] for piece in pieces])
                low = (nt(rows_in, down_weight[columns]) * gelu_slope(raised)).astype(BF16)
                small_grad[UP_BIAS_ROW : UP_BIAS_ROW + 1, columns] += column_sum(low)
                for at, piece in enumerate(pieces):
                    pre_grad[piece, columns] = low[at * size : (at + 1) * size]
            return nt(jnp.concatenate([pre_grad[piece] for piece in pieces]), up_weight[...])

        own_part[...] = feed_back([slots[0]])
        turns.take()
        if again:
            gather_mid.near()
        gather.near()
        scatter.beside(feed_back([slots[1]]))
        turns.take()
        for part in range(2):
            if again:
                gather_mid.far(part)
            gather.far(part)
            if again:
                gather_mid.diagonal(part)
            gather.diagonal(part)
            far_part[...] = feed_back(far_pieces[part])
            scatter.diagonal(part, far_part[half:])
            scatter.over(part, far_part[:half])
            turns.take()
        gather.drain()
        if again:
            gather_mid.drain()

        def weight_grad(name, left, right, columns=None):
            target = table[name + "_grad"].at[layer]
            for first in range(0, left.shape[-1], SLOT):
                last = min(first + SLOT, left.shape[-1])
                target[first:last] = tn(left[:, first:last], right[...]).astype(BF16)

        weight_grad("down", active, full_down)
        turns.add(sum_items(layer, "down"))
        turns.take()
        weight_grad("up", full_mid, pre_grad)
        turns.add(sum_items(layer, "up"))
        restore(layer - 1, PARKED[5:6])
        turns.take()
        for part in range(2):
            rows = halves[part]
            state[rows] = state[rows] + own_part[rows] + scatter.arrived(part)
        scatter.drain()
        gather = Gather(place, turning, full_out)
        scatter = Scatter(place, summing, rooms)
        for part in range(2):
            norm_step(0, part, OUT_BIAS_ROW, full_out)
        restore(layer - 1, PARKED[6:])
        turns.take()

        def attend_back(slot):
            rows = slots[slot]
            if again:
                attend(layer, slot)
            context_grad = nt(full_out[rows], out_own[layer]).astype(BF16)
            outs = attention_backward(
                query[rows], keys[rows], values[rows], context_grad,
                allowed_rows(ref.seg_cols, ref.seg_rows, slot),
            )
            total = None
            for target, parts, piece in zip(mixed_grads, outs, thirds):
                first = 0
                for out in parts:
                    target[rows, first : first + out.shape[-1]] = out
                    first += out.shape[-1]
                term = nn(target[rows], qkv_weight[piece])
                total = term if total is None else total + term
            return total

        own_part[...] = attend_back(0)
        turns.take()
        if again:
            gather_in.near()
        gather.near()
        scatter.beside(attend_back(1))
        turns.take()
        if again:
            gather_in.far(0)
            gather_in.far(1)
        gather.far(0)
        gather.far(1)
        far_part[...] = attend_back(2)
        turns.take()
        if again:
            gather_in.diagonal(0)
            gather_in.diagonal(1)
            gather_in.drain()
        gather.diagonal(0)
        gather.diagonal(1)
        term = attend_back(3)
        for part in range(2):
            scatter.diagonal(part, term[part * half : (part + 1) * half])
        for part in range(2):
            scatter.over(part, far_part[halves[part]])
        turns.take()
        gather.drain()
        weight_grad("out", context, full_out)
        for target, piece in zip(mixed_grads, thirds):
            ref.qkv_grad[layer, piece] = tn(target[...], full_in[...]).astype(BF16)
        for at, target in enumerate((mixed_grads[0], mixed_grads[2])):
            small_grad[QV_BIAS_ROW + at : QV_BIAS_ROW + at + 1, :local] = column_sum(target[...])
        turns.add(sum_items(layer, "qkv"))
        turns.add(sum_items(layer, "out"))
        turns.add(
            [
                small_item(
                    place, links, small_grad, ref.small_steps.at[layer], ref.small_land.at[layer],
                    ref.small_sum.at[layer],
                )
            ]
        )
        restore(layer - 1, PARKED[:5])
        turns.take()
        for part in range(2):
            rows = halves[part]
            state[rows] = state[rows] + own_part[rows] + scatter.arrived(part)
        scatter.drain()
        turns.take()
    ref.hidden_grad[...] = state[...]
    turns.finish()
    for copy in peers:
        copy.wait_send()


def run_whole(hidden, cotangent, segments, vectors, qkv, out, up, down):
    layers, _, width = qkv.shape
    local, hidden_units = out.shape[1], up.shape[-1]
    rows = hidden.shape[0]
    group, half = 4 * rows, rows // 2
    vmem = pl.BlockSpec(memory_space=pltpu.VMEM)
    anywhere = pl.BlockSpec(memory_space=pl.ANY)
    inputs = dict(
        hidden=(hidden, vmem),
        segments=(segments, vmem),
        cotangent_in=(cotangent, anywhere),
        qkv_in=(qkv, anywhere),
        out_in=(out, anywhere),
        up_in=(up, anywhere),
        down_in=(down, anywhere),
    )
    inputs.update({name + "_in": (array, vmem) for name, array in vectors.items()})
    saved = [
        ((group, width), BF16),
        ((group, local), BF16),
        ((group, local), BF16),
        ((group, local), BF16),
        ((group, local), BF16),
        ((group, hidden_units), BF16),
        ((2, rows, width), F32),
        ((2, rows, LANES), F32),
    ]
    grads = dict(
        down=(hidden_units, width),
        up=(width, hidden_units),
        qkv=(3 * local, width),
        out=(local, width),
    )
    outputs = dict(
        result=((rows, width), BF16, vmem),
        hidden_grad=((rows, width), F32, vmem),
        small_sum=((layers, 16, width), F32, vmem),
    )
    outputs.update({name + "_sum": ((layers,) + shape, BF16, anywhere) for name, shape in grads.items()})
    outputs.update(
        {
            "park_" + name: ((layers - 1,) + shape, dtype, anywhere)
            for name, (shape, dtype) in zip(PARKED, saved)
        }
    )
    scratch = {name: pltpu.VMEM(shape, dtype) for name, (shape, dtype) in zip(PARKED, saved)}
    scratch.update(
        seg_rows=pltpu.VMEM((4, rows), F32),
        seg_cols=pltpu.VMEM((4, rows, rows), F32),
        small=pltpu.VMEM((layers, 16, width), F32),
        cotangent=pltpu.VMEM((rows, width), BF16),
        qkv=pltpu.VMEM(qkv.shape, BF16),
        out_own=pltpu.VMEM(out.shape, BF16),
        out_got=pltpu.VMEM((3,) + out.shape[1:], BF16),
        up=pltpu.VMEM(up.shape, BF16),
        down=pltpu.VMEM(down.shape, BF16),
        full_mid=pltpu.VMEM((layers, group, width), BF16),
        pre=pltpu.VMEM((group, hidden_units), F32),
        context_own=pltpu.VMEM((rows, local), BF16),
        peer_small=pltpu.VMEM((3, 16, width), F32),
        qkv_far=pltpu.VMEM(qkv.shape[1:], BF16),
        out_far=pltpu.VMEM(out.shape[1:], BF16),
        up_far=pltpu.VMEM(up.shape[1:], BF16),
        down_far=pltpu.VMEM(down.shape[1:], BF16),
        context_in=pltpu.VMEM((3, rows, local), BF16),
        own_part=pltpu.VMEM((rows, width), F32),
        far_part=pltpu.VMEM((rows, width), F32),
        state=pltpu.VMEM((rows, width), F32),
        full_down=pltpu.VMEM((group, width), BF16),
        pre_grad=pltpu.VMEM((group, hidden_units), BF16),
        full_out=pltpu.VMEM((group, width), BF16),
        query_grad=pltpu.VMEM((group, local), BF16),
        key_grad=pltpu.VMEM((group, local), BF16),
        value_grad=pltpu.VMEM((group, local), BF16),
        small_grad=pltpu.VMEM((layers, 16, width), F32),
        small_steps=pltpu.VMEM((layers, 5, 16, width), F32),
        small_land=pltpu.VMEM((layers, 5, 16, width), F32),
    )
    room = pltpu.VMEM((2, half, width), BF16)
    scratch.update(core_out=room, core_in=room, far_out=room, far_in=room, near_out=room, near_in=room)
    items = 0
    for name, shape in grads.items():
        scratch[name + "_grad"] = pltpu.VMEM((layers,) + shape, BF16)
        for layer in range(layers):
            items += len(item_plan(name, shape[0]))
            for at, land in enumerate(item_rooms(name, *shape)):
                scratch[land_name(name, layer, at // 3, at % 3)] = land
    scratch.update(
        load_sems=pltpu.SemaphoreType.DMA((4 * layers + 1,)),
        park_sems=pltpu.SemaphoreType.DMA((layers, 2, len(PARKED))),
        item_sems=pltpu.SemaphoreType.DMA((items,)),
        out_sems=pltpu.SemaphoreType.DMA((OUT_COPIES,)),
        in_sems=pltpu.SemaphoreType.DMA((IN_COPIES,)),
    )
    names = [*inputs, *outputs, *scratch]
    done = pl.pallas_call(
        functools.partial(whole_kernel, names),
        out_shape=[jax.ShapeDtypeStruct(shape, dtype) for shape, dtype, _ in outputs.values()],
        in_specs=[spec for _, spec in inputs.values()],
        out_specs=[spec for _, _, spec in outputs.values()],
        scratch_shapes=list(scratch.values()),
        compiler_params=pltpu.CompilerParams(
            collective_id=0, has_side_effects=True, vmem_limit_bytes=62 << 20
        ),
    )(*[array for array, _ in inputs.values()])
    return done[: 3 + len(grads)]


def widen_kernel(result_in, hidden_in, small, down_in, up_in, qkv_in, out_in, *outs):
    result, hidden, qkv, qv_bias, out, out_bias, gain, shift, up, up_bias, down, down_bias = outs
    step = pl.program_id(0) * pl.num_programs(1) + pl.program_id(1)
    for source, target in ((down_in, down), (up_in, up), (qkv_in, qkv), (out_in, out)):
        target[...] = source[...].astype(F32)

    result[...] = result_in[...]
    hidden[...] = hidden_in[...]

    @pl.when(step == 0)
    def _():
        for layer in range(small.shape[0]):
            here = pl.ds(layer, 1)
            out_bias[here] = small[layer, OUT_BIAS_ROW : OUT_BIAS_ROW + 1]
            down_bias[here] = small[layer, DOWN_BIAS_ROW : DOWN_BIAS_ROW + 1]
            up_bias[here] = small[layer, UP_BIAS_ROW : UP_BIAS_ROW + 1, : up_bias.shape[-1]]
            qv_bias[layer] = small[layer, QV_BIAS_ROW : QV_BIAS_ROW + 2, : qv_bias.shape[-1]]
            gain[layer] = small[layer, GAIN_ROW : GAIN_ROW + 2]
            shift[layer] = small[layer, SHIFT_ROW : SHIFT_ROW + 2]


def on_device(
    hidden_in,
    segment_ids,
    out_cotangent,
    qkv_weight,
    qv_bias,
    out_weight,
    out_bias,
    norm_gain,
    norm_bias,
    up_weight,
    up_bias,
    down_weight,
    down_bias,
):
    layers, width, _, local = qkv_weight.shape
    vectors = dict(
        out_bias=out_bias,
        down_bias=down_bias,
        up_bias=up_bias,
        qv_bias=qv_bias,
        norm_gain=norm_gain,
        norm_bias=norm_bias,
    )
    qkv_turned = jnp.transpose(qkv_weight, (0, 2, 3, 1)).reshape(layers, 3 * local, width)
    result, hidden_grad, *sums = run_whole(
        hidden_in, out_cotangent, segment_ids, vectors, qkv_turned, out_weight, up_weight, down_weight
    )
    sums = over_outer_groups(sums)
    small, down, up, qkv, out = sums
    shape = jax.ShapeDtypeStruct
    outs = [
        shape(result.shape, BF16),
        shape(hidden_grad.shape, F32),
        shape(qkv.shape, F32),
        shape(qv_bias.shape, F32),
        shape(out.shape, F32),
        shape(out_bias.shape, F32),
        shape(norm_gain.shape, F32),
        shape(norm_bias.shape, F32),
        shape(up.shape, F32),
        shape(up_bias.shape, F32),
        shape(down.shape, F32),
        shape(down_bias.shape, F32),
    ]
    cuts = 4

    def whole(array):
        return pl.BlockSpec(array.shape, lambda layer, cut, zeros=(0,) * len(array.shape): zeros)

    def rows(array):
        size = array.shape[0] // (layers * cuts)
        return pl.BlockSpec((size, array.shape[1]), lambda layer, cut: (layer * cuts + cut, 0))

    def piece(array):
        return pl.BlockSpec((1, array.shape[1] // cuts, array.shape[2]), lambda layer, cut: (layer, cut, 0))

    inputs = (result, hidden_grad, small, down, up, qkv, out)
    done = pl.pallas_call(
        widen_kernel,
        grid=(layers, cuts),
        out_shape=outs,
        in_specs=[rows(result), rows(hidden_grad), whole(small)] + [piece(array) for array in inputs[3:]],
        out_specs=[rows(result), rows(hidden_grad)]
        + [piece(array) if at in (2, 4, 8, 10) else whole(array) for at, array in enumerate(outs) if at > 1],
        compiler_params=pltpu.CompilerParams(vmem_limit_bytes=62 << 20),
    )(*inputs)
    done = list(done)
    done[2] = jnp.transpose(done[2].reshape(layers, 3, local, width), (0, 3, 1, 2))
    return tuple(done)


def solution(mesh):
    placed = (
        P(("dp", "tensor"), None),
        P("dp", None),
        P(("dp", "tensor"), None),
        P(None, None, None, "tensor"),
        P(None, None, "tensor"),
        P(None, "tensor", None),
        P(),
        P(),
        P(),
        P(None, None, "tensor"),
        P(None, "tensor"),
        P(None, "tensor", None),
        P(),
    )
    return jax.shard_map(
        on_device,
        mesh=mesh,
        in_specs=placed,
        out_specs=(
            P(("dp", "tensor"), None),
            P(("dp", "tensor"), None),
            P(None, None, None, "tensor"),
            P(None, None, "tensor"),
            P(None, "tensor", None),
            P(),
            P(),
            P(),
            P(None, None, "tensor"),
            P(None, "tensor"),
            P(None, "tensor", None),
            P(),
        ),
        check_vma=False,
    )
```

```python
import functools
from types import SimpleNamespace

import jax
import jax.numpy as jnp
from jax import lax
from jax.experimental import pallas as pl
from jax.experimental.pallas import tpu as pltpu
from jax.sharding import PartitionSpec as P

HEAD = 64
norm_eps = 1e-05
MESH = pl.DeviceIdType.MESH
Y_SIZE = 2
Z_SIZE = 4
GROUP = Y_SIZE * Z_SIZE
F32 = jnp.float32
BF16 = jnp.bfloat16


class Place:
    def __init__(self):
        self.dp = lax.axis_index("dp")
        self.t = lax.axis_index("tensor")
        inner = lax.rem(self.dp, GROUP)
        base = self.dp - inner
        self.y = lax.rem(inner, Y_SIZE)
        self.z = inner // Y_SIZE
        z_pair = self.z + 1 - 2 * lax.rem(self.z, 2)
        z_mid = Z_SIZE - 1 - self.z
        self.is_end = jnp.logical_or(self.z == 0, self.z == Z_SIZE - 1)
        self.is_inner = jnp.logical_not(self.is_end)
        self.core = (self.dp, self.t + 1 - 2 * lax.rem(self.t, 2))
        self.over = (self.dp, lax.rem(self.t + 2, 4))
        self.diagonal = (self.dp, 3 - self.t)
        self.y_pair = (base + self.z * Y_SIZE + 1 - self.y, self.t)
        self.z_pair = (base + z_pair * Y_SIZE + self.y, self.t)
        self.z_right = (base + jnp.minimum(self.z + 1, Z_SIZE - 1) * Y_SIZE + self.y, self.t)
        self.z_left = (base + jnp.maximum(self.z - 1, 0) * Y_SIZE + self.y, self.t)
        self.z_mid = (base + z_mid * Y_SIZE + self.y, self.t)


class Links:
    def __init__(self, out_sems, in_sems, first=(0, 0), end=None):
        self.sems = (out_sems, in_sems)
        self.first = first
        self.used = list(first)
        self.end = end or (out_sems.shape[0], in_sems.shape[0])

    def take(self, side, count):
        start = self.used[side]
        self.used[side] += count
        assert self.used[side] <= self.end[side]
        return list(range(start, start + count))

    def outs(self, count):
        return self.take(0, count)

    def ins(self, count):
        return self.take(1, count)

    def keep(self, count):
        first = (self.outs(count)[0], self.ins(count)[0])
        return Links(*self.sems, first, tuple(self.used))

    def restart(self):
        self.used = list(self.first)

    def on(self, src, dst, device, out_at, in_at):
        return pltpu.make_async_remote_copy(
            src_ref=src,
            dst_ref=dst,
            send_sem=self.sems[0].at[out_at],
            recv_sem=self.sems[1].at[in_at],
            device_id=device,
            device_id_type=MESH,
        )

    def copy(self, src, dst, device):
        return self.on(src, dst, device, self.outs(1)[0], self.ins(1)[0])


def greet(devices):
    for device in devices:
        pl.semaphore_signal(pltpu.get_barrier_semaphore(), inc=1, device_id=device, device_id_type=MESH)


def met(devices):
    pl.semaphore_wait(pltpu.get_barrier_semaphore(), len(devices))


def added(one, two, dtype):
    return (one.astype(F32) + two.astype(F32)).astype(dtype)


def small_item(place, links, mine, steps, landing, result):
    top = pl.ds(0, 8)
    steps[0] = mine[...]
    near = links.copy(steps.at[0, top], landing.at[0, top], place.core)
    near.start()
    yield
    near.wait_recv()
    steps[1] = steps[0]
    steps[1, top] = steps[0, top] + landing[0, top]
    over = links.copy(steps.at[1, top], landing.at[1, top], place.over)
    over.start()
    yield
    over.wait_recv()
    steps[2] = steps[1]
    steps[2, top] = steps[1, top] + landing[1, top]
    across = links.copy(steps.at[2], landing.at[2], place.y_pair)
    across.start()
    yield
    across.wait_recv()
    steps[3] = steps[2] + landing[2]
    pair_in = links.copy(steps.at[3], landing.at[3], place.z_pair)
    mid = links.copy(steps.at[4], landing.at[4], place.z_mid)
    pair_out = links.copy(result, landing.at[3], place.z_pair)

    @pl.when(place.is_end)
    def _():
        pair_in.start()

    yield

    @pl.when(place.is_inner)
    def _():
        pair_in.wait_recv()
        steps[4] = steps[3] + landing[3]
        mid.start()

    yield

    @pl.when(place.is_inner)
    def _():
        mid.wait_recv()
        result[...] = steps[4] + landing[4]
        pair_out.start()

    yield

    @pl.when(place.is_end)
    def _():
        pair_out.wait_recv()
        result[...] = landing[3]

    yield
    near.wait_send()
    over.wait_send()
    across.wait_send()

    @pl.when(place.is_end)
    def _():
        pair_in.wait_send()

    @pl.when(place.is_inner)
    def _():
        mid.wait_send()
        pair_out.wait_send()


class Turns:
    def __init__(self, schedule):
        self.schedule = schedule
        self.place = 0
        self.items = []

    def add(self, items):
        self.items.extend(items)

    def take(self):
        for at in self.schedule[self.place] if self.place < len(self.schedule) else ():
            if at < len(self.items):
                next(self.items[at], None)
        self.place += 1

    def finish(self):
        self.take()
        running = self.items
        while running:
            running = [item for item in running if next(item, running) is not running]


def over_outer_groups(values):
    size = lax.axis_size("dp")
    if size == GROUP:
        return values
    groups = [[first + GROUP * turn for turn in range(size // GROUP)] for first in range(GROUP)]
    return [lax.psum(value, "dp", axis_index_groups=groups) for value in values]


def gelu_tanh(pre_active):
    return jax.nn.gelu(pre_active, approximate=True)


LANES = 128
SLOT = 256


def product(left, right, contract):
    return lax.dot_general(left, right, ((contract[:1], contract[1:]), ((), ())), preferred_element_type=F32)


def nn(left, right):
    return product(left, right, (1, 0))


def nt(left, right):
    return product(left, right, (1, 1))


def tn(left, right):
    return product(left, right, (0, 0))


class Gather:
    def __init__(self, place, links, rows):
        links.restart()
        half = SLOT // 2
        self.near_copies, self.far_copies, self.pass_copies = [], [], []
        for part in range(2):
            own = pl.ds(part * half, half)
            beside = pl.ds(SLOT + part * half, half)
            over = pl.ds(2 * SLOT + part * half, half)
            diagonal = pl.ds(3 * SLOT + part * half, half)
            self.near_copies.append(links.copy(rows.at[own], rows.at[beside], place.core))
            self.far_copies.append(links.copy(rows.at[own], rows.at[over], place.over))
            self.pass_copies.append(links.copy(rows.at[over], rows.at[diagonal], place.core))

    def send(self, part):
        self.far_copies[part].start()
        self.near_copies[part].start()

    def near(self):
        for copy in self.near_copies:
            copy.wait_recv()

    def far(self, part):
        self.far_copies[part].wait_recv()
        self.pass_copies[part].start()

    def diagonal(self, part):
        self.pass_copies[part].wait_recv()

    def drain(self):
        for copy in self.near_copies + self.far_copies + self.pass_copies:
            copy.wait_send()


class Scatter:
    def __init__(self, place, links, rooms):
        links.restart()
        self.core_out, self.core_in, self.far_out, self.far_in, self.near_out, self.near_in = rooms
        self.core_copies = [
            links.copy(self.core_out.at[part], self.core_in.at[part], place.core) for part in range(2)
        ]
        self.far_copies = [
            links.copy(self.far_out.at[part], self.far_in.at[part], place.over) for part in range(2)
        ]
        self.near_copies = [
            links.copy(self.near_out.at[part], self.near_in.at[part], place.core) for part in range(2)
        ]

    def beside(self, term):
        half = SLOT // 2
        for part in range(2):
            self.near_out[part] = term[part * half : (part + 1) * half].astype(BF16)
            self.near_copies[part].start()

    def diagonal(self, part, term):
        self.core_out[part] = term.astype(BF16)
        self.core_copies[part].start()

    def over(self, part, term):
        self.core_copies[part].wait_recv()
        self.far_out[part] = (term + self.core_in[part].astype(F32)).astype(BF16)
        self.far_copies[part].start()

    def arrived(self, part):
        self.near_copies[part].wait_recv()
        self.far_copies[part].wait_recv()
        return self.near_in[part].astype(F32) + self.far_in[part].astype(F32)

    def drain(self):
        for copy in self.core_copies + self.far_copies + self.near_copies:
            copy.wait_send()


def lane_masks():
    lane = lax.broadcasted_iota(jnp.int32, (1, LANES), 1)
    first = jnp.where(lane < HEAD, 1.0, 0.0).astype(BF16)
    return first, (1.0 - first.astype(F32)).astype(BF16)


def head_parts(tile, masks):
    parts = []
    width = tile.shape[-1]
    for first in range(0, width, LANES):
        piece = tile[:, first : min(first + LANES, width)]
        if piece.shape[-1] == HEAD:
            parts.append([piece])
        else:
            parts.append([piece * masks[0], piece * masks[1]])
    return parts


def whole_parts(tile):
    width = tile.shape[-1]
    return [tile[:, first : min(first + LANES, width)] for first in range(0, width, LANES)]


def allowed_rows(seg_cols, seg_rows, slot):
    return seg_cols[slot] == seg_rows[slot : slot + 1, :]


def attention_forward(query, keys, values, allowed):
    masks = lane_masks()
    outs = []
    for query_part, key_heads, value_heads in zip(
        whole_parts(query), head_parts(keys, masks), head_parts(values, masks)
    ):
        total = None
        for key_head, value_head in zip(key_heads, value_heads):
            scores = jnp.where(allowed, nt(query_part, key_head), -1000000000.0)
            grown = jnp.exp(scores - jnp.max(scores, axis=-1, keepdims=True))
            probs = grown * (1.0 / jnp.sum(grown, axis=-1, keepdims=True))
            term = nn(probs.astype(BF16), value_head)
            total = term if total is None else total + term
        outs.append(total.astype(BF16))
    return outs


def norm_rows(total, gain, shift):
    average = jnp.mean(total, axis=-1, keepdims=True)
    centered = total - average
    inverse = lax.rsqrt(jnp.mean(centered * centered, axis=-1, keepdims=True) + norm_eps)
    scaled = centered * inverse
    return scaled * gain + shift, scaled, inverse


OUT_BIAS, DOWN_BIAS, UP_BIAS, Q_BIAS, V_BIAS, GAIN, SHIFT = 0, 1, 2, 3, 4, 5, 7


def gelu_slope(raised):
    curve = (2.0 / jnp.pi) ** 0.5
    square = raised * raised
    bent = jnp.tanh(curve * raised * (1.0 + 0.044715 * square))
    return 0.5 * (1.0 + bent) + (0.5 * curve) * raised * (1.0 - bent * bent) * (1.0 + 0.134145 * square)


def attention_backward(query, keys, values, context_grad, allowed):
    masks = lane_masks()
    query_out, key_out, value_out = [], [], []
    for query_part, query_heads, key_heads, value_heads, grad_part, grad_heads in zip(
        whole_parts(query),
        head_parts(query, masks),
        head_parts(keys, masks),
        head_parts(values, masks),
        whole_parts(context_grad),
        head_parts(context_grad, masks),
    ):
        totals = None
        for query_head, key_head, value_head, grad_head in zip(
            query_heads, key_heads, value_heads, grad_heads
        ):
            scores = jnp.where(allowed, nt(key_head, query_part), -1000000000.0)
            grown = jnp.exp(scores - jnp.max(scores, axis=0, keepdims=True))
            probs = grown * (1.0 / jnp.sum(grown, axis=0, keepdims=True))
            probs_grad = nt(value_head, grad_part)
            shared = jnp.sum(probs_grad * probs, axis=0, keepdims=True)
            scores_grad = (probs * (probs_grad - shared)).astype(BF16)
            terms = (
                tn(scores_grad, key_head) * HEAD ** (-0.5),
                nn(scores_grad, query_head),
                nn(probs.astype(BF16), grad_head),
            )
            totals = terms if totals is None else tuple(map(jnp.add, totals, terms))
        query_out.append(totals[0].astype(BF16))
        key_out.append(totals[1].astype(BF16))
        value_out.append(totals[2].astype(BF16))
    return query_out, key_out, value_out


def norm_rows_backward(incoming, scaled, inverse, gain):
    inner = incoming * gain
    return inverse * (
        inner
        - jnp.mean(inner, axis=-1, keepdims=True)
        - scaled * jnp.mean(inner * scaled, axis=-1, keepdims=True)
    )


def column_sum(rows):
    return jnp.sum(rows.astype(F32), axis=0, keepdims=True)


def pair_item(place, links, mine, landing, result, local_sem, start, size):
    from_y, from_z, from_mid = landing
    half = size // 2
    here = pl.ds(pl.multiple_of(start + place.y * half, 16), half)
    there = pl.ds(pl.multiple_of(start + (1 - place.y) * half, 16), half)
    first, second = links.outs(2)
    over_y, pair, middle, back = links.ins(4)
    y_out = links.on(mine.at[there], from_y, place.y_pair, first, over_y)
    pair_in = links.on(mine.at[here], from_z, place.z_pair, second, pair)
    mid = links.on(mine.at[here], from_mid, place.z_mid, second, middle)
    pair_out = links.on(from_mid, from_z, place.z_pair, second, pair)
    back_inner = links.on(from_mid, result.at[here], place.y_pair, first, back)
    back_end = links.on(from_z, result.at[here], place.y_pair, first, back)
    keep_inner = pltpu.make_async_copy(from_mid, result.at[here], local_sem)
    keep_end = pltpu.make_async_copy(from_z, result.at[here], local_sem)
    y_out.start()
    yield
    y_out.wait_recv()
    y_out.wait_send()
    mine[here] = added(mine[here], from_y[...], BF16)

    @pl.when(place.is_end)
    def _():
        pair_in.start()

    yield

    @pl.when(place.is_inner)
    def _():
        pair_in.wait_recv()
        mine[here] = added(mine[here], from_z[...], BF16)
        mid.start()

    yield

    @pl.when(place.is_inner)
    def _():
        mid.wait_recv()
        mid.wait_send()
        from_mid[...] = added(mine[here], from_mid[...], BF16)
        pair_out.start()
        back_inner.start()
        keep_inner.start()

    yield

    @pl.when(place.is_end)
    def _():
        pair_out.wait_recv()
        back_end.start()
        keep_end.start()

    yield
    back_inner.wait_recv()
    yield

    @pl.when(place.is_end)
    def _():
        pair_in.wait_send()
        back_end.wait_send()
        keep_end.wait()

    @pl.when(place.is_inner)
    def _():
        pair_out.wait_send()
        back_inner.wait_send()
        keep_inner.wait()


def line_item(place, links, mine, landing, result, local_sem, start, size):
    from_left, from_right, from_y = landing
    quarter = size // Z_SIZE
    last = Z_SIZE - 1
    block = lambda at: pl.ds(start + at * quarter, quarter)
    own = pl.ds(pl.multiple_of(start + place.z * quarter, 16), quarter)
    send, receive, back = links.outs(last), links.ins(2 * last - 1), links.ins(last)
    right = {
        q: links.on(mine.at[block(q)], from_left.at[q - 1], place.z_right, send[q - 1], receive[q - 1])
        for q in range(1, Z_SIZE)
    }
    left = {
        q: links.on(
            mine.at[block(q)], from_right.at[q], place.z_left, send[q],
            receive[last + q] if q < last - 1 else receive[0],
        )
        for q in range(last)
    }
    across = links.copy(mine.at[own], from_y, place.y_pair)
    go_right, go_left = [], []
    for distance in range(1, Z_SIZE):
        for copies, device, sign in ((go_right, place.z_right, 1), (go_left, place.z_left, -1)):
            at = place.z - sign * (distance - 1)
            rows = pl.ds(pl.multiple_of(start + jnp.clip(at, 0, last) * quarter, 16), quarter)
            source = from_y if distance == 1 else result.at[rows]
            arrival = back[distance - 1] if sign > 0 else back[last - distance]
            copies.append(links.on(source, result.at[rows], device, send[0 if sign > 0 else 1], arrival))
    keep = pltpu.make_async_copy(from_y, result.at[own], local_sem)

    @pl.when(place.z == 0)
    def _():
        for q in range(last, 0, -1):
            right[q].start()

    @pl.when(place.z == last)
    def _():
        for q in range(last):
            left[q].start()

    yield
    for step, turn in ((1, 0), (1, 1), (2, 0), (1, 2), (2, 1), (3, 0)):

        @pl.when(place.z == step)
        def _():
            q = last - turn
            right[q].wait_recv()
            mine[block(q)] = added(mine[block(q)], from_left[q - 1], BF16)
            if q > step:
                right[q].start()

        @pl.when(place.z == last - step)
        def _():
            q = turn
            left[q].wait_recv()
            mine[block(q)] = added(mine[block(q)], from_right[q], BF16)
            if q < last - step:
                left[q].start()

        yield
    across.start()
    for q in range(1, Z_SIZE):

        @pl.when(place.z < q)
        def _():
            right[q].wait_send()

        @pl.when(place.z > last - q)
        def _():
            left[last - q].wait_send()

    yield
    across.wait_recv()
    across.wait_send()
    from_y[...] = added(mine[own], from_y[...], BF16)
    keep.start()

    @pl.when(place.z < last)
    def _():
        go_right[0].start()

    @pl.when(place.z > 0)
    def _():
        go_left[0].start()

    yield
    for distance in range(1, Z_SIZE):

        @pl.when(place.z >= distance)
        def _():
            go_right[distance - 1].wait_recv()

        if distance < last:

            @pl.when(jnp.logical_and(place.z >= distance, place.z < last))
            def _():
                go_right[distance - 1].wait_send()
                go_right[distance].start()

        @pl.when(place.z <= last - distance)
        def _():
            go_left[distance - 1].wait_recv()

        if distance < last:

            @pl.when(jnp.logical_and(place.z <= last - distance, place.z > 0))
            def _():
                go_left[distance - 1].wait_send()
                go_left[distance].start()

        yield
    keep.wait()

    @pl.when(place.z < last)
    def _():
        go_right[0].wait_send()

    @pl.when(place.z > 0)
    def _():
        go_left[0].wait_send()


ITEM_ROWS = dict(
    down=((160, False), (192, False), (128, False), (192, True), (96, False)),
    up=((160, False), (192, False), (128, False), (192, True), (96, False)),
    qkv=((64, True), (160, False), (256, True), (96, False)),
    out=((192, False),),
)
SCHEDULE = (
    (),
    (),
    (),
    (),
    (0, 1, 2, 3, 4),
    (5, 6, 8),
    (0, 3, 3, 7, 9),
    (),
    (1, 8, 3, 3, 8, 3),
    (3, 3, 8, 8, 8, 0, 2, 4, 5),
    (8, 8, 1, 6),
    (0, 2, 4, 7, 10, 11, 9, 12, 13, 14),
    (3, 1, 5, 15, 18, 8, 0),
    (2, 4, 6),
    (1, 5, 7, 9, 10, 11, 13, 13, 12, 16),
    (3, 2, 4, 6, 7, 14, 18),
    (0, 5, 9, 13, 13, 13, 8, 18, 15, 17),
    (3, 1, 18, 18, 10, 19, 20, 21, 22),
    (18, 6, 11),
    (2, 7, 10, 12, 14, 16, 9, 4),
    (8, 13, 13, 5, 11, 15, 20, 20, 12),
    (3, 8, 18, 18, 6, 10, 14, 15, 20, 20, 20, 17, 19, 11, 7, 22, 22),
    (9, 12, 14, 16, 22, 22, 13, 22, 17, 19, 21, 23, 24, 25),
    (20, 20, 15, 16, 25, 10, 21, 26, 26, 18, 17, 26, 27, 28),
    (13, 22, 22, 11, 12, 14, 19, 25, 16),
    (28, 21, 26, 26, 28, 23, 18, 26, 24, 20, 17, 23, 29, 13, 15, 19, 28, 28, 30, 24, 28, 21, 26, 26, 18, 20, 31, 23, 27, 13, 16, 28, 28, 18, 17, 31, 22, 24, 20, 27, 25, 23, 19, 31, 22, 25, 27, 29, 29, 30, 24, 20, 21, 22, 26, 25, 30, 29, 28, 27, 23, 22, 26, 25, 29, 24, 31, 30, 28, 26, 27, 31, 29, 30, 26, 28, 31, 28, 31, 30),
)


def item_plan(name, rows):
    sizes = ITEM_ROWS[name]
    if sum(size for size, _ in sizes) != rows:
        sizes = ((rows, False),)
    plan, first = [], 0
    for size, line in sizes:
        plan.append((first, size, line))
        first += size
    return plan


OUT_COPIES, IN_COPIES = 202, 294
SHARE_ROWS = dict(qkv=(576,), out=(192,), up=(384, 192, 192), down=(384, 384))
SHARES = (
    (0,),
    (0, 0),
    (1, 2, 3, 4),
    (0,),
    (),
    (),
    (6,),
    (5, 7, 1, 0, 2, 3, 4, 1, 0, 2, 0),
    (),
    (),
    (),
    (6, 3, 5, 4),
    (7,),
    (1, 2, 6, 3),
    (7,),
    (5,),
    (4, 1),
    (),
    (),
    (),
    (2, 6),
    (3, 7, 5),
    (4, 6, 1, 7, 2, 5),
    (2, 1),
    (),
    (3,),
    (),
    (4, 3),
    (6,),
    (4, 7, 5, 6, 7, 5),
)


def share_item(place, links, mine, near, over, diagonal):
    rows, columns = mine.shape
    tall, broad, end = rows // Z_SIZE, columns // Y_SIZE, Z_SIZE - 1

    def cut(array, at):
        first = pl.multiple_of(jnp.clip(at, 0, end) * tall, 16)
        return array.at[pl.ds(first, tall), pl.ds(pl.multiple_of(place.y * broad, LANES), broad)]

    beside = links.copy(mine, near, place.core)
    across = links.copy(cut(mine, place.z), cut(over, place.z), place.over)
    chains, pair_sends = links.outs(2), links.outs(Z_SIZE)
    hops, pair_hops = links.ins(end), links.ins(Z_SIZE)
    flows = []
    for sign, device in ((1, place.z_right), (-1, place.z_left)):
        along, pair = [], []
        for distance in range(Z_SIZE):
            block = cut(over, place.z - sign * distance)
            at = distance - 1 if sign > 0 else end - distance
            if distance < end:
                hop = hops[distance if sign > 0 else end - 1 - distance]
                along.append(links.on(block, block, device, chains[sign > 0], hop))
            if distance:
                pair.append(links.on(block, block, place.y_pair, pair_sends[at], pair_hops[at]))
            else:
                pair.append(links.on(block, block, place.y_pair, pair_sends[end], pair_hops[end]))
        flows.append((along, pair))
    (go_right, pair_right), (go_left, pair_left) = flows
    passing = links.copy(over, diagonal, place.core)
    beside.start()
    across.start()
    yield
    for distance in range(Z_SIZE):
        if distance == 0:
            across.wait_recv()
            pair_right[0].start()

        for z, along, pair in ((place.z, go_right, pair_right), (end - place.z, go_left, pair_left)):

            @pl.when(z >= distance)
            def _():
                if distance:
                    along[distance - 1].wait_recv()
                    pair[distance].start()

            if distance < end:

                @pl.when(jnp.logical_and(z >= distance, z < end))
                def _():
                    if distance:
                        along[distance - 1].wait_send()
                    along[distance].start()

        yield
    pair_right[0].wait_recv()
    for z, pair in ((place.z, pair_right), (end - place.z, pair_left)):
        for distance in range(1, Z_SIZE):

            @pl.when(z >= distance)
            def _():
                pair[distance].wait_recv()

    passing.start()
    yield
    passing.wait_recv()
    beside.wait_recv()
    yield
    beside.wait_send()
    across.wait_send()
    passing.wait_send()
    pair_right[0].wait_send()
    for z, along, pair in ((place.z, go_right, pair_right), (end - place.z, go_left, pair_left)):
        for distance in range(Z_SIZE):
            if distance:

                @pl.when(z >= distance)
                def _():
                    pair[distance].wait_send()


        @pl.when(z < end)
        def _():
            along[0].wait_send()


def direct_item(place, links, mine, near, over, diagonal):
    beside = links.copy(mine, near, place.core)
    across = links.copy(mine, over, place.over)
    passing = links.copy(over, diagonal, place.core)
    beside.start()
    across.start()
    yield
    across.wait_recv()
    passing.start()
    yield
    passing.wait_recv()
    beside.wait_recv()
    yield
    for copy in (beside, across, passing):
        copy.wait_send()


def land_name(*place):
    return "_".join(map(str, place))


def item_rooms(name, rows, width):
    rooms = []
    for _, size, line in item_plan(name, rows):
        if line:
            rooms += [pltpu.VMEM((Z_SIZE - 1, size // Z_SIZE, width), BF16)] * 2
            rooms += [pltpu.VMEM((size // Z_SIZE, width), BF16)]
        else:
            rooms += [pltpu.VMEM((size // 2, width), BF16)] * 3
    return rooms


GAIN_ROW, SHIFT_ROW, OUT_BIAS_ROW, DOWN_BIAS_ROW, UP_BIAS_ROW, QV_BIAS_ROW = 0, 2, 4, 5, 8, 9
PARKED = tuple(
    dict(
        full_in=0, query=0, keys=0, values=0, context=0, active=0, scaled=0, inverse=0
    )
)


def whole_kernel(names, *refs):
    place = Place()
    table = dict(zip(names, refs))
    ref = SimpleNamespace(**table)
    links = Links(ref.out_sems, ref.in_sems)
    turning, middle, entering, leaving, later, summing = (links.keep(6) for _ in range(6))
    small, state = ref.small, ref.state
    full_in, query, keys, values, context = (table[name] for name in PARKED[:5])
    active, scaled, inverse = (table[name] for name in PARKED[5:])
    pre = ref.pre
    out_own, out_got = ref.out_own, ref.out_got
    own_part, far_part, context_in = ref.own_part, ref.far_part, ref.context_in
    full_down, pre_grad, full_out = ref.full_down, ref.pre_grad, ref.full_out
    mixed_grads = [ref.query_grad, ref.key_grad, ref.value_grad]
    layers = small.shape[0]
    local = query.shape[-1]
    half = SLOT // 2
    halves = [pl.ds(part * half, half) for part in range(2)]
    thirds = [pl.ds(part * local, local) for part in range(3)]
    slots = [pl.ds(slot * SLOT, SLOT) for slot in range(4)]
    far_pieces = [
        [pl.ds(2 * SLOT + part * half, half), pl.ds(3 * SLOT + part * half, half)] for part in range(2)
    ]

    def vector(layer, row, width=small.shape[-1]):
        return small[layer, row : row + 1, :width]

    partners = (place.core, place.over, place.diagonal, place.y_pair, place.z_pair, place.z_mid)
    greet(partners)
    loads = {}
    at = 0
    for layer in range(layers):
        for name, target in (
            ("qkv", ref.qkv.at[layer]),
            ("out", out_own.at[layer]),
            ("up", ref.up.at[layer]),
            ("down", ref.down.at[layer]),
        ):
            loads[layer, name] = pltpu.make_async_copy(
                table[name + "_in"].at[layer], target, ref.load_sems.at[at]
            )
            loads[layer, name].start()
            at += 1
    cotangent = pltpu.make_async_copy(ref.cotangent_in, ref.cotangent, ref.load_sems.at[at])
    cotangent.start()
    for layer in range(layers):
        for source, row in (
            (ref.out_bias_in, OUT_BIAS),
            (ref.down_bias_in, DOWN_BIAS),
            (ref.up_bias_in, UP_BIAS),
            (ref.qv_bias_in, Q_BIAS),
            (ref.norm_gain_in, GAIN),
            (ref.norm_bias_in, SHIFT),
        ):
            rows = source[layer].astype(F32).reshape(-1, source.shape[-1])
            small[layer, row : row + rows.shape[0], : rows.shape[1]] = rows
    for slot, index in enumerate((place.t, place.core[1], place.over[1], place.diagonal[1])):
        row = ref.segments[pl.ds(index, 1), :].astype(F32)
        ref.seg_rows[slot : slot + 1] = row
        ref.seg_cols[slot] = jnp.transpose(jnp.broadcast_to(row, ref.seg_cols.shape[1:]))
    rooms = (ref.core_out, ref.core_in, ref.far_out, ref.far_in, ref.near_out, ref.near_in)
    parks = {}

    def park(layer, these):
        for name in these:
            at = PARKED.index(name)
            parks[layer, name] = pltpu.make_async_copy(
                table[name], table["park_" + name].at[layer], ref.park_sems.at[layer, at]
            )
            parks[layer, name].start()

    def parked(layer, these):
        for name in these:
            if (layer, name) in parks:
                parks.pop((layer, name)).wait()

    def restore(layer, these):
        if layer < 0:
            return
        for name in these:
            at = PARKED.index(name)
            parks[layer, name] = pltpu.make_async_copy(
                table["park_" + name].at[layer], table[name], ref.park_sems.at[layer, at]
            )
            parks[layer, name].start()

    def attend(layer, slot):
        qkv_weight = ref.qkv.at[layer]
        rows = slots[slot]
        rows_in = full_in[rows]
        mixed = [nt(rows_in, qkv_weight[piece]) for piece in thirds]
        query[rows] = ((mixed[0] + vector(layer, Q_BIAS, local)) * HEAD ** (-0.5)).astype(BF16)
        keys[rows] = mixed[1].astype(BF16)
        values[rows] = (mixed[2] + vector(layer, V_BIAS, local)).astype(BF16)
        outs = attention_forward(
            query[rows], keys[rows], values[rows],
            allowed_rows(ref.seg_cols, ref.seg_rows, slot),
        )
        first = 0
        for out in outs:
            context[rows, first : first + out.shape[-1]] = out
            first += out.shape[-1]

    state[...] = ref.hidden[...].astype(F32)
    full_in[slots[0]] = ref.hidden[...]
    loads.pop((0, "out")).wait()
    met(partners)
    shares = Turns(SHARES)
    shares.add([share_item(place, links, out_own.at[0], *[out_got.at[at] for at in range(3)])])
    share_turn = shares.take
    share_turn()
    gather = Gather(place, turning, full_in)
    for part in range(2):
        gather.send(part)
    ref.small_grad[...] = jnp.zeros_like(ref.small_grad)
    last = layers - 1
    peers = [
        links.copy(small.at[last], ref.peer_small.at[at], device)
        for at, device in enumerate((place.core, place.over, place.diagonal))
    ]
    for copy in peers:
        copy.start()
    for name in ("qkv", "out", "up", "down"):
        arrays = (
            (out_own if name == "out" else table[name]).at[last],
            table[name + "_grad"].at[0],
            table[name + "_grad"].at[1],
            table[name + "_far"],
        )
        first = 0
        for size in SHARE_ROWS[name]:
            rows = pl.ds(first, size)
            shares.add([share_item(place, links, *[array.at[rows] for array in arrays])])
            first += size
        if first < arrays[0].shape[0]:
            rows = pl.ds(first, arrays[0].shape[0] - first)
            shares.add([direct_item(place, links, *[array.at[rows] for array in arrays])])

    for layer in range(last):
        up_weight, down_weight, full_mid = ref.up.at[layer], ref.down.at[layer], ref.full_mid.at[layer]

        sends = [
            links.copy(context.at[slots[slot]], context_in.at[slot - 1], device)
            for slot, device in ((1, place.core), (2, place.over), (3, place.diagonal))
        ]
        loads[layer, "qkv"].wait()
        parked(layer - 1, PARKED)
        attend(layer, 0)
        gather.near()
        attend(layer, 1)
        sends[0].start()
        for name in ("qkv", "out", "up", "down"):
            if (last, name) in loads:
                loads.pop((last, name)).wait()
        share_turn()
        gather.far(0)
        share_turn()
        share_turn()
        gather.far(1)
        share_turn()
        attend(layer, 2)
        sends[1].start()
        share_turn()
        gather.diagonal(0)
        gather.diagonal(1)
        attend(layer, 3)
        sends[2].start()
        share_turn()
        own_part[...] = nn(context[slots[0]], out_own[layer])
        share_turn()
        sends[0].wait_recv()
        own_part[...] += nn(context_in[0], out_got[0])
        share_turn()
        sends[1].wait_recv()
        share_turn()
        sends[2].wait_recv()
        gather.drain()
        for copy in sends:
            copy.wait_send()
        park(layer, PARKED[:5])
        gather = Gather(place, turning, full_mid)
        for part in range(2):
            rows = halves[part]
            total = (
                own_part[rows]
                + nn(context_in[1, rows], out_got[1])
                + nn(context_in[2, rows], out_got[2])
                + state[rows]
                + vector(layer, OUT_BIAS)
            )
            normed, scaled_part, inverse_part = norm_rows(total, vector(layer, GAIN), vector(layer, SHIFT))
            full_mid[rows] = normed.astype(BF16)
            gather.send(part)
            state[rows] = normed
            scaled[0, rows] = scaled_part
            inverse[0, rows] = jnp.broadcast_to(inverse_part, (half, LANES))
        share_turn()
        loads[layer, "up"].wait()
        loads[layer, "down"].wait()
        scatter = Scatter(place, summing, rooms)

        def feed(pieces):
            rows_in = jnp.concatenate([full_mid[piece] for piece in pieces])
            size = rows_in.shape[0] // len(pieces)
            for first in range(0, up_weight.shape[-1], SLOT):
                columns = slice(first, first + SLOT)
                raised = nn(rows_in, up_weight[:, columns]) + small[layer, UP_BIAS : UP_BIAS + 1, columns]
                shaped = gelu_tanh(raised).astype(BF16)
                for at, piece in enumerate(pieces):
                    pre[piece, columns] = raised[at * size : (at + 1) * size]
                    active[piece, columns] = shaped[at * size : (at + 1) * size]
            return nn(jnp.concatenate([active[piece] for piece in pieces]), down_weight[...])

        share_turn()
        own_part[...] = feed([slots[0]])
        share_turn()
        gather.near()
        parked(layer, PARKED[:5])
        scatter.beside(feed([slots[1]]))
        for part in range(2):
            share_turn()
            gather.far(part)
            share_turn()
            gather.diagonal(part)
            far_part[...] = feed(far_pieces[part])
            scatter.diagonal(part, far_part[half:])
            scatter.over(part, far_part[:half])
            share_turn()
            share_turn()
        gather.drain()
        gather = Gather(place, entering, full_in)
        for part in range(2):
            rows = halves[part]
            share_turn()
            total = state[rows] + own_part[rows] + scatter.arrived(part) + vector(layer, DOWN_BIAS)
            normed, scaled_part, inverse_part = norm_rows(
                total, vector(layer, GAIN + 1), vector(layer, SHIFT + 1)
            )
            state[rows] = normed
            full_in[rows] = normed.astype(BF16)
            gather.send(part)
            scaled[1, rows] = scaled_part
            inverse[1, rows] = jnp.broadcast_to(inverse_part, (half, LANES))
        scatter.drain()
        park(layer, PARKED[5:])

    vectors = [small.at[last]] + [ref.peer_small.at[at] for at in range(3)]
    for copy in peers:
        copy.wait_recv()

    def quarters(name):
        own = out_own if name == "out" else table[name]
        return [own.at[last], table[name + "_grad"].at[0], table[name + "_grad"].at[1], table[name + "_far"]]

    gather_in = gather
    share_turn()
    rows_in = full_in[slots[0]]
    allowed = allowed_rows(ref.seg_cols, ref.seg_rows, 0)
    for role, (weight, out_weight, own) in enumerate(zip(quarters("qkv"), quarters("out"), vectors)):
        mixed = [nt(rows_in, weight[piece]) for piece in thirds]
        outs = attention_forward(
            ((mixed[0] + own[Q_BIAS : Q_BIAS + 1, :local]) * HEAD ** (-0.5)).astype(BF16),
            mixed[1].astype(BF16),
            (mixed[2] + own[V_BIAS : V_BIAS + 1, :local]).astype(BF16),
            allowed,
        )
        first = 0
        for out in outs:
            ref.context_own[:, first : first + out.shape[-1]] = out
            first += out.shape[-1]
        term = nn(ref.context_own[...], out_weight[...])
        own_part[...] = term if role == 0 else own_part[...] + term
        share_turn()
    parked(last - 1, PARKED)
    full_mid = ref.full_mid.at[last]
    gather_mid = Gather(place, middle, full_mid)
    for part in range(2):
        rows = halves[part]
        total = own_part[rows] + state[rows] + vector(last, OUT_BIAS)
        normed, scaled_part, inverse_part = norm_rows(total, vector(last, GAIN), vector(last, SHIFT))
        full_mid[rows] = normed.astype(BF16)
        gather_mid.send(part)
        state[rows] = normed
        scaled[0, rows] = scaled_part
        inverse[0, rows] = jnp.broadcast_to(inverse_part, (half, LANES))
    share_turn()
    share_turn()
    for role, (weight, down_weight, own) in enumerate(zip(quarters("up"), quarters("down"), vectors)):
        raised = nn(full_mid[slots[0]], weight[...]) + own[UP_BIAS : UP_BIAS + 1]
        term = nn(gelu_tanh(raised).astype(BF16), down_weight[...])
        own_part[...] = term if role == 0 else own_part[...] + term
    for part in range(2):
        rows = halves[part]
        total = state[rows] + own_part[rows] + vector(last, DOWN_BIAS)
        normed, scaled_part, inverse_part = norm_rows(
            total, vector(last, GAIN + 1), vector(last, SHIFT + 1)
        )
        ref.result[rows] = normed.astype(BF16)
        scaled[1, rows] = scaled_part
        inverse[1, rows] = jnp.broadcast_to(inverse_part, (half, LANES))
    shares.finish()

    turns = Turns(SCHEDULE)
    item_count = 0

    def sum_items(layer, name):
        nonlocal item_count
        mine = table[name + "_grad"].at[layer]
        items = []
        for at, (start, size, line) in enumerate(item_plan(name, mine.shape[0])):
            landing = tuple(table[land_name(name, layer, at, room)] for room in range(3))
            make = line_item if line else pair_item
            items.append(
                make(
                    place, links, mine, landing, table[name + "_sum"].at[layer],
                    ref.item_sems.at[item_count], start, size,
                )
            )
            item_count += 1
        return items

    cotangent.wait()
    state[...] = ref.cotangent[...].astype(F32)
    assert layers == 2
    full_low = ref.full_low

    def norm_step(layer, at, part, bias_row, target, gather):
        rows = halves[part]
        small_grad = ref.small_grad.at[layer]
        incoming, scaled_part = state[rows], scaled[at, rows]
        small_grad[GAIN_ROW + at : GAIN_ROW + at + 1] += column_sum(incoming * scaled_part)
        small_grad[SHIFT_ROW + at : SHIFT_ROW + at + 1] += column_sum(incoming)
        total = norm_rows_backward(incoming, scaled_part, inverse[at, rows][:, :1], vector(layer, GAIN + at))
        state[rows] = total
        low = total.astype(BF16)
        target[rows] = low
        gather.send(part)
        small_grad[bias_row : bias_row + 1] += column_sum(low)

    def weight_grad(layer, name, left, right):
        target = table[name + "_grad"].at[layer]
        for first in range(0, left.shape[-1], SLOT):
            end = min(first + SLOT, left.shape[-1])
            target[first:end] = tn(left[:, first:end], right[...]).astype(BF16)

    def feed_back(layer, pieces, grads):
        up_weight, down_weight, full_mid = ref.up.at[layer], ref.down.at[layer], ref.full_mid.at[layer]
        rows_in = jnp.concatenate([grads[piece] for piece in pieces])
        mid_in = jnp.concatenate([full_mid[piece] for piece in pieces])
        size = rows_in.shape[0] // len(pieces)
        for first in range(0, up_weight.shape[-1], SLOT):
            columns = slice(first, first + SLOT)
            if layer == last:
                raised = nn(mid_in, up_weight[:, columns]) + small[layer, UP_BIAS : UP_BIAS + 1, columns]
                shaped = gelu_tanh(raised).astype(BF16)
                for at, piece in enumerate(pieces):
                    active[piece, columns] = shaped[at * size : (at + 1) * size]
            else:
                raised = jnp.concatenate([pre[piece, columns] for piece in pieces])
            low = (nt(rows_in, down_weight[columns]) * gelu_slope(raised)).astype(BF16)
            ref.small_grad[layer, UP_BIAS_ROW : UP_BIAS_ROW + 1, columns] += column_sum(low)
            for at, piece in enumerate(pieces):
                pre_grad[piece, columns] = low[at * size : (at + 1) * size]

    def feed_term(layer, pieces):
        return nt(jnp.concatenate([pre_grad[piece] for piece in pieces]), ref.up[layer])

    def spread(outs, targets, rows):
        for target, parts in zip(targets, outs):
            first = 0
            for out in parts:
                target[rows, first : first + out.shape[-1]] = out
                first += out.shape[-1]

    def attend_back(layer, slot, grads):
        rows = slots[slot]
        if layer == last:
            attend(layer, slot)
        context_grad = nt(grads[rows], out_own[layer]).astype(BF16)
        outs = attention_backward(
            query[rows], keys[rows], values[rows], context_grad,
            allowed_rows(ref.seg_cols, ref.seg_rows, slot),
        )
        spread(outs, mixed_grads, rows)

    def attend_term(weight, rows):
        return sum(nn(target[rows], weight[piece]) for target, piece in zip(mixed_grads, thirds))

    def attention_sums(layer, grads):
        weight_grad(layer, "out", context, grads)
        small_grad = ref.small_grad.at[layer]
        for target, piece in zip(mixed_grads, thirds):
            ref.qkv_grad[layer, piece] = tn(target[...], full_in[...]).astype(BF16)
        for at, target in enumerate((mixed_grads[0], mixed_grads[2])):
            small_grad[QV_BIAS_ROW + at : QV_BIAS_ROW + at + 1, :local] = column_sum(target[...])
        turns.add(sum_items(layer, "qkv"))
        turns.add(sum_items(layer, "out"))
        turns.add(
            [
                small_item(
                    place, links, small_grad, ref.small_steps.at[layer], ref.small_land.at[layer],
                    ref.small_sum.at[layer],
                )
            ]
        )

    gather_low = Gather(place, turning, full_down)
    for part in range(2):
        norm_step(last, 1, part, DOWN_BIAS_ROW, full_down, gather_low)
    for role, (weight, down_weight, own) in enumerate(zip(quarters("up"), quarters("down"), vectors)):
        raised = nn(full_mid[slots[0]], weight[...]) + own[UP_BIAS : UP_BIAS + 1]
        low = (nt(full_down[slots[0]], down_weight[...]) * gelu_slope(raised)).astype(BF16)
        term = nt(low, weight[...])
        own_part[...] = term if role == 0 else own_part[...] + term
    state[...] += own_part[...]
    gather_out = Gather(place, leaving, full_out)
    for part in range(2):
        norm_step(last, 0, part, OUT_BIAS_ROW, full_out, gather_out)
    restore(last - 1, PARKED[6:])
    rows_in = full_in[slots[0]]
    roles = list(zip(quarters("qkv"), quarters("out"), vectors))

    def attend_whole(role):
        weight, out_weight, own = roles[role]
        mixed = [nt(rows_in, weight[piece]) for piece in thirds]
        outs = attention_backward(
            ((mixed[0] + own[Q_BIAS : Q_BIAS + 1, :local]) * HEAD ** (-0.5)).astype(BF16),
            mixed[1].astype(BF16),
            (mixed[2] + own[V_BIAS : V_BIAS + 1, :local]).astype(BF16),
            nt(full_out[slots[0]], out_weight[...]).astype(BF16),
            allowed,
        )
        spread(outs, mixed_grads, slots[role])
        term = attend_term(weight, slots[role])
        own_part[...] = term if role == 0 else own_part[...] + term

    layer = last - 1
    attend_whole(0)
    attend_whole(1)
    feed_back(last, [slots[0]], full_down)
    turns.take()
    gather_mid.near()
    gather_low.near()
    feed_back(last, [slots[1]], full_down)
    turns.take()
    for part in range(2):
        gather_mid.far(part)
        gather_low.far(part)
        gather_mid.diagonal(part)
        gather_low.diagonal(part)
        feed_back(last, far_pieces[part], full_down)
        turns.take()
        if part == 0:
            attend_whole(2)
    gather_mid.drain()
    gather_low.drain()
    weight_grad(last, "down", active, full_down)
    turns.add(sum_items(last, "down"))
    restore(layer, PARKED[5:6])
    turns.take()
    weight_grad(last, "up", full_mid, pre_grad)
    turns.add(sum_items(last, "up"))
    turns.take()
    attend_whole(3)
    state[...] += own_part[...]
    parked(layer, PARKED[6:])
    gather = Gather(place, later, full_low)
    scatter = Scatter(place, summing, rooms)
    for part in range(2):
        norm_step(layer, 1, part, DOWN_BIAS_ROW, full_low, gather)
    turns.take()

    parked(layer, PARKED[5:6])
    feed_back(layer, [slots[0]], full_low)
    own_part[...] = feed_term(layer, [slots[0]])
    turns.take()
    gather.near()
    feed_back(layer, [slots[1]], full_low)
    scatter.beside(feed_term(layer, [slots[1]]))
    turns.take()
    for part in range(2):
        gather.far(part)
        gather.diagonal(part)
        feed_back(layer, far_pieces[part], full_low)
        far_part[...] = feed_term(layer, far_pieces[part])
        scatter.diagonal(part, far_part[half:])
        scatter.over(part, far_part[:half])
        turns.take()
    gather.drain()
    weight_grad(layer, "down", active, full_low)
    turns.add(sum_items(layer, "down"))
    turns.take()
    weight_grad(layer, "up", ref.full_mid.at[layer], pre_grad)
    turns.add(sum_items(layer, "up"))
    turns.take()

    for slot in range(4):
        if slot == 1:
            gather_in.near()
            gather_out.near()
        if slot == 2:
            for part in range(2):
                gather_in.far(part)
                gather_out.far(part)
        if slot == 3:
            for part in range(2):
                gather_in.diagonal(part)
                gather_out.diagonal(part)
        attend_back(last, slot, full_out)
        turns.take()
    gather_in.drain()
    gather_out.drain()
    attention_sums(last, full_out)
    restore(layer, PARKED[:5])
    turns.take()

    gather = Gather(place, turning, full_down)
    for part in range(2):
        rows = halves[part]
        state[rows] = state[rows] + own_part[rows] + scatter.arrived(part)
        norm_step(layer, 0, part, OUT_BIAS_ROW, full_down, gather)
    scatter.drain()
    scatter = Scatter(place, summing, rooms)
    turns.take()
    parked(layer, PARKED[:5])
    qkv_weight = ref.qkv.at[layer]
    attend_back(layer, 0, full_down)
    own_part[...] = attend_term(qkv_weight, slots[0])
    turns.take()
    gather.near()
    attend_back(layer, 1, full_down)
    scatter.beside(attend_term(qkv_weight, slots[1]))
    turns.take()
    gather.far(0)
    gather.far(1)
    attend_back(layer, 2, full_down)
    far_part[...] = attend_term(qkv_weight, slots[2])
    turns.take()
    gather.diagonal(0)
    gather.diagonal(1)
    attend_back(layer, 3, full_down)
    term = attend_term(qkv_weight, slots[3])
    for part in range(2):
        scatter.diagonal(part, term[part * half : (part + 1) * half])
    for part in range(2):
        scatter.over(part, far_part[halves[part]])
    turns.take()
    gather.drain()
    attention_sums(layer, full_down)
    turns.take()
    for part in range(2):
        rows = halves[part]
        state[rows] = state[rows] + own_part[rows] + scatter.arrived(part)
    scatter.drain()
    turns.take()
    ref.hidden_grad[...] = state[...]
    turns.finish()
    for copy in peers:
        copy.wait_send()


def run_whole(hidden, cotangent, segments, vectors, qkv, out, up, down):
    layers, _, width = qkv.shape
    local, hidden_units = out.shape[1], up.shape[-1]
    rows = hidden.shape[0]
    group, half = 4 * rows, rows // 2
    vmem = pl.BlockSpec(memory_space=pltpu.VMEM)
    anywhere = pl.BlockSpec(memory_space=pl.ANY)
    inputs = dict(
        hidden=(hidden, vmem),
        segments=(segments, vmem),
        cotangent_in=(cotangent, anywhere),
        qkv_in=(qkv, anywhere),
        out_in=(out, anywhere),
        up_in=(up, anywhere),
        down_in=(down, anywhere),
    )
    inputs.update({name + "_in": (array, vmem) for name, array in vectors.items()})
    saved = [
        ((group, width), BF16),
        ((group, local), BF16),
        ((group, local), BF16),
        ((group, local), BF16),
        ((group, local), BF16),
        ((group, hidden_units), BF16),
        ((2, rows, width), F32),
        ((2, rows, LANES), F32),
    ]
    grads = dict(
        down=(hidden_units, width),
        up=(width, hidden_units),
        qkv=(3 * local, width),
        out=(local, width),
    )
    outputs = dict(
        result=((rows, width), BF16, vmem),
        hidden_grad=((rows, width), F32, vmem),
        small_sum=((layers, 16, width), F32, vmem),
    )
    outputs.update({name + "_sum": ((layers,) + shape, BF16, anywhere) for name, shape in grads.items()})
    outputs.update(
        {
            "park_" + name: ((layers - 1,) + shape, dtype, anywhere)
            for name, (shape, dtype) in zip(PARKED, saved)
        }
    )
    scratch = {name: pltpu.VMEM(shape, dtype) for name, (shape, dtype) in zip(PARKED, saved)}
    scratch.update(
        seg_rows=pltpu.VMEM((4, rows), F32),
        seg_cols=pltpu.VMEM((4, rows, rows), F32),
        small=pltpu.VMEM((layers, 16, width), F32),
        cotangent=pltpu.VMEM((rows, width), BF16),
        qkv=pltpu.VMEM(qkv.shape, BF16),
        out_own=pltpu.VMEM(out.shape, BF16),
        out_got=pltpu.VMEM((3,) + out.shape[1:], BF16),
        up=pltpu.VMEM(up.shape, BF16),
        down=pltpu.VMEM(down.shape, BF16),
        full_mid=pltpu.VMEM((layers, group, width), BF16),
        pre=pltpu.VMEM((group, hidden_units), F32),
        context_own=pltpu.VMEM((rows, local), BF16),
        peer_small=pltpu.VMEM((3, 16, width), F32),
        qkv_far=pltpu.VMEM(qkv.shape[1:], BF16),
        out_far=pltpu.VMEM(out.shape[1:], BF16),
        up_far=pltpu.VMEM(up.shape[1:], BF16),
        down_far=pltpu.VMEM(down.shape[1:], BF16),
        context_in=pltpu.VMEM((3, rows, local), BF16),
        own_part=pltpu.VMEM((rows, width), F32),
        far_part=pltpu.VMEM((rows, width), F32),
        state=pltpu.VMEM((rows, width), F32),
        full_down=pltpu.VMEM((group, width), BF16),
        pre_grad=pltpu.VMEM((group, hidden_units), BF16),
        full_low=pltpu.VMEM((group, width), BF16),
        full_out=pltpu.VMEM((group, width), BF16),
        query_grad=pltpu.VMEM((group, local), BF16),
        key_grad=pltpu.VMEM((group, local), BF16),
        value_grad=pltpu.VMEM((group, local), BF16),
        small_grad=pltpu.VMEM((layers, 16, width), F32),
        small_steps=pltpu.VMEM((layers, 5, 16, width), F32),
        small_land=pltpu.VMEM((layers, 5, 16, width), F32),
    )
    room = pltpu.VMEM((2, half, width), BF16)
    scratch.update(core_out=room, core_in=room, far_out=room, far_in=room, near_out=room, near_in=room)
    items = 0
    for name, shape in grads.items():
        scratch[name + "_grad"] = pltpu.VMEM((layers,) + shape, BF16)
        for layer in range(layers):
            items += len(item_plan(name, shape[0]))
            for at, land in enumerate(item_rooms(name, *shape)):
                scratch[land_name(name, layer, at // 3, at % 3)] = land
    scratch.update(
        load_sems=pltpu.SemaphoreType.DMA((4 * layers + 1,)),
        park_sems=pltpu.SemaphoreType.DMA((layers - 1, len(PARKED))),
        item_sems=pltpu.SemaphoreType.DMA((items,)),
        out_sems=pltpu.SemaphoreType.DMA((OUT_COPIES,)),
        in_sems=pltpu.SemaphoreType.DMA((IN_COPIES,)),
    )
    names = [*inputs, *outputs, *scratch]
    done = pl.pallas_call(
        functools.partial(whole_kernel, names),
        out_shape=[jax.ShapeDtypeStruct(shape, dtype) for shape, dtype, _ in outputs.values()],
        in_specs=[spec for _, spec in inputs.values()],
        out_specs=[spec for _, _, spec in outputs.values()],
        scratch_shapes=list(scratch.values()),
        compiler_params=pltpu.CompilerParams(
            collective_id=0, has_side_effects=True, vmem_limit_bytes=62 << 20
        ),
    )(*[array for array, _ in inputs.values()])
    return done[: 3 + len(grads)]


def widen_kernel(result_in, hidden_in, small, down_in, up_in, qkv_in, out_in, *outs):
    result, hidden, qkv, qv_bias, out, out_bias, gain, shift, up, up_bias, down, down_bias = outs
    step = pl.program_id(0) * pl.num_programs(1) + pl.program_id(1)
    for source, target in ((down_in, down), (up_in, up), (qkv_in, qkv), (out_in, out)):
        target[...] = source[...].astype(F32)

    result[...] = result_in[...]
    hidden[...] = hidden_in[...]

    @pl.when(step == 0)
    def _():
        for layer in range(small.shape[0]):
            here = pl.ds(layer, 1)
            out_bias[here] = small[layer, OUT_BIAS_ROW : OUT_BIAS_ROW + 1]
            down_bias[here] = small[layer, DOWN_BIAS_ROW : DOWN_BIAS_ROW + 1]
            up_bias[here] = small[layer, UP_BIAS_ROW : UP_BIAS_ROW + 1, : up_bias.shape[-1]]
            qv_bias[layer] = small[layer, QV_BIAS_ROW : QV_BIAS_ROW + 2, : qv_bias.shape[-1]]
            gain[layer] = small[layer, GAIN_ROW : GAIN_ROW + 2]
            shift[layer] = small[layer, SHIFT_ROW : SHIFT_ROW + 2]


def on_device(
    hidden_in,
    segment_ids,
    out_cotangent,
    qkv_weight,
    qv_bias,
    out_weight,
    out_bias,
    norm_gain,
    norm_bias,
    up_weight,
    up_bias,
    down_weight,
    down_bias,
):
    layers, width, _, local = qkv_weight.shape
    vectors = dict(
        out_bias=out_bias,
        down_bias=down_bias,
        up_bias=up_bias,
        qv_bias=qv_bias,
        norm_gain=norm_gain,
        norm_bias=norm_bias,
    )
    qkv_turned = jnp.transpose(qkv_weight, (0, 2, 3, 1)).reshape(layers, 3 * local, width)
    result, hidden_grad, *sums = run_whole(
        hidden_in, out_cotangent, segment_ids, vectors, qkv_turned, out_weight, up_weight, down_weight
    )
    sums = over_outer_groups(sums)
    small, down, up, qkv, out = sums
    shape = jax.ShapeDtypeStruct
    outs = [
        shape(result.shape, BF16),
        shape(hidden_grad.shape, F32),
        shape(qkv.shape, F32),
        shape(qv_bias.shape, F32),
        shape(out.shape, F32),
        shape(out_bias.shape, F32),
        shape(norm_gain.shape, F32),
        shape(norm_bias.shape, F32),
        shape(up.shape, F32),
        shape(up_bias.shape, F32),
        shape(down.shape, F32),
        shape(down_bias.shape, F32),
    ]
    cuts = 4

    def whole(array):
        return pl.BlockSpec(array.shape, lambda layer, cut, zeros=(0,) * len(array.shape): zeros)

    def rows(array):
        size = array.shape[0] // (layers * cuts)
        return pl.BlockSpec((size, array.shape[1]), lambda layer, cut: (layer * cuts + cut, 0))

    def piece(array):
        return pl.BlockSpec((1, array.shape[1] // cuts, array.shape[2]), lambda layer, cut: (layer, cut, 0))

    inputs = (result, hidden_grad, small, down, up, qkv, out)
    done = pl.pallas_call(
        widen_kernel,
        grid=(layers, cuts),
        out_shape=outs,
        in_specs=[rows(result), rows(hidden_grad), whole(small)] + [piece(array) for array in inputs[3:]],
        out_specs=[rows(result), rows(hidden_grad)]
        + [piece(array) if at in (2, 4, 8, 10) else whole(array) for at, array in enumerate(outs) if at > 1],
        compiler_params=pltpu.CompilerParams(vmem_limit_bytes=62 << 20),
    )(*inputs)
    done = list(done)
    done[2] = jnp.transpose(done[2].reshape(layers, 3, local, width), (0, 3, 1, 2))
    return tuple(done)


def solution(mesh):
    placed = (
        P(("dp", "tensor"), None),
        P("dp", None),
        P(("dp", "tensor"), None),
        P(None, None, None, "tensor"),
        P(None, None, "tensor"),
        P(None, "tensor", None),
        P(),
        P(),
        P(),
        P(None, None, "tensor"),
        P(None, "tensor"),
        P(None, "tensor", None),
        P(),
    )
    return jax.shard_map(
        on_device,
        mesh=mesh,
        in_specs=placed,
        out_specs=(
            P(("dp", "tensor"), None),
            P(("dp", "tensor"), None),
            P(None, None, None, "tensor"),
            P(None, None, "tensor"),
            P(None, "tensor", None),
            P(),
            P(),
            P(),
            P(None, None, "tensor"),
            P(None, "tensor"),
            P(None, "tensor", None),
            P(),
        ),
        check_vma=False,
    )
```
